32 devices in a mesh: grp: 2 (over y), aux: 4 (over x, core), occ: 4 (over z).
Axes of the slice: x: 2, y: 2, z: 4, core: 2. Of those that a mesh axis runs over, the one named last changes fastest.
Arguments:
- integrals: bfloat16 [256, 4, 16, 128, 128], P(('grp', 'aux', 'occ')), parts along dimension 0, may hold values from -6 to 6
- pair_list: int32 [256, 4], P(('grp', 'aux', 'occ')), parts along dimension 0, may hold values from 0 to 3, as said below
- pair_count: int32 [256], P(('grp', 'aux', 'occ')), parts along dimension 0, may hold values from 1 to 4, as said below
- coefficients: bfloat16 [512, 384], P('grp'), parts along dimension 0, may hold values from -1 to 1
- metric: bfloat16 [4096, 2048], P(('grp', 'aux', 'occ')), parts along dimension 0, as said below
Outputs:
- exchange: float32 [512, 256], P(('grp', 'aux', 'occ')), parts along dimension 0
The draws below stay inside these ranges and needn't reach their ends.
There are 2 independent parts, one for each index of `grp`. The reference program is written for one: setup_inputs(seed, part) draws one part's arguments, and reference() takes and returns one part's arrays. A program takes and returns all parts, laid end to end along the dimension named above; each array names one. Nothing has to cross between parts.
Inputs may be any that keep to these rules, and one draw needn't show every extreme that they name: `pair_list`: each row names 4 distinct block pairs; only the first pair_count entries of a row are used. `pair_count`: some screening block uses all 4 slots. `metric`: zero above the diagonal; diagonal entries between 0.5 and 2.
All inputs are finite; a program needn't handle non-finite values.
Results may differ from the reference program's by a relative error of at most 0.0003.
Values may be sent and summed in bfloat16 or wider, within the bound.
No kernel may reach another device: no remote copies, remote signals or barrier semaphores. Data moves between devices by JAX's collectives and lax.ppermute only.
A program may use at most 256 MiB of HBM per device.

```python
import math
import jax
import jax.numpy as jnp
from jax import lax

NOCC = 384
NAUX = 2048
BLK = 128
ABLK = 16
NB = 2
PAIR_MOST = 4
NBF = 256
NABLK = 128


def draw_pair_list(key, part):
    key = jax.random.fold_in(key, 21)
    block_keys = jax.random.split(key, NABLK)

    def one_block(block_key):
        return jax.random.permutation(block_key, NB * NB)[:PAIR_MOST]
    return jax.vmap(one_block)(block_keys).astype(jnp.int32)


def draw_pair_count(key, part):
    key = jax.random.fold_in(key, 31)
    key_one, key_three = jax.random.split(key, 2)
    lowest = PAIR_MOST // 2
    counts = lowest + jax.random.randint(key_one, (NABLK,), 0, PAIR_MOST - lowest + 1)
    fullest = jax.random.randint(key_three, (), 0, NABLK)
    counts = jnp.where(jnp.arange(NABLK) == fullest, PAIR_MOST, counts)
    return counts.astype(jnp.int32)


def draw_coefficients(key, part):
    key = jax.random.fold_in(key, 51)
    key_perm, key_sign, key_noise, key_mag = jax.random.split(key, 4)
    leading = 0.97 * math.sqrt(32.0 / (BLK * NAUX))
    spread = 0.25 * leading / math.sqrt(NOCC)
    columns = jax.random.permutation(key_perm, NOCC)[:NBF]
    placed = jnp.arange(NOCC)[None, :] == columns[:, None]
    signs = jnp.where(jax.random.bernoulli(key_sign, 0.5, (NBF, 1)), 1.0, -1.0)
    noise = jnp.clip(jax.random.normal(key_noise, (NBF, NOCC), jnp.float32), -4.0, 4.0) * spread
    sizes = jax.random.uniform(key_mag, (NBF, 1), jnp.float32, 0.95, 1.05) * leading
    result = jnp.where(placed, signs * sizes, noise)
    return result.astype(jnp.bfloat16)


def draw_metric(key, part):
    key = jax.random.fold_in(key, 41)
    key_off, key_diag = jax.random.split(key)
    row_index = jnp.arange(NAUX)[:, None]
    col_index = jnp.arange(NAUX)[None, :]
    offdiag = jax.random.normal(key_off, (NAUX, NAUX), jnp.float32)
    diagonal = jnp.exp(jax.random.uniform(key_diag, (NAUX,), jnp.float32, math.log(0.5), math.log(2.0)))
    lower_part = jnp.where(col_index < row_index, offdiag * NAUX ** (-0.5), 0.0)
    result = lower_part + jnp.where(col_index == row_index, diagonal[:, None], 0.0)
    return result.astype(jnp.bfloat16)


def shard_levels(stream_key, extent, cuts, low, high):
    level, own = 1.0, jax.random.fold_in(stream_key, 6)
    for position, shards_of in cuts:
        steps = jnp.exp(jax.random.uniform(jax.random.fold_in(own, position), (shards_of,), jnp.float32, low / len(cuts), high / len(cuts)))
        level = level * jnp.repeat(steps, extent[position] // shards_of).reshape([-1 if axis == position else 1 for axis in range(len(extent))])
    return level


def gaussian(key, shape, deviation, limit, cuts=(), kind=jnp.bfloat16):
    gain = shard_levels(key, shape, cuts, -0.22, 0.18) if cuts else 1.0
    values = jax.random.normal(key, shape, jnp.float32) * deviation * gain
    return jnp.minimum(jnp.maximum(values, -limit), limit).astype(kind)


def setup_inputs(seed: int = 0, part: int = 0) -> dict:
    arg_keys = jax.random.split(jax.random.key(seed), 6)
    part_splits = jax.random.split(jax.random.fold_in(arg_keys[5], part), 6)
    return {
        "integrals": gaussian(part_splits[0], (NABLK, PAIR_MOST, ABLK, BLK, BLK), 1.0, 6.0, ((0, 16),)),
        "pair_list": draw_pair_list(jax.random.fold_in(jax.random.fold_in(arg_keys[5], part), 71), part),
        "pair_count": draw_pair_count(jax.random.fold_in(jax.random.fold_in(arg_keys[5], part), 71), part),
        "coefficients": draw_coefficients(jax.random.fold_in(jax.random.fold_in(arg_keys[5], part), 71), part),
        "metric": draw_metric(jax.random.fold_in(jax.random.fold_in(arg_keys[5], part), 71), part),
    }


def block_half(ints_block, list_block, count_block, coef_block):
    start_totals = jnp.zeros((ABLK, coef_block.shape[1], NBF), jnp.float32)

    def add_slot(slot_index, totals):
        pair_id = list_block[slot_index].astype(jnp.int32)
        row_block = (pair_id // NB).astype(jnp.int32)
        col_block = (pair_id % NB).astype(jnp.int32)
        coef_rows = lax.dynamic_slice_in_dim(coef_block, col_block * BLK, BLK, 0)
        contrib = jnp.einsum("pmn,ni->pim", ints_block[slot_index].astype(jnp.float32), coef_rows.astype(jnp.float32))
        current = lax.dynamic_slice_in_dim(totals, row_block * BLK, BLK, 2)
        return lax.dynamic_update_slice_in_dim(totals, current + contrib, row_block * BLK, 2)

    return lax.fori_loop(0, count_block, add_slot, start_totals)


def fitting(factor, columns):
    step_rows = factor.shape[0] // 8
    pieces = []
    for block_number in range(8):
        upper_end = (block_number + 1) * step_rows
        product = jnp.dot(factor[block_number * step_rows:upper_end, :upper_end], columns[:upper_end], preferred_element_type=jnp.float32)
        pieces.append(product.astype(jnp.bfloat16))
    return jnp.concatenate(pieces, axis=0)


def reference(integrals, pair_list, pair_count, coefficients, metric):
    orbital_width = NOCC // 8
    exchange_total = jnp.zeros((NBF, NBF), jnp.float32)
    for block_number in range(8):
        coef_block = coefficients[:, block_number * orbital_width:(block_number + 1) * orbital_width]
        half_tensor = lax.map(lambda operands: block_half(operands[0], operands[1], operands[2], coef_block), (integrals, pair_list, pair_count))
        half_tensor = half_tensor.reshape(NAUX, orbital_width * NBF).astype(jnp.bfloat16)
        fitted = fitting(metric, half_tensor)
        flattened = fitted.reshape(NAUX * orbital_width, NBF)
        exchange_total = exchange_total + jnp.dot(flattened.T, flattened, preferred_element_type=jnp.float32)
    return exchange_total
```

```python
import functools

import jax
import jax.numpy as jnp
from jax import lax
from jax.experimental import pallas as pl
from jax.experimental.pallas import tpu as pltpu
from jax.sharding import PartitionSpec as P

BOTH = ("aux", "occ")
VMEM_BYTES = 58 * 2**20


def half_kernel(list_ref, count_ref, ints_ref, basis_ref, out_ref, rows_ref):
    block = pl.program_id(0)
    slots, aux_width, size_block = ints_ref.shape[1:4]
    vectors, basis_total = basis_ref.shape
    side = basis_total // size_block
    where_slot, is_used = [], []
    for pair in range(side * side):
        slot_of = jnp.int32(0)
        used = jnp.int32(0)
        for slot in range(slots):
            hit = jnp.logical_and(
                list_ref[block, slot] == pair, slot < count_ref[block]
            ).astype(jnp.int32)
            slot_of = slot_of + hit * slot
            used = used + hit
        where_slot.append(slot_of)
        is_used.append(used > 0)

    def one(p, carry):
        rows = []
        for m in range(side):
            row = []
            for n in range(side):
                pair = m * side + n
                tile = ints_ref[0, where_slot[pair], p]
                row.append(jnp.where(is_used[pair], tile, jnp.zeros_like(tile)))
            rows.append(jnp.concatenate(row, axis=1))
        window = jnp.concatenate(rows, axis=0)
        product = lax.dot_general(
            basis_ref[...], window, (((1,), (1,)), ((), ())), preferred_element_type=jnp.float32
        )
        for m in range(side):
            rows_ref[m, pl.ds(p, vectors, stride=aux_width), :] = product[
                :, m * size_block : (m + 1) * size_block
            ]
        return carry

    lax.fori_loop(0, aux_width, one, 0, unroll=2)
    for m in range(side):
        out_ref[..., m * size_block : (m + 1) * size_block] = (
            rows_ref[m].astype(jnp.bfloat16).reshape(out_ref.shape[:-1] + (size_block,))
        )


def half_transform(integrals, pair_list, pair_count, basis_rows, devices):
    blocks, slots, aux_width, size_block, _ = integrals.shape
    vectors, basis_total = basis_rows.shape
    own = vectors // devices
    return pl.pallas_call(
        half_kernel,
        out_shape=jax.ShapeDtypeStruct(
            (devices, own, blocks * aux_width, basis_total), jnp.bfloat16
        ),
        grid_spec=pltpu.PrefetchScalarGridSpec(
            num_scalar_prefetch=2,
            grid=(blocks,),
            in_specs=[
                pl.BlockSpec(
                    (1, slots, aux_width, size_block, size_block), lambda b, *_: (b, 0, 0, 0, 0)
                ),
                pl.BlockSpec((vectors, basis_total), lambda b, *_: (0, 0)),
            ],
            out_specs=pl.BlockSpec(
                (devices, own, aux_width, basis_total), lambda b, *_: (0, 0, b, 0)
            ),
            scratch_shapes=[pltpu.VMEM(
                    (basis_total // size_block, vectors * aux_width, size_block), jnp.float32
                )],
        ),
        compiler_params=pltpu.CompilerParams(vmem_limit_bytes=VMEM_BYTES),
        cost_estimate=pl.CostEstimate(
            flops=2 * blocks * aux_width * vectors * basis_total * basis_total,
            bytes_accessed=integrals.size * 2 + vectors * blocks * aux_width * basis_total * 2,
            transcendentals=0,
        ),
        name="half_transform",
    )(pair_list, pair_count, integrals, basis_rows)


def fit_kernel(step_rows, factor_ref, half_ref, out_ref):
    aux_total = factor_ref.shape[0]
    columns = half_ref[...].reshape(aux_total, half_ref.shape[-1])
    total = jnp.zeros(out_ref.shape, jnp.float32)
    for low in range(0, aux_total, step_rows):
        high = low + step_rows
        fitted = jnp.dot(
            factor_ref[low:high, :high], columns[:high], preferred_element_type=jnp.float32
        ).astype(jnp.bfloat16)
        total = total + lax.dot_general(
            fitted, fitted, (((0,), (0,)), ((), ())), preferred_element_type=jnp.float32
        )

    @pl.when(pl.program_id(0) == 0)
    def _():
        out_ref[...] = total

    @pl.when(pl.program_id(0) > 0)
    def _():
        out_ref[...] += total


def fit_exchange(factor, arrived):
    devices, own, aux_local, basis_total = arrived.shape
    aux_total = factor.shape[0]
    return pl.pallas_call(
        functools.partial(fit_kernel, aux_total // 8),
        out_shape=jax.ShapeDtypeStruct((basis_total, basis_total), jnp.float32),
        grid=(own,),
        in_specs=[
            pl.BlockSpec(
                (aux_total, aux_total), lambda k: (0, 0), pipeline_mode=pl.Buffered(1)
            ),
            pl.BlockSpec((devices, 1, aux_local, basis_total), lambda k: (0, k, 0, 0)),
        ],
        out_specs=pl.BlockSpec((basis_total, basis_total), lambda k: (0, 0)),
        compiler_params=pltpu.CompilerParams(vmem_limit_bytes=VMEM_BYTES),
        cost_estimate=pl.CostEstimate(
            flops=own * aux_total * basis_total * (aux_total * 9 // 8 + 2 * basis_total),
            bytes_accessed=(factor.size + arrived.size) * 2,
            transcendentals=0,
        ),
        name="fit_exchange",
    )(factor, arrived)


def per_device(integrals, pair_list, pair_count, coefficients, metric):
    devices = lax.axis_size("aux") * lax.axis_size("occ")
    basis_total = coefficients.shape[0]
    factor = lax.all_gather(metric, BOTH, axis=0, tiled=True)
    half = half_transform(integrals, pair_list, pair_count, coefficients.T, devices)
    arrived = lax.all_to_all(half, BOTH, split_axis=0, concat_axis=0, tiled=True)
    partial_value = fit_exchange(factor, arrived)
    shares = partial_value.reshape(devices, basis_total // devices, basis_total)
    return jnp.sum(lax.all_to_all(shares, BOTH, split_axis=0, concat_axis=0, tiled=True).reshape(shares.shape), axis=0)


def solution(mesh):
    in_specs = (
        P(("grp", "aux", "occ"), None, None, None, None),
        P(("grp", "aux", "occ"), None),
        P(("grp", "aux", "occ")),
        P("grp", None),
        P(("grp", "aux", "occ"), None),
    )
    out_specs = P(("grp", "aux", "occ"), None)
    return jax.shard_map(
        per_device, mesh=mesh, in_specs=in_specs, out_specs=out_specs, check_vma=False
    )
```

```python
import functools

import jax
import jax.numpy as jnp
from jax import lax
from jax.experimental import pallas as pl
from jax.experimental.pallas import tpu as pltpu
from jax.sharding import PartitionSpec as P

BOTH = ("aux", "occ")
VMEM_BYTES = 58 * 2**20
PANEL = 16
SCALE = 2.0**40
PIVOT_FLOOR = 1e-6


def root(value):
    return value * lax.rsqrt(jnp.maximum(value, 1e-37))


def factor_kernel(start, *refs):
    if start == 0:
        coef_ref, rows_ref, rest_ref, diag_ref = refs
        scaled = (coef_ref[...].astype(jnp.float32) * SCALE).astype(jnp.bfloat16)
        gram = lax.dot_general(
            scaled, scaled, (((1,), (1,)), ((), ())), preferred_element_type=jnp.float32
        )
        total = gram.shape[0]
        on_diagonal = lax.broadcasted_iota(jnp.int32, gram.shape, 0) == (
            lax.broadcasted_iota(jnp.int32, gram.shape, 1)
        )
        diagonal = jnp.sum(jnp.where(on_diagonal, gram, 0.0), axis=0, keepdims=True)
        which = lax.broadcasted_iota(jnp.int32, diag_ref.shape, 0)
        diag_ref[...] = jnp.where(
            which == 0, diagonal, jnp.maximum(diagonal * PIVOT_FLOOR, 1e-37)
        )
        rest_ref[...] = gram
    else:
        rest_in_ref, diag_in_ref, rows_ref, rest_ref, diag_ref = refs
        rest_ref[...] = rest_in_ref[...]
        diag_ref[...] = diag_in_ref[...]
        total = rest_ref.shape[1]
    own = rows_ref.shape[0] // 2
    lanes = min(total, 128)
    lane = lax.broadcasted_iota(jnp.int32, (PANEL, total), 1)
    row = lax.broadcasted_iota(jnp.int32, (PANEL, total), 0)
    row_of_column = lax.broadcasted_iota(jnp.int32, (PANEL, 1), 0)

    def panel(number, carry):
        low = pl.multiple_of(start + number * PANEL, PANEL)
        rest = rest_ref[pl.ds(low, PANEL), :]
        left = diag_ref[0:1, :]
        floor = diag_ref[1:2, :]
        on_diagonal = lane == low + row
        left_column = jnp.sum(jnp.where(on_diagonal, left, 0.0), axis=1, keepdims=True)
        floor_column = jnp.sum(jnp.where(on_diagonal, floor, 0.0), axis=1, keepdims=True)
        corner = rest[:, :lanes]
        for part in range(1, total // lanes):
            corner = jnp.where(
                low >= part * lanes, rest[:, part * lanes : (part + 1) * lanes], corner
            )
        corner = pltpu.roll(corner, lax.rem(lanes - lax.rem(low, lanes), lanes), 1)
        done = jnp.zeros((PANEL, total), jnp.float32)
        for t in range(PANEL):
            pivot = jnp.maximum(left_column[t : t + 1], floor_column[t : t + 1])
            inverse = lax.rsqrt(pivot)
            inverse = inverse * (1.5 - 0.5 * (pivot * inverse) * inverse)
            most = root(left)
            here = jnp.clip(rest[t : t + 1] * inverse, -most, most)
            here = jnp.where(lane[:1] > low + t, here, 0.0)
            left = jnp.maximum(left - here * here, 0.0)
            here = jnp.where(lane[:1] == low + t, pivot * inverse, here)
            done = jnp.where(row == t, here, done)
            most = root(left_column)
            weight = jnp.clip(corner[:, t : t + 1] * inverse, -most, most)
            weight = jnp.where(row_of_column > t, weight, 0.0)
            left_column = jnp.maximum(left_column - weight * weight, 0.0)
            rest = rest - weight * here
            corner = corner - weight * (corner[t : t + 1] * inverse)
        diag_ref[0:1, :] = left
        rest_ref[...] -= lax.dot_general(
            done,
            done,
            (((0,), (0,)), ((), ())),
            precision=lax.Precision.HIGHEST,
            preferred_element_type=jnp.float32,
        )
        done = done * (1.0 / SCALE)
        high = done.astype(jnp.bfloat16)
        place = pl.multiple_of(number * PANEL, PANEL)
        rows_ref[pl.ds(place, PANEL), :] = high
        rows_ref[pl.ds(own + place, PANEL), :] = (done - high.astype(jnp.float32)).astype(
            jnp.bfloat16
        )
        return carry

    lax.fori_loop(0, own // PANEL, panel, 0)


def factor_rows(start, own, total, operands):
    rows, rest, diagonals = pl.pallas_call(
        functools.partial(factor_kernel, start),
        out_shape=(
            jax.ShapeDtypeStruct((2 * own, total), jnp.bfloat16),
            jax.ShapeDtypeStruct((total, total), jnp.float32),
            jax.ShapeDtypeStruct((8, total), jnp.float32),
        ),
        compiler_params=pltpu.CompilerParams(vmem_limit_bytes=VMEM_BYTES),
        name="factor_rows",
    )(*operands)
    return rows, (rest, diagonals)


def half_kernel(low_block, list_ref, count_ref, ints_ref, basis_ref, out_ref, rows_ref):
    block = pl.program_id(0)
    slots, aux_width, size_block = ints_ref.shape[1:4]
    vectors = basis_ref.shape[0] // 2
    side = basis_ref.shape[1] // size_block
    where_slot, is_used = [], []
    for pair in range(side * side):
        slot_of = jnp.int32(0)
        used = jnp.int32(0)
        for slot in range(slots):
            hit = jnp.logical_and(
                list_ref[block, slot] == pair, slot < count_ref[block]
            ).astype(jnp.int32)
            slot_of = slot_of + hit * slot
            used = used + hit
        where_slot.append(slot_of)
        is_used.append(used > 0)

    def one(p, carry):
        rows = []
        for m in range(side):
            row = []
            for n in range(low_block, side):
                pair = m * side + n
                tile = ints_ref[0, where_slot[pair], p]
                row.append(jnp.where(is_used[pair], tile, jnp.zeros_like(tile)))
            rows.append(jnp.concatenate(row, axis=1))
        window = jnp.concatenate(rows, axis=0)
        product = lax.dot_general(
            basis_ref[:, low_block * size_block :],
            window,
            (((1,), (1,)), ((), ())),
            preferred_element_type=jnp.float32,
        )
        product = product[:vectors] + product[vectors:]
        for m in range(side):
            rows_ref[m, pl.ds(p, vectors, stride=aux_width), :] = product[
                :, m * size_block : (m + 1) * size_block
            ]
        return carry

    lax.fori_loop(0, aux_width, one, 0, unroll=2)
    for m in range(side):
        out_ref[..., m * size_block : (m + 1) * size_block] = (
            rows_ref[m].astype(jnp.bfloat16).reshape(out_ref.shape[:-1] + (size_block,))
        )


def half_transform(integrals, pair_list, pair_count, basis_rows, start, devices):
    blocks, slots, aux_width, size_block, _ = integrals.shape
    vectors, basis_total = basis_rows.shape[0] // 2, basis_rows.shape[1]
    own = vectors // devices
    return pl.pallas_call(
        functools.partial(half_kernel, start // size_block),
        out_shape=jax.ShapeDtypeStruct(
            (devices, own, blocks * aux_width, basis_total), jnp.bfloat16
        ),
        grid_spec=pltpu.PrefetchScalarGridSpec(
            num_scalar_prefetch=2,
            grid=(blocks,),
            in_specs=[
                pl.BlockSpec(
                    (1, slots, aux_width, size_block, size_block), lambda b, *_: (b, 0, 0, 0, 0)
                ),
                pl.BlockSpec(basis_rows.shape, lambda b, *_: (0, 0)),
            ],
            out_specs=pl.BlockSpec(
                (devices, own, aux_width, basis_total), lambda b, *_: (0, 0, b, 0)
            ),
            scratch_shapes=[
                pltpu.VMEM(
                    (basis_total // size_block, vectors * aux_width, size_block), jnp.float32
                )
            ],
        ),
        compiler_params=pltpu.CompilerParams(vmem_limit_bytes=VMEM_BYTES),
        cost_estimate=pl.CostEstimate(
            flops=4 * blocks * aux_width * vectors * basis_total * basis_total,
            bytes_accessed=integrals.size * 2 + vectors * blocks * aux_width * basis_total * 2,
            transcendentals=0,
        ),
        name="half_transform",
    )(pair_list, pair_count, integrals, basis_rows)


def fit_kernel(step_rows, factor_ref, half_ref, before_ref, out_ref):
    aux_total = factor_ref.shape[0]
    columns = half_ref[...].reshape(aux_total, half_ref.shape[-1])
    total = jnp.zeros(out_ref.shape, jnp.float32)
    for low in range(0, aux_total, step_rows):
        high = low + step_rows
        fitted = jnp.dot(
            factor_ref[low:high, :high], columns[:high], preferred_element_type=jnp.float32
        ).astype(jnp.bfloat16)
        total = total + lax.dot_general(
            fitted, fitted, (((0,), (0,)), ((), ())), preferred_element_type=jnp.float32
        )

    @pl.when(pl.program_id(0) == 0)
    def _():
        out_ref[...] = before_ref[...] + total

    @pl.when(pl.program_id(0) > 0)
    def _():
        out_ref[...] += total


def fit_exchange(factor, arrived, before):
    devices, own, aux_local, basis_total = arrived.shape
    aux_total = factor.shape[0]
    return pl.pallas_call(
        functools.partial(fit_kernel, aux_total // 8),
        out_shape=jax.ShapeDtypeStruct((basis_total, basis_total), jnp.float32),
        grid=(own,),
        in_specs=[
            pl.BlockSpec(
                (aux_total, aux_total), lambda k: (0, 0), pipeline_mode=pl.Buffered(1)
            ),
            pl.BlockSpec((devices, 1, aux_local, basis_total), lambda k: (0, k, 0, 0)),
            pl.BlockSpec((basis_total, basis_total), lambda k: (0, 0)),
        ],
        out_specs=pl.BlockSpec((basis_total, basis_total), lambda k: (0, 0)),
        compiler_params=pltpu.CompilerParams(vmem_limit_bytes=VMEM_BYTES),
        cost_estimate=pl.CostEstimate(
            flops=own * aux_total * basis_total * (aux_total * 9 // 8 + 2 * basis_total),
            bytes_accessed=(factor.size + arrived.size) * 2,
            transcendentals=0,
        ),
        name="fit_exchange",
    )(factor, arrived, before)


def per_device(integrals, pair_list, pair_count, coefficients, metric):
    devices = lax.axis_size("aux") * lax.axis_size("occ")
    basis_total = coefficients.shape[0]
    chunks = min(4, basis_total // devices)
    width = basis_total // chunks
    factor = lax.all_gather(metric, BOTH, axis=0, tiled=True)
    total = jnp.zeros((basis_total, basis_total), jnp.float32)
    state = (coefficients,)
    for chunk in range(chunks):
        rows, state = factor_rows(chunk * width, width, basis_total, state)
        half = half_transform(integrals, pair_list, pair_count, rows, chunk * width, devices)
        half, state = lax.optimization_barrier((half, state))
        arrived = lax.all_to_all(half, BOTH, split_axis=0, concat_axis=0, tiled=True)
        total = fit_exchange(factor, arrived, total)
    shares = total.reshape(devices, basis_total // devices, basis_total)
    return jnp.sum(lax.all_to_all(shares, BOTH, split_axis=0, concat_axis=0, tiled=True), axis=0)


def solution(mesh):
    in_specs = (
        P(("grp", "aux", "occ"), None, None, None, None),
        P(("grp", "aux", "occ"), None),
        P(("grp", "aux", "occ")),
        P("grp", None),
        P(("grp", "aux", "occ"), None),
    )
    out_specs = P(("grp", "aux", "occ"), None)
    return jax.shard_map(
        per_device, mesh=mesh, in_specs=in_specs, out_specs=out_specs, check_vma=False
    )
```

```python
import functools

import jax
import jax.numpy as jnp
from jax import lax
from jax.experimental import pallas as pl
from jax.experimental.pallas import tpu as pltpu
from jax.sharding import PartitionSpec as P

BOTH = ("aux", "occ")
VMEM_BYTES = 58 * 2**20
PANEL = 16
GROUP = 4
SCALE = 2.0**40
PIVOT_FLOOR = 1e-6


def root(value):
    return value * lax.rsqrt(jnp.maximum(value, 1e-37))


def factor_kernel(start, *refs):
    if start == 0:
        coef_ref, rows_ref, rest_ref, diag_ref = refs
        scaled = (coef_ref[...].astype(jnp.float32) * SCALE).astype(jnp.bfloat16)
        gram = lax.dot_general(
            scaled, scaled, (((1,), (1,)), ((), ())), preferred_element_type=jnp.float32
        )
        total = gram.shape[0]
        on_diagonal = lax.broadcasted_iota(jnp.int32, gram.shape, 0) == (
            lax.broadcasted_iota(jnp.int32, gram.shape, 1)
        )
        diagonal = jnp.sum(jnp.where(on_diagonal, gram, 0.0), axis=0, keepdims=True)
        which = lax.broadcasted_iota(jnp.int32, diag_ref.shape, 0)
        diag_ref[...] = jnp.where(
            which == 0, diagonal, jnp.maximum(diagonal * PIVOT_FLOOR, 1e-37)
        )
        rest_ref[...] = gram
    else:
        rest_in_ref, diag_in_ref, rows_ref, rest_ref, diag_ref = refs
        rest_ref[...] = rest_in_ref[...]
        diag_ref[...] = diag_in_ref[...]
        total = rest_ref.shape[1]
    own = rows_ref.shape[0] // 2
    lanes = min(total, 128)
    lane = lax.broadcasted_iota(jnp.int32, (PANEL, total), 1)
    row = lax.broadcasted_iota(jnp.int32, (PANEL, total), 0)
    row_of_column = lax.broadcasted_iota(jnp.int32, (PANEL, 1), 0)

    def panel(number, carry):
        low = pl.multiple_of(start + number * PANEL, PANEL)
        rest = rest_ref[pl.ds(low, PANEL), :]
        left = diag_ref[0:1, :]
        floor = diag_ref[1:2, :]
        on_diagonal = lane == low + row
        left_column = jnp.sum(jnp.where(on_diagonal, left, 0.0), axis=1, keepdims=True)
        floor_column = jnp.sum(jnp.where(on_diagonal, floor, 0.0), axis=1, keepdims=True)
        corner = rest[:, :lanes]
        for part in range(1, total // lanes):
            corner = jnp.where(
                low >= part * lanes, rest[:, part * lanes : (part + 1) * lanes], corner
            )
        corner = pltpu.roll(corner, lax.rem(lanes - lax.rem(low, lanes), lanes), 1)
        done = jnp.zeros((PANEL, total), jnp.float32)
        for t in range(PANEL):
            pivot = jnp.maximum(left_column[t : t + 1], floor_column[t : t + 1])
            inverse = lax.rsqrt(pivot)
            inverse = inverse * (1.5 - 0.5 * (pivot * inverse) * inverse)
            most = root(left)
            here = jnp.clip(rest[t : t + 1] * inverse, -most, most)
            here = jnp.where(lane[:1] > low + t, here, 0.0)
            left = jnp.maximum(left - here * here, 0.0)
            here = jnp.where(lane[:1] == low + t, pivot * inverse, here)
            done = jnp.where(row == t, here, done)
            most = root(left_column)
            weight = jnp.clip(corner[:, t : t + 1] * inverse, -most, most)
            weight = jnp.where(row_of_column > t, weight, 0.0)
            left_column = jnp.maximum(left_column - weight * weight, 0.0)
            rest = rest - weight * here
            corner = corner - weight * (corner[t : t + 1] * inverse)
        diag_ref[0:1, :] = left
        rest_ref[...] -= lax.dot_general(
            done,
            done,
            (((0,), (0,)), ((), ())),
            precision=lax.Precision.HIGHEST,
            preferred_element_type=jnp.float32,
        )
        done = done * (1.0 / SCALE)
        high = done.astype(jnp.bfloat16)
        place = pl.multiple_of(number * PANEL, PANEL)
        rows_ref[pl.ds(place, PANEL), :] = high
        rows_ref[pl.ds(own + place, PANEL), :] = (done - high.astype(jnp.float32)).astype(
            jnp.bfloat16
        )
        return carry

    lax.fori_loop(0, own // PANEL, panel, 0)


def factor_rows(start, own, total, operands):
    rows, rest, diagonals = pl.pallas_call(
        functools.partial(factor_kernel, start),
        out_shape=(
            jax.ShapeDtypeStruct((2 * own, total), jnp.bfloat16),
            jax.ShapeDtypeStruct((total, total), jnp.float32),
            jax.ShapeDtypeStruct((8, total), jnp.float32),
        ),
        compiler_params=pltpu.CompilerParams(vmem_limit_bytes=VMEM_BYTES),
        name="factor_rows",
    )(*operands)
    return rows, (rest, diagonals)


def half_kernel(low_block, list_ref, count_ref, ints_ref, basis_ref, out_ref, rows_ref, window_ref):
    block = pl.program_id(0)
    slots, aux_width, size_block = ints_ref.shape[1:4]
    vectors = basis_ref.shape[0] // 2
    side = basis_ref.shape[1] // size_block
    where_slot, is_used = [], []
    for pair in range(side * side):
        slot_of = jnp.int32(0)
        used = jnp.int32(0)
        for slot in range(slots):
            hit = jnp.logical_and(
                list_ref[block, slot] == pair, slot < count_ref[block]
            ).astype(jnp.int32)
            slot_of = slot_of + hit * slot
            used = used + hit
        where_slot.append(slot_of)
        is_used.append(used > 0)

    for m in range(side):
        for n in range(low_block, side):
            pair = m * side + n
            tile = ints_ref[0, where_slot[pair]]
            column = (n - low_block) * size_block
            window_ref[:, m * size_block : (m + 1) * size_block, column : column + size_block] = (
                jnp.where(is_used[pair], tile, jnp.zeros_like(tile))
            )

    def some(group, carry):
        low = group * GROUP
        window = window_ref[pl.ds(low, GROUP)]
        product = lax.dot_general(
            basis_ref[:, low_block * size_block :],
            window.reshape(GROUP * window.shape[1], window.shape[2]),
            (((1,), (1,)), ((), ())),
            preferred_element_type=jnp.float32,
        )
        product = product[:vectors] + product[vectors:]
        for p in range(GROUP):
            for m in range(side):
                column = (p * side + m) * size_block
                rows_ref[m, pl.ds(low + p, vectors, stride=aux_width), :] = product[
                    :, column : column + size_block
                ]
        return carry

    lax.fori_loop(0, aux_width // GROUP, some, 0)
    for m in range(side):
        out_ref[..., m * size_block : (m + 1) * size_block] = (
            rows_ref[m].astype(jnp.bfloat16).reshape(out_ref.shape[:-1] + (size_block,))
        )


def half_transform(integrals, pair_list, pair_count, basis_rows, start, devices):
    blocks, slots, aux_width, size_block, _ = integrals.shape
    vectors, basis_total = basis_rows.shape[0] // 2, basis_rows.shape[1]
    own = vectors // devices
    return pl.pallas_call(
        functools.partial(half_kernel, start // size_block),
        out_shape=jax.ShapeDtypeStruct(
            (devices, own, blocks * aux_width, basis_total), jnp.bfloat16
        ),
        grid_spec=pltpu.PrefetchScalarGridSpec(
            num_scalar_prefetch=2,
            grid=(blocks,),
            in_specs=[
                pl.BlockSpec(
                    (1, slots, aux_width, size_block, size_block), lambda b, *_: (b, 0, 0, 0, 0)
                ),
                pl.BlockSpec(basis_rows.shape, lambda b, *_: (0, 0)),
            ],
            out_specs=pl.BlockSpec(
                (devices, own, aux_width, basis_total), lambda b, *_: (0, 0, b, 0)
            ),
            scratch_shapes=[
                pltpu.VMEM(
                    (basis_total // size_block, vectors * aux_width, size_block), jnp.float32
                ),
                pltpu.VMEM(
                    (aux_width, basis_total, basis_total - start // size_block * size_block),
                    jnp.bfloat16,
                ),
            ],
        ),
        compiler_params=pltpu.CompilerParams(vmem_limit_bytes=VMEM_BYTES),
        cost_estimate=pl.CostEstimate(
            flops=4 * blocks * aux_width * vectors * basis_total * basis_total,
            bytes_accessed=integrals.size * 2 + vectors * blocks * aux_width * basis_total * 2,
            transcendentals=0,
        ),
        name="half_transform",
    )(pair_list, pair_count, integrals, basis_rows)


def fit_kernel(step_rows, factor_ref, half_ref, before_ref, out_ref):
    aux_total = factor_ref.shape[0]
    basis_total = out_ref.shape[0]
    steps = half_ref.shape[1]
    columns = jnp.concatenate(
        [half_ref[:, k].reshape(aux_total, basis_total) for k in range(steps)], axis=1
    )
    total = jnp.zeros(out_ref.shape, jnp.float32)
    for low in range(0, aux_total, step_rows):
        high = low + step_rows
        fitted = jnp.dot(
            factor_ref[low:high, :high], columns[:high], preferred_element_type=jnp.float32
        ).astype(jnp.bfloat16)
        for k in range(steps):
            one = fitted[:, k * basis_total : (k + 1) * basis_total]
            total = total + lax.dot_general(
                one, one, (((0,), (0,)), ((), ())), preferred_element_type=jnp.float32
            )

    @pl.when(pl.program_id(0) == 0)
    def _():
        out_ref[...] = before_ref[...] + total

    @pl.when(pl.program_id(0) > 0)
    def _():
        out_ref[...] += total


def fit_exchange(factor, arrived, before):
    devices, own, aux_local, basis_total = arrived.shape
    aux_total = factor.shape[0]
    steps = 2 if own % 2 == 0 else 1
    return pl.pallas_call(
        functools.partial(fit_kernel, aux_total // 8),
        out_shape=jax.ShapeDtypeStruct((basis_total, basis_total), jnp.float32),
        grid=(own // steps,),
        in_specs=[
            pl.BlockSpec(
                (aux_total, aux_total), lambda k: (0, 0), pipeline_mode=pl.Buffered(1)
            ),
            pl.BlockSpec((devices, steps, aux_local, basis_total), lambda k: (0, k, 0, 0)),
            pl.BlockSpec((basis_total, basis_total), lambda k: (0, 0)),
        ],
        out_specs=pl.BlockSpec((basis_total, basis_total), lambda k: (0, 0)),
        compiler_params=pltpu.CompilerParams(vmem_limit_bytes=VMEM_BYTES),
        cost_estimate=pl.CostEstimate(
            flops=own * aux_total * basis_total * (aux_total * 9 // 8 + 2 * basis_total),
            bytes_accessed=(factor.size + arrived.size) * 2,
            transcendentals=0,
        ),
        name="fit_exchange",
    )(factor, arrived, before)


def line_step(step, upward, downward, axis):
    devices = lax.axis_size(axis)
    upward = lax.ppermute(upward, axis, [(i, i + 1) for i in range(step, devices - 1)])
    downward = lax.ppermute(downward, axis, [(i, i - 1) for i in range(1, devices - step)])
    return upward, downward


def line_blocks(block, passed, axis):
    devices = lax.axis_size(axis)
    up, down = [pair[0] for pair in passed], [pair[1] for pair in passed]
    around = jnp.stack(up[::-1] + [block] + down)
    first = devices - 1 - lax.axis_index(axis)
    blocks = lax.dynamic_slice_in_dim(around, first, devices, 0)
    return blocks.reshape(devices * block.shape[0], block.shape[1])


def chunk_sizes(own):
    if own % 8 == 0:
        return [own // 8, 3 * own // 8, 3 * own // 8, own // 8]
    return [1] * own


def per_device(integrals, pair_list, pair_count, coefficients, metric):
    devices = lax.axis_size("aux") * lax.axis_size("occ")
    basis_total = coefficients.shape[0]
    passed = [line_step(0, metric, metric, "occ")]
    total = jnp.zeros((basis_total, basis_total), jnp.float32)
    state = (coefficients,)
    start = 0
    arrived = None
    factor = None
    waiting = []
    for chunk, own in enumerate(chunk_sizes(basis_total // devices)):
        width = own * devices
        rows, state = factor_rows(start, width, basis_total, state)
        if chunk == 0:
            rows, passed[0] = lax.optimization_barrier((rows, passed[0]))
            passed.append(line_step(1, *passed[0], "occ"))
        half = half_transform(integrals, pair_list, pair_count, rows, start, devices)
        if chunk == 0:
            half, state, passed[1] = lax.optimization_barrier((half, state, passed[1]))
            for step in range(2, lax.axis_size("occ") - 1):
                passed.append(line_step(step, *passed[-1], "occ"))
            line = line_blocks(metric, passed, "occ")
        elif chunk == 1:
            half, state, arrived, line = lax.optimization_barrier((half, state, arrived, line))
            factor = lax.all_gather(line, "aux", axis=0, tiled=True)
        elif chunk == 2:
            half, state, arrived, factor = lax.optimization_barrier(
                (half, state, arrived, factor)
            )
        else:
            half, state, arrived = lax.optimization_barrier((half, state, arrived))
        if chunk > 0:
            waiting.append(arrived)
        if chunk > 1:
            total = fit_exchange(factor, waiting.pop(0), total)
        arrived = lax.all_to_all(half, BOTH, split_axis=0, concat_axis=0, tiled=True)
        start += width
    for piece in waiting + [arrived]:
        total = fit_exchange(factor, piece, total)
    shares = total.reshape(devices, basis_total // devices, basis_total)
    return jnp.sum(lax.all_to_all(shares, BOTH, split_axis=0, concat_axis=0, tiled=True), axis=0)


def solution(mesh):
    in_specs = (
        P(("grp", "aux", "occ"), None, None, None, None),
        P(("grp", "aux", "occ"), None),
        P(("grp", "aux", "occ")),
        P("grp", None),
        P(("grp", "aux", "occ"), None),
    )
    out_specs = P(("grp", "aux", "occ"), None)
    return jax.shard_map(
        per_device, mesh=mesh, in_specs=in_specs, out_specs=out_specs, check_vma=False
    )
```

```python
import functools

import jax
import jax.numpy as jnp
from jax import lax
from jax.experimental import pallas as pl
from jax.experimental.pallas import tpu as pltpu
from jax.sharding import PartitionSpec as P

BOTH = ("aux", "occ")
VMEM_BYTES = 58 * 2**20
PANEL = 16
GROUP = 4
SCALE = 2.0**40
PIVOT_FLOOR = 1e-6


def root(value):
    return value * lax.rsqrt(jnp.maximum(value, 1e-37))


def factor_kernel(start, *refs):
    if start == 0:
        coef_ref, rows_ref, rest_ref, diag_ref = refs
        scaled = (coef_ref[...].astype(jnp.float32) * SCALE).astype(jnp.bfloat16)
        gram = lax.dot_general(
            scaled, scaled, (((1,), (1,)), ((), ())), preferred_element_type=jnp.float32
        )
        total = gram.shape[0]
        on_diagonal = lax.broadcasted_iota(jnp.int32, gram.shape, 0) == (
            lax.broadcasted_iota(jnp.int32, gram.shape, 1)
        )
        diagonal = jnp.sum(jnp.where(on_diagonal, gram, 0.0), axis=0, keepdims=True)
        which = lax.broadcasted_iota(jnp.int32, diag_ref.shape, 0)
        diag_ref[...] = jnp.where(
            which == 0, diagonal, jnp.maximum(diagonal * PIVOT_FLOOR, 1e-37)
        )
        rest_ref[...] = gram
    else:
        rest_in_ref, diag_in_ref, rows_ref, rest_ref, diag_ref = refs
        rest_ref[...] = rest_in_ref[...]
        diag_ref[...] = diag_in_ref[...]
        total = rest_ref.shape[1]
    own = rows_ref.shape[0] // 2
    lanes = min(total, 128)
    lane = lax.broadcasted_iota(jnp.int32, (PANEL, total), 1)
    row = lax.broadcasted_iota(jnp.int32, (PANEL, total), 0)
    row_of_column = lax.broadcasted_iota(jnp.int32, (PANEL, 1), 0)

    def panel(number, carry):
        low = pl.multiple_of(start + number * PANEL, PANEL)
        rest = rest_ref[pl.ds(low, PANEL), :]
        left = diag_ref[0:1, :]
        floor = diag_ref[1:2, :]
        on_diagonal = lane == low + row
        left_column = jnp.sum(jnp.where(on_diagonal, left, 0.0), axis=1, keepdims=True)
        floor_column = jnp.sum(jnp.where(on_diagonal, floor, 0.0), axis=1, keepdims=True)
        corner = rest[:, :lanes]
        for part in range(1, total // lanes):
            corner = jnp.where(
                low >= part * lanes, rest[:, part * lanes : (part + 1) * lanes], corner
            )
        corner = pltpu.roll(corner, lax.rem(lanes - lax.rem(low, lanes), lanes), 1)
        done = jnp.zeros((PANEL, total), jnp.float32)
        for t in range(PANEL):
            pivot = jnp.maximum(left_column[t : t + 1], floor_column[t : t + 1])
            inverse = lax.rsqrt(pivot)
            inverse = inverse * (1.5 - 0.5 * (pivot * inverse) * inverse)
            most = root(left)
            here = jnp.clip(rest[t : t + 1] * inverse, -most, most)
            here = jnp.where(lane[:1] > low + t, here, 0.0)
            left = jnp.maximum(left - here * here, 0.0)
            here = jnp.where(lane[:1] == low + t, pivot * inverse, here)
            done = jnp.where(row == t, here, done)
            most = root(left_column)
            weight = jnp.clip(corner[:, t : t + 1] * inverse, -most, most)
            weight = jnp.where(row_of_column > t, weight, 0.0)
            left_column = jnp.maximum(left_column - weight * weight, 0.0)
            rest = rest - weight * here
            corner = corner - weight * (corner[t : t + 1] * inverse)
        diag_ref[0:1, :] = left
        rest_ref[...] -= lax.dot_general(
            done,
            done,
            (((0,), (0,)), ((), ())),
            precision=lax.Precision.HIGHEST,
            preferred_element_type=jnp.float32,
        )
        done = done * (1.0 / SCALE)
        high = done.astype(jnp.bfloat16)
        place = pl.multiple_of(number * PANEL, PANEL)
        rows_ref[pl.ds(place, PANEL), :] = high
        rows_ref[pl.ds(own + place, PANEL), :] = (done - high.astype(jnp.float32)).astype(
            jnp.bfloat16
        )
        return carry

    lax.fori_loop(0, own // PANEL, panel, 0)


def factor_rows(start, own, total, operands):
    rows, rest, diagonals = pl.pallas_call(
        functools.partial(factor_kernel, start),
        out_shape=(
            jax.ShapeDtypeStruct((2 * own, total), jnp.bfloat16),
            jax.ShapeDtypeStruct((total, total), jnp.float32),
            jax.ShapeDtypeStruct((8, total), jnp.float32),
        ),
        compiler_params=pltpu.CompilerParams(vmem_limit_bytes=VMEM_BYTES),
        name="factor_rows",
    )(*operands)
    return rows, (rest, diagonals)


def half_kernel(low_block, list_ref, count_ref, me_ref, ints_ref, basis_ref, *refs):
    out_refs, (rows_ref, window_ref) = refs[:-2], refs[-2:]
    block = pl.program_id(0)
    slots, aux_width, size_block = ints_ref.shape[1:4]
    vectors = basis_ref.shape[0] // 2
    side = basis_ref.shape[1] // size_block
    where_slot, is_used = [], []
    for pair in range(side * side):
        slot_of = jnp.int32(0)
        used = jnp.int32(0)
        for slot in range(slots):
            hit = jnp.logical_and(
                list_ref[block, slot] == pair, slot < count_ref[block]
            ).astype(jnp.int32)
            slot_of = slot_of + hit * slot
            used = used + hit
        where_slot.append(slot_of)
        is_used.append(used > 0)

    for m in range(side):
        for n in range(low_block, side):
            pair = m * side + n
            tile = ints_ref[0, where_slot[pair]]
            column = (n - low_block) * size_block
            window_ref[:, m * size_block : (m + 1) * size_block, column : column + size_block] = (
                jnp.where(is_used[pair], tile, jnp.zeros_like(tile))
            )

    def some(group, carry):
        low = group * GROUP
        window = window_ref[pl.ds(low, GROUP)]
        product = lax.dot_general(
            basis_ref[:, low_block * size_block :],
            window.reshape(GROUP * window.shape[1], window.shape[2]),
            (((1,), (1,)), ((), ())),
            preferred_element_type=jnp.float32,
        )
        product = product[:vectors] + product[vectors:]
        for p in range(GROUP):
            for m in range(side):
                column = (p * side + m) * size_block
                rows_ref[m, pl.ds(low + p, vectors, stride=aux_width), :] = product[
                    :, column : column + size_block
                ]
        return carry

    lax.fori_loop(0, aux_width // GROUP, some, 0)
    share = vectors // len(out_refs) * aux_width
    for slot, out_ref in enumerate(out_refs):
        low = pl.multiple_of((me_ref[0] ^ slot) * share, share)
        for m in range(side):
            out_ref[..., m * size_block : (m + 1) * size_block] = (
                rows_ref[m, pl.ds(low, share), :]
                .astype(jnp.bfloat16)
                .reshape(out_ref.shape[:-1] + (size_block,))
            )


def half_transform(integrals, pair_list, pair_count, me, basis_rows, start, devices):
    blocks, slots, aux_width, size_block, _ = integrals.shape
    vectors, basis_total = basis_rows.shape[0] // 2, basis_rows.shape[1]
    own = vectors // devices
    return pl.pallas_call(
        functools.partial(half_kernel, start // size_block),
        out_shape=[
            jax.ShapeDtypeStruct((own, blocks * aux_width, basis_total), jnp.bfloat16)
        ]
        * devices,
        grid_spec=pltpu.PrefetchScalarGridSpec(
            num_scalar_prefetch=3,
            grid=(blocks,),
            in_specs=[
                pl.BlockSpec(
                    (1, slots, aux_width, size_block, size_block), lambda b, *_: (b, 0, 0, 0, 0)
                ),
                pl.BlockSpec(basis_rows.shape, lambda b, *_: (0, 0)),
            ],
            out_specs=[pl.BlockSpec((own, aux_width, basis_total), lambda b, *_: (0, b, 0))]
            * devices,
            scratch_shapes=[
                pltpu.VMEM(
                    (basis_total // size_block, vectors * aux_width, size_block), jnp.float32
                ),
                pltpu.VMEM(
                    (aux_width, basis_total, basis_total - start // size_block * size_block),
                    jnp.bfloat16,
                ),
            ],
        ),
        compiler_params=pltpu.CompilerParams(vmem_limit_bytes=VMEM_BYTES),
        cost_estimate=pl.CostEstimate(
            flops=4 * blocks * aux_width * vectors * basis_total * basis_total,
            bytes_accessed=integrals.size * 2 + vectors * blocks * aux_width * basis_total * 2,
            transcendentals=0,
        ),
        name="half_transform",
    )(pair_list, pair_count, me, integrals, basis_rows)


def fit_kernel(step_rows, me_ref, factor_ref, before_ref, *refs):
    half_refs, (out_ref, columns_ref) = refs[:-2], refs[-2:]
    aux_total = factor_ref.shape[0]
    basis_total = out_ref.shape[0]
    steps, aux_local = half_refs[0].shape[:2]
    for slot, half_ref in enumerate(half_refs):
        low = pl.multiple_of((me_ref[0] ^ slot) * aux_local, aux_local)
        for k in range(steps):
            columns_ref[pl.ds(low, aux_local), k * basis_total : (k + 1) * basis_total] = (
                half_ref[k]
            )
    total = jnp.zeros(out_ref.shape, jnp.float32)
    for low in range(0, aux_total, step_rows):
        high = low + step_rows
        fitted = jnp.dot(
            factor_ref[low:high, :high], columns_ref[:high], preferred_element_type=jnp.float32
        ).astype(jnp.bfloat16)
        for k in range(steps):
            one = fitted[:, k * basis_total : (k + 1) * basis_total]
            total = total + lax.dot_general(
                one, one, (((0,), (0,)), ((), ())), preferred_element_type=jnp.float32
            )

    @pl.when(pl.program_id(0) == 0)
    def _():
        out_ref[...] = before_ref[...] + total

    @pl.when(pl.program_id(0) > 0)
    def _():
        out_ref[...] += total


def fit_exchange(me, factor, arrived, before):
    own, aux_local, basis_total = arrived[0].shape
    aux_total = factor.shape[0]
    steps = 2 if own % 2 == 0 else 1
    return pl.pallas_call(
        functools.partial(fit_kernel, aux_total // 8),
        out_shape=jax.ShapeDtypeStruct((basis_total, basis_total), jnp.float32),
        grid_spec=pltpu.PrefetchScalarGridSpec(
            num_scalar_prefetch=1,
            grid=(own // steps,),
            in_specs=[
                pl.BlockSpec(
                    (aux_total, aux_total), lambda k, *_: (0, 0), pipeline_mode=pl.Buffered(1)
                ),
                pl.BlockSpec((basis_total, basis_total), lambda k, *_: (0, 0)),
            ]
            + [pl.BlockSpec((steps, aux_local, basis_total), lambda k, *_: (k, 0, 0))]
            * len(arrived),
            out_specs=pl.BlockSpec((basis_total, basis_total), lambda k, *_: (0, 0)),
            scratch_shapes=[pltpu.VMEM((aux_total, steps * basis_total), jnp.bfloat16)],
        ),
        compiler_params=pltpu.CompilerParams(vmem_limit_bytes=VMEM_BYTES),
        cost_estimate=pl.CostEstimate(
            flops=own * aux_total * basis_total * (aux_total * 9 // 8 + 2 * basis_total),
            bytes_accessed=(factor.size + own * aux_total * basis_total) * 2,
            transcendentals=0,
        ),
        name="fit_exchange",
    )(me, factor, before, *arrived)


def line_near(block):
    up = lax.ppermute(block, "occ", [(0, 1), (1, 2), (2, 3)])
    down = lax.ppermute(block, "occ", [(3, 2), (2, 1), (1, 0)])
    far = lax.ppermute(block, "occ", [(0, 2), (3, 1)])
    return up, down, far


def line_ends(block, up, down, far):
    me = lax.axis_index("occ")
    left = me < 2
    later = lax.ppermute(
        jnp.stack([jnp.where(left, down, up), far]), "occ", [(1, 0), (2, 3)]
    )
    order = lax.switch(
        me,
        [
            lambda: (block, down, later[0], later[1]),
            lambda: (up, block, down, far),
            lambda: (far, up, block, down),
            lambda: (later[1], later[0], up, block),
        ],
    )
    return jnp.concatenate(order)


def exchange(pieces):
    count = len(pieces)
    return [pieces[0]] + [
        lax.ppermute(pieces[slot], BOTH, [(i, i ^ slot) for i in range(count)])
        for slot in range(1, count)
    ]


def chunk_sizes(own):
    if own % 8 == 0:
        return [own // 8, 3 * own // 8, 3 * own // 8, own // 8]
    return [1] * own


def per_device(integrals, pair_list, pair_count, coefficients, metric):
    devices = lax.axis_size("aux") * lax.axis_size("occ")
    basis_total = coefficients.shape[0]
    me = lax.axis_index(BOTH).reshape(1)
    in_line = lax.axis_size("occ") == 4
    near = line_near(metric) if in_line else ()
    total = jnp.zeros((basis_total, basis_total), jnp.float32)
    state = (coefficients,)
    start = 0
    arrived = []
    factor = None
    for chunk, own in enumerate(chunk_sizes(basis_total // devices)):
        width = own * devices
        rows, state = factor_rows(start, width, basis_total, state)
        half = half_transform(integrals, pair_list, pair_count, me, rows, start, devices)
        if chunk == 0:
            half, state, near = lax.optimization_barrier((half, state, near))
            if in_line:
                factor = lax.all_gather(line_ends(metric, *near), "aux", axis=0, tiled=True)
            else:
                factor = lax.all_gather(metric, BOTH, axis=0, tiled=True)
        elif chunk == 2:
            half, state, arrived[0] = lax.optimization_barrier((half, state, arrived[0]))
        elif chunk > 2:
            half, state, arrived[chunk - 2], factor = lax.optimization_barrier(
                (half, state, arrived[chunk - 2], factor)
            )
        else:
            half, state = lax.optimization_barrier((half, state))
        arrived.append(exchange(half))
        start += width
    for pieces in arrived:
        total = fit_exchange(me, factor, pieces, total)
    shares = total.reshape(devices, basis_total // devices, basis_total)
    return jnp.sum(lax.all_to_all(shares, BOTH, split_axis=0, concat_axis=0, tiled=True), axis=0)


def solution(mesh):
    in_specs = (
        P(("grp", "aux", "occ"), None, None, None, None),
        P(("grp", "aux", "occ"), None),
        P(("grp", "aux", "occ")),
        P("grp", None),
        P(("grp", "aux", "occ"), None),
    )
    out_specs = P(("grp", "aux", "occ"), None)
    return jax.shard_map(
        per_device, mesh=mesh, in_specs=in_specs, out_specs=out_specs, check_vma=False
    )
```

```python
import functools

import jax
import jax.numpy as jnp
from jax import lax
from jax.experimental import pallas as pl
from jax.experimental.pallas import tpu as pltpu
from jax.sharding import PartitionSpec as P

BOTH = ("aux", "occ")
VMEM_BYTES = 58 * 2**20
PANEL = 16
GROUP = 4
SCALE = 2.0**40
PIVOT_FLOOR = 1e-6


def root(value):
    return value * lax.rsqrt(jnp.maximum(value, 1e-37))


def factor_kernel(start, *refs):
    if start == 0:
        coef_ref, rows_ref, rest_ref, diag_ref = refs
        scaled = (coef_ref[...].astype(jnp.float32) * SCALE).astype(jnp.bfloat16)
        gram = lax.dot_general(
            scaled, scaled, (((1,), (1,)), ((), ())), preferred_element_type=jnp.float32
        )
        total = gram.shape[0]
        on_diagonal = lax.broadcasted_iota(jnp.int32, gram.shape, 0) == (
            lax.broadcasted_iota(jnp.int32, gram.shape, 1)
        )
        diagonal = jnp.sum(jnp.where(on_diagonal, gram, 0.0), axis=0, keepdims=True)
        which = lax.broadcasted_iota(jnp.int32, diag_ref.shape, 0)
        diag_ref[...] = jnp.where(
            which == 0, diagonal, jnp.maximum(diagonal * PIVOT_FLOOR, 1e-37)
        )
        rest_ref[...] = gram
    else:
        rest_in_ref, diag_in_ref, rows_ref, rest_ref, diag_ref = refs
        rest_ref[...] = rest_in_ref[...]
        diag_ref[...] = diag_in_ref[...]
        total = rest_ref.shape[1]
    own = rows_ref.shape[0] // 2
    lanes = min(total, 128)
    lane = lax.broadcasted_iota(jnp.int32, (PANEL, total), 1)
    row = lax.broadcasted_iota(jnp.int32, (PANEL, total), 0)
    row_of_column = lax.broadcasted_iota(jnp.int32, (PANEL, 1), 0)

    def panel(number, carry):
        low = pl.multiple_of(start + number * PANEL, PANEL)
        rest = rest_ref[pl.ds(low, PANEL), :]
        left = diag_ref[0:1, :]
        floor = diag_ref[1:2, :]
        on_diagonal = lane == low + row
        left_column = jnp.sum(jnp.where(on_diagonal, left, 0.0), axis=1, keepdims=True)
        floor_column = jnp.sum(jnp.where(on_diagonal, floor, 0.0), axis=1, keepdims=True)
        corner = rest[:, :lanes]
        for part in range(1, total // lanes):
            corner = jnp.where(
                low >= part * lanes, rest[:, part * lanes : (part + 1) * lanes], corner
            )
        corner = pltpu.roll(corner, lax.rem(lanes - lax.rem(low, lanes), lanes), 1)
        done = jnp.zeros((PANEL, total), jnp.float32)
        for t in range(PANEL):
            pivot = jnp.maximum(left_column[t : t + 1], floor_column[t : t + 1])
            inverse = lax.rsqrt(pivot)
            inverse = inverse * (1.5 - 0.5 * (pivot * inverse) * inverse)
            most = root(left)
            here = jnp.clip(rest[t : t + 1] * inverse, -most, most)
            here = jnp.where(lane[:1] > low + t, here, 0.0)
            left = jnp.maximum(left - here * here, 0.0)
            here = jnp.where(lane[:1] == low + t, pivot * inverse, here)
            done = jnp.where(row == t, here, done)
            most = root(left_column)
            weight = jnp.clip(corner[:, t : t + 1] * inverse, -most, most)
            weight = jnp.where(row_of_column > t, weight, 0.0)
            left_column = jnp.maximum(left_column - weight * weight, 0.0)
            rest = rest - weight * here
            corner = corner - weight * (corner[t : t + 1] * inverse)
        diag_ref[0:1, :] = left
        rest_ref[...] -= lax.dot_general(
            done,
            done,
            (((0,), (0,)), ((), ())),
            precision=lax.Precision.HIGHEST,
            preferred_element_type=jnp.float32,
        )
        done = done * (1.0 / SCALE)
        high = done.astype(jnp.bfloat16)
        place = pl.multiple_of(number * PANEL, PANEL)
        rows_ref[pl.ds(place, PANEL), :] = high
        rows_ref[pl.ds(own + place, PANEL), :] = (done - high.astype(jnp.float32)).astype(
            jnp.bfloat16
        )
        return carry

    lax.fori_loop(0, own // PANEL, panel, 0)


def factor_rows(start, own, total, operands):
    rows, rest, diagonals = pl.pallas_call(
        functools.partial(factor_kernel, start),
        out_shape=(
            jax.ShapeDtypeStruct((2 * own, total), jnp.bfloat16),
            jax.ShapeDtypeStruct((total, total), jnp.float32),
            jax.ShapeDtypeStruct((8, total), jnp.float32),
        ),
        compiler_params=pltpu.CompilerParams(vmem_limit_bytes=VMEM_BYTES),
        name="factor_rows",
    )(*operands)
    return rows, (rest, diagonals)


def half_kernel(low_block, list_ref, count_ref, ints_ref, basis_ref, out_ref, rows_ref, window_ref):
    block = pl.program_id(0)
    slots, aux_width, size_block = ints_ref.shape[1:4]
    vectors = basis_ref.shape[0] // 2
    side = basis_ref.shape[1] // size_block
    where_slot, is_used = [], []
    for pair in range(side * side):
        slot_of = jnp.int32(0)
        used = jnp.int32(0)
        for slot in range(slots):
            hit = jnp.logical_and(
                list_ref[block, slot] == pair, slot < count_ref[block]
            ).astype(jnp.int32)
            slot_of = slot_of + hit * slot
            used = used + hit
        where_slot.append(slot_of)
        is_used.append(used > 0)

    for m in range(side):
        for n in range(low_block, side):
            pair = m * side + n
            tile = ints_ref[0, where_slot[pair]]
            column = (n - low_block) * size_block
            window_ref[:, m * size_block : (m + 1) * size_block, column : column + size_block] = (
                jnp.where(is_used[pair], tile, jnp.zeros_like(tile))
            )

    def some(group, carry):
        low = group * GROUP
        window = window_ref[pl.ds(low, GROUP)]
        product = lax.dot_general(
            basis_ref[:, low_block * size_block :],
            window.reshape(GROUP * window.shape[1], window.shape[2]),
            (((1,), (1,)), ((), ())),
            preferred_element_type=jnp.float32,
        )
        product = product[:vectors] + product[vectors:]
        for p in range(GROUP):
            for m in range(side):
                column = (p * side + m) * size_block
                rows_ref[m, pl.ds(low + p, vectors, stride=aux_width), :] = product[
                    :, column : column + size_block
                ]
        return carry

    lax.fori_loop(0, aux_width // GROUP, some, 0)
    for m in range(side):
        out_ref[..., m * size_block : (m + 1) * size_block] = (
            rows_ref[m].astype(jnp.bfloat16).reshape(out_ref.shape[:-1] + (size_block,))
        )


def half_transform(integrals, pair_list, pair_count, basis_rows, start, devices):
    blocks, slots, aux_width, size_block, _ = integrals.shape
    vectors, basis_total = basis_rows.shape[0] // 2, basis_rows.shape[1]
    own = vectors // devices
    return pl.pallas_call(
        functools.partial(half_kernel, start // size_block),
        out_shape=jax.ShapeDtypeStruct(
            (devices, own, blocks * aux_width, basis_total), jnp.bfloat16
        ),
        grid_spec=pltpu.PrefetchScalarGridSpec(
            num_scalar_prefetch=2,
            grid=(blocks,),
            in_specs=[
                pl.BlockSpec(
                    (1, slots, aux_width, size_block, size_block), lambda b, *_: (b, 0, 0, 0, 0)
                ),
                pl.BlockSpec(basis_rows.shape, lambda b, *_: (0, 0)),
            ],
            out_specs=pl.BlockSpec(
                (devices, own, aux_width, basis_total), lambda b, *_: (0, 0, b, 0)
            ),
            scratch_shapes=[
                pltpu.VMEM(
                    (basis_total // size_block, vectors * aux_width, size_block), jnp.float32
                ),
                pltpu.VMEM(
                    (aux_width, basis_total, basis_total - start // size_block * size_block),
                    jnp.bfloat16,
                ),
            ],
        ),
        compiler_params=pltpu.CompilerParams(vmem_limit_bytes=VMEM_BYTES),
        cost_estimate=pl.CostEstimate(
            flops=4 * blocks * aux_width * vectors * basis_total * basis_total,
            bytes_accessed=integrals.size * 2 + vectors * blocks * aux_width * basis_total * 2,
            transcendentals=0,
        ),
        name="half_transform",
    )(pair_list, pair_count, integrals, basis_rows)


def fit_kernel(step_rows, half_ref, before_ref, factor_ref, out_ref, lower_ref, sems):
    aux_total = factor_ref.shape[0]
    basis_total = out_ref.shape[0]
    steps = half_ref.shape[1]
    lows = range(0, aux_total, step_rows)
    copies = []
    for number, low in enumerate(lows):
        part = (slice(low, low + step_rows), slice(0, low + step_rows))
        copies.append(
            pltpu.make_async_copy(factor_ref.at[part], lower_ref.at[part], sems.at[number])
        )

    @pl.when(pl.program_id(0) == 0)
    def _():
        for copy in copies:
            copy.start()

    columns = jnp.concatenate(
        [half_ref[:, k].reshape(aux_total, basis_total) for k in range(steps)], axis=1
    )
    total = jnp.zeros(out_ref.shape, jnp.float32)
    for number, low in enumerate(lows):
        high = low + step_rows
        pl.when(pl.program_id(0) == 0)(copies[number].wait)
        fitted = jnp.dot(
            lower_ref[low:high, :high], columns[:high], preferred_element_type=jnp.float32
        ).astype(jnp.bfloat16)
        for k in range(steps):
            one = fitted[:, k * basis_total : (k + 1) * basis_total]
            total = total + lax.dot_general(
                one, one, (((0,), (0,)), ((), ())), preferred_element_type=jnp.float32
            )

    @pl.when(pl.program_id(0) == 0)
    def _():
        out_ref[...] = before_ref[...] + total

    @pl.when(pl.program_id(0) > 0)
    def _():
        out_ref[...] += total


def fit_exchange(factor, arrived, before):
    devices, own, aux_local, basis_total = arrived.shape
    aux_total = factor.shape[0]
    steps = 2 if own % 2 == 0 else 1
    return pl.pallas_call(
        functools.partial(fit_kernel, aux_total // 8),
        out_shape=jax.ShapeDtypeStruct((basis_total, basis_total), jnp.float32),
        grid=(own // steps,),
        in_specs=[
            pl.BlockSpec((devices, steps, aux_local, basis_total), lambda k: (0, k, 0, 0)),
            pl.BlockSpec((basis_total, basis_total), lambda k: (0, 0)),
            pl.BlockSpec(memory_space=pl.ANY),
        ],
        out_specs=pl.BlockSpec((basis_total, basis_total), lambda k: (0, 0)),
        scratch_shapes=[
            pltpu.VMEM((aux_total, aux_total), jnp.bfloat16),
            pltpu.SemaphoreType.DMA((8,)),
        ],
        compiler_params=pltpu.CompilerParams(vmem_limit_bytes=VMEM_BYTES),
        cost_estimate=pl.CostEstimate(
            flops=own * aux_total * basis_total * (aux_total * 9 // 8 + 2 * basis_total),
            bytes_accessed=(factor.size + arrived.size) * 2,
            transcendentals=0,
        ),
        name="fit_exchange",
    )(arrived, before, factor)


def chunk_sizes(own):
    if own % 16 == 0:
        return [own // 8, 3 * own // 8, 7 * own // 16, own // 16]
    return [1] * own


def per_device(integrals, pair_list, pair_count, coefficients, metric):
    devices = lax.axis_size("aux") * lax.axis_size("occ")
    basis_total = coefficients.shape[0]
    line = lax.all_gather(metric, "occ", axis=0, tiled=True)
    total = jnp.zeros((basis_total, basis_total), jnp.float32)
    state = (coefficients,)
    start = 0
    arrived = []
    factor = None
    for chunk, own in enumerate(chunk_sizes(basis_total // devices)):
        width = own * devices
        rows, state = factor_rows(start, width, basis_total, state)
        half = half_transform(integrals, pair_list, pair_count, rows, start, devices)
        if chunk == 0:
            half, state, line = lax.optimization_barrier((half, state, line))
            factor = lax.all_gather(line, "aux", axis=0, tiled=True)
        else:
            if chunk > 1:
                total = fit_exchange(factor, arrived[chunk - 2], total)
            half, state, arrived[chunk - 1], total = lax.optimization_barrier(
                (half, state, arrived[chunk - 1], total)
            )
        arrived.append(lax.all_to_all(half, BOTH, split_axis=0, concat_axis=0, tiled=True))
        start += width
    for piece in arrived[-2:]:
        total = fit_exchange(factor, piece, total)
    shares = total.reshape(devices, basis_total // devices, basis_total)
    return jnp.sum(lax.all_to_all(shares, BOTH, split_axis=0, concat_axis=0, tiled=True), axis=0)


def solution(mesh):
    in_specs = (
        P(("grp", "aux", "occ"), None, None, None, None),
        P(("grp", "aux", "occ"), None),
        P(("grp", "aux", "occ")),
        P("grp", None),
        P(("grp", "aux", "occ"), None),
    )
    out_specs = P(("grp", "aux", "occ"), None)
    return jax.shard_map(
        per_device, mesh=mesh, in_specs=in_specs, out_specs=out_specs, check_vma=False
    )
```

```python
import functools

import jax
import jax.numpy as jnp
from jax import lax
from jax.experimental import pallas as pl
from jax.experimental.pallas import tpu as pltpu
from jax.sharding import PartitionSpec as P

BOTH = ("aux", "occ")
VMEM_BYTES = 58 * 2**20
FIT_VMEM_BYTES = 63 * 2**20
PANEL = 16
GROUP = 4
SCALE = 2.0**40
PIVOT_FLOOR = 1e-6


def root(value):
    return value * lax.rsqrt(jnp.maximum(value, 1e-37))


def factor_kernel(start, *refs):
    if start == 0:
        coef_ref, rows_ref, rest_ref, diag_ref = refs
        scaled = (coef_ref[...].astype(jnp.float32) * SCALE).astype(jnp.bfloat16)
        gram = lax.dot_general(
            scaled, scaled, (((1,), (1,)), ((), ())), preferred_element_type=jnp.float32
        )
        total = gram.shape[0]
        on_diagonal = lax.broadcasted_iota(jnp.int32, gram.shape, 0) == (
            lax.broadcasted_iota(jnp.int32, gram.shape, 1)
        )
        diagonal = jnp.sum(jnp.where(on_diagonal, gram, 0.0), axis=0, keepdims=True)
        which = lax.broadcasted_iota(jnp.int32, diag_ref.shape, 0)
        diag_ref[...] = jnp.where(
            which == 0, diagonal, jnp.maximum(diagonal * PIVOT_FLOOR, 1e-37)
        )
        rest_ref[...] = gram
    else:
        rest_in_ref, diag_in_ref, rows_ref, rest_ref, diag_ref = refs
        rest_ref[...] = rest_in_ref[...]
        diag_ref[...] = diag_in_ref[...]
        total = rest_ref.shape[1]
    own = rows_ref.shape[0] // 2
    lanes = min(total, 128)
    lane = lax.broadcasted_iota(jnp.int32, (PANEL, total), 1)
    row = lax.broadcasted_iota(jnp.int32, (PANEL, total), 0)
    row_of_column = lax.broadcasted_iota(jnp.int32, (PANEL, 1), 0)

    def panel(number, carry):
        low = pl.multiple_of(start + number * PANEL, PANEL)
        rest = rest_ref[pl.ds(low, PANEL), :]
        left = diag_ref[0:1, :]
        floor = diag_ref[1:2, :]
        on_diagonal = lane == low + row
        left_column = jnp.sum(jnp.where(on_diagonal, left, 0.0), axis=1, keepdims=True)
        floor_column = jnp.sum(jnp.where(on_diagonal, floor, 0.0), axis=1, keepdims=True)
        corner = rest[:, :lanes]
        for part in range(1, total // lanes):
            corner = jnp.where(
                low >= part * lanes, rest[:, part * lanes : (part + 1) * lanes], corner
            )
        corner = pltpu.roll(corner, lax.rem(lanes - lax.rem(low, lanes), lanes), 1)
        done = jnp.zeros((PANEL, total), jnp.float32)
        for t in range(PANEL):
            pivot = jnp.maximum(left_column[t : t + 1], floor_column[t : t + 1])
            inverse = lax.rsqrt(pivot)
            inverse = inverse * (1.5 - 0.5 * (pivot * inverse) * inverse)
            most = root(left)
            here = jnp.clip(rest[t : t + 1] * inverse, -most, most)
            here = jnp.where(lane[:1] > low + t, here, 0.0)
            left = jnp.maximum(left - here * here, 0.0)
            here = jnp.where(lane[:1] == low + t, pivot * inverse, here)
            done = jnp.where(row == t, here, done)
            most = root(left_column)
            weight = jnp.clip(corner[:, t : t + 1] * inverse, -most, most)
            weight = jnp.where(row_of_column > t, weight, 0.0)
            left_column = jnp.maximum(left_column - weight * weight, 0.0)
            rest = rest - weight * here
            corner = corner - weight * (corner[t : t + 1] * inverse)
        diag_ref[0:1, :] = left
        rest_ref[...] -= lax.dot_general(
            done,
            done,
            (((0,), (0,)), ((), ())),
            precision=lax.Precision.HIGHEST,
            preferred_element_type=jnp.float32,
        )
        done = done * (1.0 / SCALE)
        high = done.astype(jnp.bfloat16)
        place = pl.multiple_of(number * PANEL, PANEL)
        rows_ref[pl.ds(place, PANEL), :] = high
        rows_ref[pl.ds(own + place, PANEL), :] = (done - high.astype(jnp.float32)).astype(
            jnp.bfloat16
        )
        return carry

    lax.fori_loop(0, own // PANEL, panel, 0)


def factor_rows(start, own, total, operands):
    rows, rest, diagonals = pl.pallas_call(
        functools.partial(factor_kernel, start),
        out_shape=(
            jax.ShapeDtypeStruct((2 * own, total), jnp.bfloat16),
            jax.ShapeDtypeStruct((total, total), jnp.float32),
            jax.ShapeDtypeStruct((8, total), jnp.float32),
        ),
        compiler_params=pltpu.CompilerParams(vmem_limit_bytes=VMEM_BYTES),
        name="factor_rows",
    )(*operands)
    return rows, (rest, diagonals)


def half_kernel(low_block, list_ref, count_ref, ints_ref, basis_ref, out_ref, rows_ref, window_ref):
    block = pl.program_id(0)
    slots, aux_width, size_block = ints_ref.shape[1:4]
    vectors = basis_ref.shape[0] // 2
    side = basis_ref.shape[1] // size_block
    where_slot, is_used = [], []
    for pair in range(side * side):
        slot_of = jnp.int32(0)
        used = jnp.int32(0)
        for slot in range(slots):
            hit = jnp.logical_and(
                list_ref[block, slot] == pair, slot < count_ref[block]
            ).astype(jnp.int32)
            slot_of = slot_of + hit * slot
            used = used + hit
        where_slot.append(slot_of)
        is_used.append(used > 0)

    for m in range(side):
        for n in range(low_block, side):
            pair = m * side + n
            tile = ints_ref[0, where_slot[pair]]
            column = (n - low_block) * size_block
            window_ref[:, m * size_block : (m + 1) * size_block, column : column + size_block] = (
                jnp.where(is_used[pair], tile, jnp.zeros_like(tile))
            )

    def some(group, carry):
        low = group * GROUP
        window = window_ref[pl.ds(low, GROUP)]
        product = lax.dot_general(
            basis_ref[:, low_block * size_block :],
            window.reshape(GROUP * window.shape[1], window.shape[2]),
            (((1,), (1,)), ((), ())),
            preferred_element_type=jnp.float32,
        )
        product = product[:vectors] + product[vectors:]
        for p in range(GROUP):
            for m in range(side):
                column = (p * side + m) * size_block
                rows_ref[m, pl.ds(low + p, vectors, stride=aux_width), :] = product[
                    :, column : column + size_block
                ]
        return carry

    lax.fori_loop(0, aux_width // GROUP, some, 0)
    for m in range(side):
        out_ref[..., m * size_block : (m + 1) * size_block] = (
            rows_ref[m].astype(jnp.bfloat16).reshape(out_ref.shape[:-1] + (size_block,))
        )


def half_transform(integrals, pair_list, pair_count, basis_rows, start, devices):
    blocks, slots, aux_width, size_block, _ = integrals.shape
    vectors, basis_total = basis_rows.shape[0] // 2, basis_rows.shape[1]
    own = vectors // devices
    return pl.pallas_call(
        functools.partial(half_kernel, start // size_block),
        out_shape=jax.ShapeDtypeStruct(
            (devices, own, blocks * aux_width, basis_total), jnp.bfloat16
        ),
        grid_spec=pltpu.PrefetchScalarGridSpec(
            num_scalar_prefetch=2,
            grid=(blocks,),
            in_specs=[
                pl.BlockSpec(
                    (1, slots, aux_width, size_block, size_block), lambda b, *_: (b, 0, 0, 0, 0)
                ),
                pl.BlockSpec(basis_rows.shape, lambda b, *_: (0, 0)),
            ],
            out_specs=pl.BlockSpec(
                (devices, own, aux_width, basis_total), lambda b, *_: (0, 0, b, 0)
            ),
            scratch_shapes=[
                pltpu.VMEM(
                    (basis_total // size_block, vectors * aux_width, size_block), jnp.float32
                ),
                pltpu.VMEM(
                    (aux_width, basis_total, basis_total - start // size_block * size_block),
                    jnp.bfloat16,
                ),
            ],
        ),
        compiler_params=pltpu.CompilerParams(vmem_limit_bytes=VMEM_BYTES),
        cost_estimate=pl.CostEstimate(
            flops=4 * blocks * aux_width * vectors * basis_total * basis_total,
            bytes_accessed=integrals.size * 2 + vectors * blocks * aux_width * basis_total * 2,
            transcendentals=0,
        ),
        name="half_transform",
    )(pair_list, pair_count, integrals, basis_rows)


def fit_kernel(step_rows, half_ref, before_ref, left_ref, right_ref, out_ref, lower_ref, sems):
    aux_total, split = left_ref.shape
    basis_total = out_ref.shape[0]
    steps = half_ref.shape[1]
    lows = range(0, aux_total, step_rows)
    copies = []
    for number, low in enumerate(lows):
        high = low + step_rows
        width = min(high, split)
        copies.append(
            [
                pltpu.make_async_copy(
                    left_ref.at[low:high, :width], lower_ref.at[low:high, :width], sems.at[0, number]
                )
            ]
        )
        if high > split:
            copies[-1].append(
                pltpu.make_async_copy(
                    right_ref.at[low:high, : high - split],
                    lower_ref.at[low:high, split:high],
                    sems.at[1, number],
                )
            )

    @pl.when(pl.program_id(0) == 0)
    def _():
        for pair in copies:
            for copy in pair:
                copy.start()

    columns = jnp.concatenate(
        [half_ref[:, k].reshape(aux_total, basis_total) for k in range(steps)], axis=1
    )
    total = jnp.zeros(out_ref.shape, jnp.float32)
    for number, low in enumerate(lows):
        high = low + step_rows

        @pl.when(pl.program_id(0) == 0)
        def _():
            for copy in copies[number]:
                copy.wait()

        fitted = jnp.dot(
            lower_ref[low:high, :high], columns[:high], preferred_element_type=jnp.float32
        ).astype(jnp.bfloat16)
        for k in range(steps):
            one = fitted[:, k * basis_total : (k + 1) * basis_total]
            total = total + lax.dot_general(
                one, one, (((0,), (0,)), ((), ())), preferred_element_type=jnp.float32
            )

    @pl.when(pl.program_id(0) == 0)
    def _():
        out_ref[...] = before_ref[...] + total

    @pl.when(pl.program_id(0) > 0)
    def _():
        out_ref[...] += total


def fit_exchange(factor, arrived, before):
    devices, own, aux_local, basis_total = arrived.shape
    aux_total = factor[0].shape[0]
    steps = 2 if own % 2 == 0 else 1
    return pl.pallas_call(
        functools.partial(fit_kernel, aux_total // 8),
        out_shape=jax.ShapeDtypeStruct((basis_total, basis_total), jnp.float32),
        grid=(own // steps,),
        in_specs=[
            pl.BlockSpec((devices, steps, aux_local, basis_total), lambda k: (0, k, 0, 0)),
            pl.BlockSpec((basis_total, basis_total), lambda k: (0, 0)),
            pl.BlockSpec(memory_space=pl.ANY),
            pl.BlockSpec(memory_space=pl.ANY),
        ],
        out_specs=pl.BlockSpec((basis_total, basis_total), lambda k: (0, 0)),
        scratch_shapes=[
            pltpu.VMEM((aux_total, aux_total), jnp.bfloat16),
            pltpu.SemaphoreType.DMA((2, 8)),
        ],
        compiler_params=pltpu.CompilerParams(vmem_limit_bytes=FIT_VMEM_BYTES),
        cost_estimate=pl.CostEstimate(
            flops=own * aux_total * basis_total * (aux_total * 9 // 8 + 2 * basis_total),
            bytes_accessed=(aux_total * aux_total + arrived.size) * 2,
            transcendentals=0,
        ),
        name="fit_exchange",
    )(arrived, before, *factor)


def chunk_sizes(own):
    if own % 8 == 0:
        return [own // 4, 5 * own // 8, own // 8]
    return [1] * own


def per_device(integrals, pair_list, pair_count, coefficients, metric):
    devices = lax.axis_size("aux") * lax.axis_size("occ")
    basis_total = coefficients.shape[0]
    split = metric.shape[1] * 5 // 8
    left, right = metric[:, :split], metric[:, split:]
    left = lax.all_gather(left, "occ", axis=0, tiled=True)
    total = jnp.zeros((basis_total, basis_total), jnp.float32)
    state = (coefficients,)
    start = 0
    arrived = []
    factor = None
    for chunk, own in enumerate(chunk_sizes(basis_total // devices)):
        width = own * devices
        rows, state = factor_rows(start, width, basis_total, state)
        half = half_transform(integrals, pair_list, pair_count, rows, start, devices)
        if chunk == 0:
            half, state, left, right = lax.optimization_barrier((half, state, left, right))
            right = lax.all_gather(right, "occ", axis=0, tiled=True)
            factor = [lax.all_gather(part, "aux", axis=0, tiled=True) for part in (left, right)]
        else:
            if chunk > 1:
                total = fit_exchange(factor, arrived[chunk - 2], total)
            half, state, arrived[chunk - 1], total = lax.optimization_barrier(
                (half, state, arrived[chunk - 1], total)
            )
        arrived.append(lax.all_to_all(half, BOTH, split_axis=0, concat_axis=0, tiled=True))
        start += width
    for piece in arrived[-2:]:
        total = fit_exchange(factor, piece, total)
    shares = total.reshape(devices, basis_total // devices, basis_total)
    return jnp.sum(lax.all_to_all(shares, BOTH, split_axis=0, concat_axis=0, tiled=True), axis=0)


def solution(mesh):
    in_specs = (
        P(("grp", "aux", "occ"), None, None, None, None),
        P(("grp", "aux", "occ"), None),
        P(("grp", "aux", "occ")),
        P("grp", None),
        P(("grp", "aux", "occ"), None),
    )
    out_specs = P(("grp", "aux", "occ"), None)
    return jax.shard_map(
        per_device, mesh=mesh, in_specs=in_specs, out_specs=out_specs, check_vma=False
    )
```

```python
import functools

import jax
import jax.numpy as jnp
from jax import lax
from jax.experimental import pallas as pl
from jax.experimental.pallas import tpu as pltpu
from jax.sharding import PartitionSpec as P

BOTH = ("aux", "occ")
VMEM_BYTES = 58 * 2**20
FIT_VMEM_BYTES = 63 * 2**20
PANEL = 16
GROUP = 4
SCALE = 2.0**40
PIVOT_FLOOR = 1e-6


def root(value):
    return value * lax.rsqrt(jnp.maximum(value, 1e-37))


def factor_kernel(start, *refs):
    if start == 0:
        coef_ref, rows_ref, rest_ref, diag_ref = refs
        scaled = (coef_ref[...].astype(jnp.float32) * SCALE).astype(jnp.bfloat16)
        gram = lax.dot_general(
            scaled, scaled, (((1,), (1,)), ((), ())), preferred_element_type=jnp.float32
        )
        total = gram.shape[0]
        on_diagonal = lax.broadcasted_iota(jnp.int32, gram.shape, 0) == (
            lax.broadcasted_iota(jnp.int32, gram.shape, 1)
        )
        diagonal = jnp.sum(jnp.where(on_diagonal, gram, 0.0), axis=0, keepdims=True)
        which = lax.broadcasted_iota(jnp.int32, diag_ref.shape, 0)
        diag_ref[...] = jnp.where(
            which == 0, diagonal, jnp.maximum(diagonal * PIVOT_FLOOR, 1e-37)
        )
        rest_ref[...] = gram
    else:
        rest_in_ref, diag_in_ref, rows_ref, rest_ref, diag_ref = refs
        rest_ref[...] = rest_in_ref[...]
        diag_ref[...] = diag_in_ref[...]
        total = rest_ref.shape[1]
    own = rows_ref.shape[0] // 2
    lanes = min(total, 128)
    parts = [slice(part * lanes, (part + 1) * lanes) for part in range(total // lanes)]
    row = lax.broadcasted_iota(jnp.int32, (PANEL, lanes), 0)
    lane = lax.broadcasted_iota(jnp.int32, (PANEL, lanes), 1)

    def panel(number, carry):
        low = pl.multiple_of(start + number * PANEL, PANEL)
        rest = [rest_ref[pl.ds(low, PANEL), part] for part in parts]
        left = [diag_ref[0:1, part] for part in parts]
        floor = [diag_ref[1:2, part] for part in parts]

        def as_column(values):
            picked = jnp.zeros((PANEL, lanes), jnp.float32)
            for part, value in zip(parts, values):
                picked = picked + jnp.where(lane + part.start == low + row, value, 0.0)
            return jnp.broadcast_to(jnp.sum(picked, axis=1, keepdims=True), (PANEL, lanes))

        left_column, floor_column = as_column(left), as_column(floor)
        corner = rest[0]
        for part, value in zip(parts[1:], rest[1:]):
            corner = jnp.where(low >= part.start, value, corner)
        corner = pltpu.roll(corner, lax.rem(lanes - lax.rem(low, lanes), lanes), 1)
        columns = [
            jnp.broadcast_to(corner[:, t : t + 1], (PANEL, lanes)) for t in range(PANEL)
        ]
        done = [jnp.zeros((PANEL, lanes), jnp.float32) for part in parts]
        for t in range(PANEL):
            pivot = jnp.maximum(left_column[t : t + 1], floor_column[t : t + 1])
            inverse = lax.rsqrt(pivot)
            inverse = inverse * (1.5 - 0.5 * (pivot * inverse) * inverse)
            most = root(left_column)
            weight = jnp.clip(columns[t] * inverse, -most, most)
            weight = jnp.where(row > t, weight, 0.0)
            left_column = jnp.maximum(left_column - weight * weight, 0.0)
            for s in range(t + 1, PANEL):
                columns[s] = columns[s] - weight * weight[s : s + 1]
            for i, part in enumerate(parts):
                place = lane[:1] + part.start
                most = root(left[i])
                here = jnp.clip(rest[i][t : t + 1] * inverse, -most, most)
                here = jnp.where(place > low + t, here, 0.0)
                left[i] = jnp.maximum(left[i] - here * here, 0.0)
                here = jnp.where(place == low + t, pivot * inverse, here)
                done[i] = jnp.where(row == t, here, done[i])
                rest[i] = rest[i] - weight * here
        for part, value in zip(parts, left):
            diag_ref[0:1, part] = value
        done = jnp.concatenate(done, axis=1)
        rest_ref[...] -= lax.dot_general(
            done,
            done,
            (((0,), (0,)), ((), ())),
            precision=lax.Precision.HIGHEST,
            preferred_element_type=jnp.float32,
        )
        done = done * (1.0 / SCALE)
        high = done.astype(jnp.bfloat16)
        place = pl.multiple_of(number * PANEL, PANEL)
        rows_ref[pl.ds(place, PANEL), :] = high
        rows_ref[pl.ds(own + place, PANEL), :] = (done - high.astype(jnp.float32)).astype(
            jnp.bfloat16
        )
        return carry

    lax.fori_loop(0, own // PANEL, panel, 0)


def factor_rows(start, own, total, operands):
    rows, rest, diagonals = pl.pallas_call(
        functools.partial(factor_kernel, start),
        out_shape=(
            jax.ShapeDtypeStruct((2 * own, total), jnp.bfloat16),
            jax.ShapeDtypeStruct((total, total), jnp.float32),
            jax.ShapeDtypeStruct((8, total), jnp.float32),
        ),
        compiler_params=pltpu.CompilerParams(vmem_limit_bytes=VMEM_BYTES),
        name="factor_rows",
    )(*operands)
    return rows, (rest, diagonals)


def half_kernel(low_block, list_ref, count_ref, basis_ref, *refs):
    tile_refs, (out_ref, rows_ref, window_ref) = refs[:-3], refs[-3:]
    block = pl.program_id(0)
    aux_width, size_block = tile_refs[0].shape[2:4]
    vectors = basis_ref.shape[0] // 2
    side = basis_ref.shape[1] // size_block
    pairs = [(m, n) for m in range(side) for n in range(low_block, side)]
    for (m, n), tile_ref in zip(pairs, tile_refs):
        used = jnp.bool_(False)
        for slot in range(list_ref.shape[0]):
            hit = jnp.logical_and(list_ref[slot, block] == m * side + n, slot < count_ref[block])
            used = jnp.logical_or(used, hit)
        tile = tile_ref[0, 0]
        column = (n - low_block) * size_block
        window_ref[:, m * size_block : (m + 1) * size_block, column : column + size_block] = (
            jnp.where(used, tile, jnp.zeros_like(tile))
        )

    def some(group, carry):
        low = group * GROUP
        window = window_ref[pl.ds(low, GROUP)]
        product = lax.dot_general(
            basis_ref[:, low_block * size_block :],
            window.reshape(GROUP * window.shape[1], window.shape[2]),
            (((1,), (1,)), ((), ())),
            preferred_element_type=jnp.float32,
        )
        product = product[:vectors] + product[vectors:]
        for p in range(GROUP):
            for m in range(side):
                column = (p * side + m) * size_block
                rows_ref[m, pl.ds(low + p, vectors, stride=aux_width), :] = product[
                    :, column : column + size_block
                ]
        return carry

    lax.fori_loop(0, aux_width // GROUP, some, 0)
    for m in range(side):
        out_ref[..., m * size_block : (m + 1) * size_block] = (
            rows_ref[m].astype(jnp.bfloat16).reshape(out_ref.shape[:-1] + (size_block,))
        )


def half_transform(integrals, pair_list, pair_count, basis_rows, start, devices):
    blocks, slots, aux_width, size_block, _ = integrals.shape
    vectors, basis_total = basis_rows.shape[0] // 2, basis_rows.shape[1]
    own = vectors // devices
    side = basis_total // size_block
    low_block = start // size_block

    def tile_spec(pair):
        def place(b, list_ref, count_ref):
            slot_of = jnp.int32(0)
            for slot in range(1, slots):
                slot_of = jnp.where(list_ref[slot, b] == pair, slot, slot_of)
            return b, slot_of, 0, 0, 0

        return pl.BlockSpec((1, 1, aux_width, size_block, size_block), place)

    tiles = [tile_spec(m * side + n) for m in range(side) for n in range(low_block, side)]
    return pl.pallas_call(
        functools.partial(half_kernel, low_block),
        out_shape=jax.ShapeDtypeStruct(
            (devices, own, blocks * aux_width, basis_total), jnp.bfloat16
        ),
        grid_spec=pltpu.PrefetchScalarGridSpec(
            num_scalar_prefetch=2,
            grid=(blocks,),
            in_specs=[pl.BlockSpec(basis_rows.shape, lambda b, *_: (0, 0))] + tiles,
            out_specs=pl.BlockSpec(
                (devices, own, aux_width, basis_total), lambda b, *_: (0, 0, b, 0)
            ),
            scratch_shapes=[
                pltpu.VMEM(
                    (basis_total // size_block, vectors * aux_width, size_block), jnp.float32
                ),
                pltpu.VMEM(
                    (aux_width, basis_total, basis_total - low_block * size_block),
                    jnp.bfloat16,
                ),
            ],
        ),
        compiler_params=pltpu.CompilerParams(vmem_limit_bytes=VMEM_BYTES),
        cost_estimate=pl.CostEstimate(
            flops=4 * blocks * aux_width * vectors * basis_total * basis_total,
            bytes_accessed=integrals.size * 2 + vectors * blocks * aux_width * basis_total * 2,
            transcendentals=0,
        ),
        name="half_transform",
    )(pair_list.T, pair_count, basis_rows, *[integrals] * len(tiles))


def fit_kernel(step_rows, before_ref, factor_ref, half_ref, out_ref, lower_ref, columns_ref, factor_sems, half_sems):
    step = pl.program_id(0)
    aux_total = factor_ref.shape[0]
    basis_total = out_ref.shape[0]
    width = columns_ref.shape[-1] // basis_total
    blocks = aux_total // step_rows
    sources = half_ref.shape[0] // blocks

    def factor_copy(number):
        low, high = number * step_rows, (number + 1) * step_rows
        part = (slice(low, high), slice(0, high))
        return pltpu.make_async_copy(
            factor_ref.at[part], lower_ref.at[part], factor_sems.at[number]
        )

    def half_copy(index, number, k):
        slot = lax.rem(index, 2)
        part = slice(number * sources, (number + 1) * sources)
        return pltpu.make_async_copy(
            half_ref.at[part, index * width + k],
            columns_ref.at[slot, part, :, k * basis_total : (k + 1) * basis_total],
            half_sems.at[slot, number, k],
        )

    def start_half(index):
        for number in range(blocks):
            for k in range(width):
                half_copy(index, number, k).start()

    @pl.when(step == 0)
    def _():
        for number in range(blocks):
            for k in range(width):
                half_copy(step, number, k).start()
            factor_copy(number).start()

    pl.when(step + 1 < pl.num_programs(0))(lambda: start_half(step + 1))

    total = jnp.zeros(out_ref.shape, jnp.float32)
    for number in range(blocks):
        low, high = number * step_rows, (number + 1) * step_rows
        for k in range(width):
            half_copy(step, number, k).wait()
        pl.when(step == 0)(lambda number=number: factor_copy(number).wait())
        columns = columns_ref[lax.rem(step, 2), : (number + 1) * sources]
        fitted = jnp.dot(
            lower_ref[low:high, :high],
            columns.reshape(high, columns.shape[-1]),
            preferred_element_type=jnp.float32,
        ).astype(jnp.bfloat16)
        for k in range(width):
            one = fitted[:, k * basis_total : (k + 1) * basis_total]
            total = total + lax.dot_general(
                one, one, (((0,), (0,)), ((), ())), preferred_element_type=jnp.float32
            )

    @pl.when(step == 0)
    def _():
        out_ref[...] = before_ref[...] + total

    @pl.when(step > 0)
    def _():
        out_ref[...] += total


def fit_exchange(factor, arrived, before):
    devices, own, aux_local, basis_total = arrived.shape
    aux_total = factor.shape[0]
    width = 2 if own % 2 == 0 else 1
    return pl.pallas_call(
        functools.partial(fit_kernel, aux_total // 8),
        out_shape=jax.ShapeDtypeStruct((basis_total, basis_total), jnp.float32),
        grid=(own // width,),
        in_specs=[
            pl.BlockSpec((basis_total, basis_total), lambda k: (0, 0)),
            pl.BlockSpec(memory_space=pl.ANY),
            pl.BlockSpec(memory_space=pl.ANY),
        ],
        out_specs=pl.BlockSpec((basis_total, basis_total), lambda k: (0, 0)),
        scratch_shapes=[
            pltpu.VMEM((aux_total, aux_total), jnp.bfloat16),
            pltpu.VMEM((2, devices, aux_local, width * basis_total), jnp.bfloat16),
            pltpu.SemaphoreType.DMA((8,)),
            pltpu.SemaphoreType.DMA((2, 8, width)),
        ],
        compiler_params=pltpu.CompilerParams(vmem_limit_bytes=FIT_VMEM_BYTES),
        cost_estimate=pl.CostEstimate(
            flops=own * aux_total * basis_total * (aux_total * 9 // 8 + 2 * basis_total),
            bytes_accessed=(factor.size + arrived.size) * 2,
            transcendentals=0,
        ),
        name="fit_exchange",
    )(before, factor, arrived)


def line_step(step, upward, downward, axis):
    devices = lax.axis_size(axis)
    upward = lax.ppermute(upward, axis, [(i, i + 1) for i in range(step, devices - 1)])
    downward = lax.ppermute(downward, axis, [(i, i - 1) for i in range(1, devices - step)])
    return upward, downward


def line_blocks(block, passed, axis):
    devices = lax.axis_size(axis)
    up, down = [pair[0] for pair in passed], [pair[1] for pair in passed]
    around = jnp.stack(up[::-1] + [block] + down)
    first = devices - 1 - lax.axis_index(axis)
    blocks = lax.dynamic_slice_in_dim(around, first, devices, 0)
    return blocks.reshape(devices * block.shape[0], block.shape[1])


def chunk_sizes(own):
    if own % 8 == 0:
        return [own // 8, 3 * own // 4, own // 8]
    return [1] * own


def per_device(integrals, pair_list, pair_count, coefficients, metric):
    devices = lax.axis_size("aux") * lax.axis_size("occ")
    basis_total = coefficients.shape[0]
    passed = [line_step(0, metric, metric, "occ")]
    total = jnp.zeros((basis_total, basis_total), jnp.float32)
    state = (coefficients,)
    start = 0
    arrived = []
    factor = None
    for chunk, own in enumerate(chunk_sizes(basis_total // devices)):
        width = own * devices
        rows, state = factor_rows(start, width, basis_total, state)
        half = half_transform(integrals, pair_list, pair_count, rows, start, devices)
        if chunk == 0:
            half, state, passed[0] = lax.optimization_barrier((half, state, passed[0]))
            for step in range(1, lax.axis_size("occ") - 1):
                passed.append(line_step(step, *passed[-1], "occ"))
            line = line_blocks(metric, passed, "occ")
        elif chunk == 1:
            half, state, arrived[0], line = lax.optimization_barrier(
                (half, state, arrived[0], line)
            )
            factor = lax.all_gather(line, "aux", axis=0, tiled=True)
        else:
            total = fit_exchange(factor, arrived[chunk - 2], total)
            half, state, arrived[chunk - 1], total = lax.optimization_barrier(
                (half, state, arrived[chunk - 1], total)
            )
        arrived.append(lax.all_to_all(half, BOTH, split_axis=0, concat_axis=0, tiled=True))
        start += width
    for piece in arrived[-2:]:
        total = fit_exchange(factor, piece, total)
    shares = total.reshape(devices, basis_total // devices, basis_total)
    return jnp.sum(lax.all_to_all(shares, BOTH, split_axis=0, concat_axis=0, tiled=True), axis=0)


def solution(mesh):
    in_specs = (
        P(("grp", "aux", "occ"), None, None, None, None),
        P(("grp", "aux", "occ"), None),
        P(("grp", "aux", "occ")),
        P("grp", None),
        P(("grp", "aux", "occ"), None),
    )
    out_specs = P(("grp", "aux", "occ"), None)
    return jax.shard_map(
        per_device, mesh=mesh, in_specs=in_specs, out_specs=out_specs, check_vma=False
    )
```

```python
import functools

import jax
import jax.numpy as jnp
from jax import lax
from jax.experimental import pallas as pl
from jax.experimental.pallas import tpu as pltpu
from jax.sharding import PartitionSpec as P

BOTH = ("aux", "occ")
VMEM_BYTES = 58 * 2**20
FIT_VMEM_BYTES = 63 * 2**20
PANEL = 16
SCALE = 2.0**40
PIVOT_FLOOR = 1e-6


def root(value):
    return value * lax.rsqrt(jnp.maximum(value, 1e-37))


def factor_kernel(start, *refs):
    if start == 0:
        coef_ref, rows_ref, rest_ref, diag_ref = refs
        scaled = (coef_ref[...].astype(jnp.float32) * SCALE).astype(jnp.bfloat16)
        gram = lax.dot_general(
            scaled, scaled, (((1,), (1,)), ((), ())), preferred_element_type=jnp.float32
        )
        total = gram.shape[0]
        on_diagonal = lax.broadcasted_iota(jnp.int32, gram.shape, 0) == (
            lax.broadcasted_iota(jnp.int32, gram.shape, 1)
        )
        diagonal = jnp.sum(jnp.where(on_diagonal, gram, 0.0), axis=0, keepdims=True)
        which = lax.broadcasted_iota(jnp.int32, diag_ref.shape, 0)
        diag_ref[...] = jnp.where(
            which == 0, diagonal, jnp.maximum(diagonal * PIVOT_FLOOR, 1e-37)
        )
        rest_ref[...] = gram
    else:
        rest_in_ref, diag_in_ref, rows_ref, rest_ref, diag_ref = refs
        rest_ref[...] = rest_in_ref[...]
        diag_ref[...] = diag_in_ref[...]
        total = rest_ref.shape[1]
    own = rows_ref.shape[0] // 2
    lanes = min(total, 128)
    parts = [slice(part * lanes, (part + 1) * lanes) for part in range(total // lanes)]
    row = lax.broadcasted_iota(jnp.int32, (PANEL, lanes), 0)
    lane = lax.broadcasted_iota(jnp.int32, (PANEL, lanes), 1)

    def panel(number, carry):
        low = pl.multiple_of(start + number * PANEL, PANEL)
        rest = [rest_ref[pl.ds(low, PANEL), part] for part in parts]
        left = [diag_ref[0:1, part] for part in parts]
        floor = [diag_ref[1:2, part] for part in parts]

        def as_column(values):
            picked = jnp.zeros((PANEL, lanes), jnp.float32)
            for part, value in zip(parts, values):
                picked = picked + jnp.where(lane + part.start == low + row, value, 0.0)
            return jnp.broadcast_to(jnp.sum(picked, axis=1, keepdims=True), (PANEL, lanes))

        left_column, floor_column = as_column(left), as_column(floor)
        corner = rest[0]
        for part, value in zip(parts[1:], rest[1:]):
            corner = jnp.where(low >= part.start, value, corner)
        corner = pltpu.roll(corner, lax.rem(lanes - lax.rem(low, lanes), lanes), 1)
        columns = [
            jnp.broadcast_to(corner[:, t : t + 1], (PANEL, lanes)) for t in range(PANEL)
        ]
        done = [jnp.zeros((PANEL, lanes), jnp.float32) for part in parts]
        for t in range(PANEL):
            pivot = jnp.maximum(left_column[t : t + 1], floor_column[t : t + 1])
            inverse = lax.rsqrt(pivot)
            inverse = inverse * (1.5 - 0.5 * (pivot * inverse) * inverse)
            most = root(left_column)
            weight = jnp.clip(columns[t] * inverse, -most, most)
            weight = jnp.where(row > t, weight, 0.0)
            left_column = jnp.maximum(left_column - weight * weight, 0.0)
            for s in range(t + 1, PANEL):
                columns[s] = columns[s] - weight * weight[s : s + 1]
            for i, part in enumerate(parts):
                place = lane[:1] + part.start
                most = root(left[i])
                here = jnp.clip(rest[i][t : t + 1] * inverse, -most, most)
                here = jnp.where(place > low + t, here, 0.0)
                left[i] = jnp.maximum(left[i] - here * here, 0.0)
                here = jnp.where(place == low + t, pivot * inverse, here)
                done[i] = jnp.where(row == t, here, done[i])
                rest[i] = rest[i] - weight * here
        for part, value in zip(parts, left):
            diag_ref[0:1, part] = value
        done = jnp.concatenate(done, axis=1)
        rest_ref[...] -= lax.dot_general(
            done,
            done,
            (((0,), (0,)), ((), ())),
            precision=lax.Precision.HIGHEST,
            preferred_element_type=jnp.float32,
        )
        done = done * (1.0 / SCALE)
        high = done.astype(jnp.bfloat16)
        place = pl.multiple_of(number * PANEL, PANEL)
        rows_ref[pl.ds(place, PANEL), :] = high
        rows_ref[pl.ds(own + place, PANEL), :] = (done - high.astype(jnp.float32)).astype(
            jnp.bfloat16
        )
        return carry

    lax.fori_loop(0, own // PANEL, panel, 0)


def factor_rows(start, own, total, operands):
    rows, rest, diagonals = pl.pallas_call(
        functools.partial(factor_kernel, start),
        out_shape=(
            jax.ShapeDtypeStruct((2 * own, total), jnp.bfloat16),
            jax.ShapeDtypeStruct((total, total), jnp.float32),
            jax.ShapeDtypeStruct((8, total), jnp.float32),
        ),
        compiler_params=pltpu.CompilerParams(vmem_limit_bytes=VMEM_BYTES),
        name="factor_rows",
    )(*operands)
    return rows, (rest, diagonals)


def half_kernel(low_block, list_ref, count_ref, basis_ref, *refs):
    tile_refs, (out_ref, rows_ref, window_ref) = refs[:-3], refs[-3:]
    block = pl.program_id(0)
    aux_width, size_block = tile_refs[0].shape[2:4]
    vectors = basis_ref.shape[0] // 2
    side = basis_ref.shape[1] // size_block
    pairs = [(m, n) for m in range(side) for n in range(low_block, side)]
    for (m, n), tile_ref in zip(pairs, tile_refs):
        used = jnp.bool_(False)
        for slot in range(list_ref.shape[0]):
            hit = jnp.logical_and(list_ref[slot, block] == m * side + n, slot < count_ref[block])
            used = jnp.logical_or(used, hit)
        tile = tile_ref[0, 0]
        column = (n - low_block) * size_block
        window_ref[:, m * size_block : (m + 1) * size_block, column : column + size_block] = (
            jnp.where(used, tile, jnp.zeros_like(tile))
        )

    together = aux_width if vectors <= 64 else 4

    def some(group, carry):
        low = group * together
        window = window_ref[pl.ds(low, together)]
        product = lax.dot_general(
            basis_ref[:, low_block * size_block :],
            window.reshape(together * window.shape[1], window.shape[2]),
            (((1,), (1,)), ((), ())),
            preferred_element_type=jnp.float32,
        )
        product = product[:vectors] + product[vectors:]
        for p in range(together):
            for m in range(side):
                column = (p * side + m) * size_block
                rows_ref[m, pl.ds(low + p, vectors, stride=aux_width), :] = product[
                    :, column : column + size_block
                ]
        return carry

    lax.fori_loop(0, aux_width // together, some, 0)
    for m in range(side):
        out_ref[..., m * size_block : (m + 1) * size_block] = (
            rows_ref[m].astype(jnp.bfloat16).reshape(out_ref.shape[:-1] + (size_block,))
        )


def half_transform(integrals, pair_list, pair_count, basis_rows, start, devices):
    blocks, slots, aux_width, size_block, _ = integrals.shape
    vectors, basis_total = basis_rows.shape[0] // 2, basis_rows.shape[1]
    own = vectors // devices
    side = basis_total // size_block
    low_block = start // size_block

    def tile_spec(pair):
        def place(b, list_ref, count_ref):
            slot_of = jnp.int32(0)
            for slot in range(1, slots):
                slot_of = jnp.where(list_ref[slot, b] == pair, slot, slot_of)
            return b, slot_of, 0, 0, 0

        return pl.BlockSpec((1, 1, aux_width, size_block, size_block), place)

    tiles = [tile_spec(m * side + n) for m in range(side) for n in range(low_block, side)]
    return pl.pallas_call(
        functools.partial(half_kernel, low_block),
        out_shape=jax.ShapeDtypeStruct(
            (devices, own, blocks * aux_width, basis_total), jnp.bfloat16
        ),
        grid_spec=pltpu.PrefetchScalarGridSpec(
            num_scalar_prefetch=2,
            grid=(blocks,),
            in_specs=[pl.BlockSpec(basis_rows.shape, lambda b, *_: (0, 0))] + tiles,
            out_specs=pl.BlockSpec(
                (devices, own, aux_width, basis_total), lambda b, *_: (0, 0, b, 0)
            ),
            scratch_shapes=[
                pltpu.VMEM(
                    (basis_total // size_block, vectors * aux_width, size_block), jnp.float32
                ),
                pltpu.VMEM(
                    (aux_width, basis_total, basis_total - low_block * size_block),
                    jnp.bfloat16,
                ),
            ],
        ),
        compiler_params=pltpu.CompilerParams(vmem_limit_bytes=VMEM_BYTES),
        cost_estimate=pl.CostEstimate(
            flops=4 * blocks * aux_width * vectors * basis_total * basis_total,
            bytes_accessed=integrals.size * 2 + vectors * blocks * aux_width * basis_total * 2,
            transcendentals=0,
        ),
        name="half_transform",
    )(pair_list.T, pair_count, basis_rows, *[integrals] * len(tiles))


def fit_kernel(
    step_rows,
    before_ref,
    factor_ref,
    half_ref,
    out_ref,
    sum_ref,
    lower_ref,
    columns_ref,
    sum_sem,
    factor_sems,
    half_sems,
):
    step = pl.program_id(0)
    aux_total = factor_ref.shape[0]
    basis_total = out_ref.shape[0]
    width = columns_ref.shape[-1] // basis_total
    blocks = aux_total // step_rows
    sources = half_ref.shape[0] // blocks
    sum_copy = pltpu.make_async_copy(before_ref, sum_ref, sum_sem)

    def factor_copy(number):
        low, high = number * step_rows, (number + 1) * step_rows
        part = (slice(low, high), slice(0, high))
        return pltpu.make_async_copy(
            factor_ref.at[part], lower_ref.at[part], factor_sems.at[number]
        )

    def half_copy(index, number, k):
        slot = lax.rem(index, 2)
        part = slice(number * sources, (number + 1) * sources)
        return pltpu.make_async_copy(
            half_ref.at[part, index * width + k],
            columns_ref.at[slot, part, :, k * basis_total : (k + 1) * basis_total],
            half_sems.at[slot, number, k],
        )

    def start_half(index):
        for number in range(blocks):
            for k in range(width):
                half_copy(index, number, k).start()

    @pl.when(step == 0)
    def _():
        for number in range(blocks):
            for k in range(width):
                half_copy(step, number, k).start()
            factor_copy(number).start()
        sum_copy.start()

    pl.when(step + 1 < pl.num_programs(0))(lambda: start_half(step + 1))

    total = jnp.zeros(out_ref.shape, jnp.float32)
    for number in range(blocks):
        low, high = number * step_rows, (number + 1) * step_rows
        for k in range(width):
            half_copy(step, number, k).wait()
        pl.when(step == 0)(lambda number=number: factor_copy(number).wait())
        columns = columns_ref[lax.rem(step, 2), : (number + 1) * sources]
        fitted = jnp.dot(
            lower_ref[low:high, :high],
            columns.reshape(high, columns.shape[-1]),
            preferred_element_type=jnp.float32,
        ).astype(jnp.bfloat16)
        for k in range(width):
            one = fitted[:, k * basis_total : (k + 1) * basis_total]
            total = total + lax.dot_general(
                one, one, (((0,), (0,)), ((), ())), preferred_element_type=jnp.float32
            )

    @pl.when(step == 0)
    def _():
        sum_copy.wait()
        out_ref[...] = sum_ref[...] + total

    @pl.when(step > 0)
    def _():
        out_ref[...] += total


def fit_exchange(factor, arrived, before):
    devices, own, aux_local, basis_total = arrived.shape
    aux_total = factor.shape[0]
    width = 2 if own % 2 == 0 else 1
    return pl.pallas_call(
        functools.partial(fit_kernel, aux_total // 8),
        out_shape=jax.ShapeDtypeStruct((basis_total, basis_total), jnp.float32),
        grid=(own // width,),
        in_specs=[
            pl.BlockSpec(memory_space=pl.ANY),
            pl.BlockSpec(memory_space=pl.ANY),
            pl.BlockSpec(memory_space=pl.ANY),
        ],
        out_specs=pl.BlockSpec((basis_total, basis_total), lambda k: (0, 0)),
        scratch_shapes=[
            pltpu.VMEM((basis_total, basis_total), jnp.float32),
            pltpu.VMEM((aux_total, aux_total), jnp.bfloat16),
            pltpu.VMEM((2, devices, aux_local, width * basis_total), jnp.bfloat16),
            pltpu.SemaphoreType.DMA,
            pltpu.SemaphoreType.DMA((8,)),
            pltpu.SemaphoreType.DMA((2, 8, width)),
        ],
        compiler_params=pltpu.CompilerParams(vmem_limit_bytes=FIT_VMEM_BYTES),
        cost_estimate=pl.CostEstimate(
            flops=own * aux_total * basis_total * (aux_total * 9 // 8 + 2 * basis_total),
            bytes_accessed=(factor.size + arrived.size) * 2,
            transcendentals=0,
        ),
        name="fit_exchange",
    )(before, factor, arrived)


def line_step(step, upward, downward, axis):
    devices = lax.axis_size(axis)
    upward = lax.ppermute(upward, axis, [(i, i + 1) for i in range(step, devices - 1)])
    downward = lax.ppermute(downward, axis, [(i, i - 1) for i in range(1, devices - step)])
    return upward, downward


def line_blocks(block, passed, axis):
    devices = lax.axis_size(axis)
    up, down = [pair[0] for pair in passed], [pair[1] for pair in passed]
    around = jnp.stack(up[::-1] + [block] + down)
    first = devices - 1 - lax.axis_index(axis)
    blocks = lax.dynamic_slice_in_dim(around, first, devices, 0)
    return blocks.reshape(devices * block.shape[0], block.shape[1])


def chunk_sizes(own):
    if own % 8 == 0:
        return [own // 8, 3 * own // 4, own // 8]
    return [1] * own


def per_device(integrals, pair_list, pair_count, coefficients, metric):
    devices = lax.axis_size("aux") * lax.axis_size("occ")
    basis_total = coefficients.shape[0]
    passed = [line_step(0, metric, metric, "occ")]
    total = jnp.zeros((basis_total, basis_total), jnp.float32)
    state = (coefficients,)
    start = 0
    arrived = []
    factor = None
    for chunk, own in enumerate(chunk_sizes(basis_total // devices)):
        width = own * devices
        rows, state = factor_rows(start, width, basis_total, state)
        half = half_transform(integrals, pair_list, pair_count, rows, start, devices)
        if chunk == 0:
            half, state, passed[0] = lax.optimization_barrier((half, state, passed[0]))
            for step in range(1, lax.axis_size("occ") - 1):
                passed.append(line_step(step, *passed[-1], "occ"))
            line = line_blocks(metric, passed, "occ")
            factor = lax.all_gather(line, "aux", axis=0, tiled=True)
        elif chunk == 1:
            half, state, arrived[0] = lax.optimization_barrier((half, state, arrived[0]))
        else:
            total = fit_exchange(factor, arrived[chunk - 2], total)
            half, state, arrived[chunk - 1], total = lax.optimization_barrier(
                (half, state, arrived[chunk - 1], total)
            )
        arrived.append(lax.all_to_all(half, BOTH, split_axis=0, concat_axis=0, tiled=True))
        start += width
    for piece in arrived[-2:]:
        total = fit_exchange(factor, piece, total)
    shares = total.reshape(devices, basis_total // devices, basis_total)
    return jnp.sum(lax.all_to_all(shares, BOTH, split_axis=0, concat_axis=0, tiled=True), axis=0)


def solution(mesh):
    in_specs = (
        P(("grp", "aux", "occ"), None, None, None, None),
        P(("grp", "aux", "occ"), None),
        P(("grp", "aux", "occ")),
        P("grp", None),
        P(("grp", "aux", "occ"), None),
    )
    out_specs = P(("grp", "aux", "occ"), None)
    return jax.shard_map(
        per_device, mesh=mesh, in_specs=in_specs, out_specs=out_specs, check_vma=False
    )
```

```python
import functools

import jax
import jax.numpy as jnp
from jax import lax
from jax.experimental import pallas as pl
from jax.experimental.pallas import tpu as pltpu
from jax.sharding import PartitionSpec as P

BOTH = ("aux", "occ")
VMEM_BYTES = 58 * 2**20
FIT_VMEM_BYTES = 63 * 2**20
PANEL = 16
SCALE = 2.0**40
PIVOT_FLOOR = 1e-6


def root(value):
    return value * lax.rsqrt(jnp.maximum(value, 1e-37))


def factor_kernel(start, *refs):
    if start == 0:
        coef_ref, rows_ref, rest_ref, diag_ref = refs
        scaled = (coef_ref[...].astype(jnp.float32) * SCALE).astype(jnp.bfloat16)
        gram = lax.dot_general(
            scaled, scaled, (((1,), (1,)), ((), ())), preferred_element_type=jnp.float32
        )
        total = gram.shape[0]
        on_diagonal = lax.broadcasted_iota(jnp.int32, gram.shape, 0) == (
            lax.broadcasted_iota(jnp.int32, gram.shape, 1)
        )
        diagonal = jnp.sum(jnp.where(on_diagonal, gram, 0.0), axis=0, keepdims=True)
        which = lax.broadcasted_iota(jnp.int32, diag_ref.shape, 0)
        diag_ref[...] = jnp.where(
            which == 0, diagonal, jnp.maximum(diagonal * PIVOT_FLOOR, 1e-37)
        )
        rest_ref[...] = gram
    else:
        rest_in_ref, diag_in_ref, rows_ref, rest_ref, diag_ref = refs
        rest_ref[...] = rest_in_ref[...]
        diag_ref[...] = diag_in_ref[...]
        total = rest_ref.shape[1]
    own = rows_ref.shape[0] // 2
    lanes = min(total, 128)
    parts = [slice(part * lanes, (part + 1) * lanes) for part in range(total // lanes)]
    row = lax.broadcasted_iota(jnp.int32, (PANEL, lanes), 0)
    lane = lax.broadcasted_iota(jnp.int32, (PANEL, lanes), 1)

    def panel(number, carry):
        low = pl.multiple_of(start + number * PANEL, PANEL)
        rest = [rest_ref[pl.ds(low, PANEL), part] for part in parts]
        left = [diag_ref[0:1, part] for part in parts]
        floor = [diag_ref[1:2, part] for part in parts]

        def as_column(values):
            picked = jnp.zeros((PANEL, lanes), jnp.float32)
            for part, value in zip(parts, values):
                picked = picked + jnp.where(lane + part.start == low + row, value, 0.0)
            return jnp.broadcast_to(jnp.sum(picked, axis=1, keepdims=True), (PANEL, lanes))

        left_column, floor_column = as_column(left), as_column(floor)
        corner = rest[0]
        for part, value in zip(parts[1:], rest[1:]):
            corner = jnp.where(low >= part.start, value, corner)
        corner = pltpu.roll(corner, lax.rem(lanes - lax.rem(low, lanes), lanes), 1)
        columns = [
            jnp.broadcast_to(corner[:, t : t + 1], (PANEL, lanes)) for t in range(PANEL)
        ]
        done = [jnp.zeros((PANEL, lanes), jnp.float32) for part in parts]
        for t in range(PANEL):
            pivot = jnp.maximum(left_column[t : t + 1], floor_column[t : t + 1])
            inverse = lax.rsqrt(pivot)
            inverse = inverse * (1.5 - 0.5 * (pivot * inverse) * inverse)
            most = root(left_column)
            weight = jnp.clip(columns[t] * inverse, -most, most)
            weight = jnp.where(row > t, weight, 0.0)
            left_column = jnp.maximum(left_column - weight * weight, 0.0)
            for s in range(t + 1, PANEL):
                columns[s] = columns[s] - weight * weight[s : s + 1]
            for i, part in enumerate(parts):
                place = lane[:1] + part.start
                most = root(left[i])
                here = jnp.clip(rest[i][t : t + 1] * inverse, -most, most)
                here = jnp.where(place > low + t, here, 0.0)
                left[i] = jnp.maximum(left[i] - here * here, 0.0)
                here = jnp.where(place == low + t, pivot * inverse, here)
                done[i] = jnp.where(row == t, here, done[i])
                rest[i] = rest[i] - weight * here
        for part, value in zip(parts, left):
            diag_ref[0:1, part] = value
        done = jnp.concatenate(done, axis=1)
        rest_ref[...] -= lax.dot_general(
            done,
            done,
            (((0,), (0,)), ((), ())),
            precision=lax.Precision.HIGHEST,
            preferred_element_type=jnp.float32,
        )
        done = done * (1.0 / SCALE)
        high = done.astype(jnp.bfloat16)
        place = pl.multiple_of(number * PANEL, PANEL)
        rows_ref[pl.ds(place, PANEL), :] = high
        rows_ref[pl.ds(own + place, PANEL), :] = (done - high.astype(jnp.float32)).astype(
            jnp.bfloat16
        )
        return carry

    lax.fori_loop(0, own // PANEL, panel, 0)


def factor_rows(start, own, total, operands):
    rows, rest, diagonals = pl.pallas_call(
        functools.partial(factor_kernel, start),
        out_shape=(
            jax.ShapeDtypeStruct((2 * own, total), jnp.bfloat16),
            jax.ShapeDtypeStruct((total, total), jnp.float32),
            jax.ShapeDtypeStruct((8, total), jnp.float32),
        ),
        compiler_params=pltpu.CompilerParams(vmem_limit_bytes=VMEM_BYTES),
        name="factor_rows",
    )(*operands)
    return rows, (rest, diagonals)


def half_kernel(low_block, list_ref, count_ref, basis_ref, *refs):
    tile_refs, (out_ref, rows_ref, window_ref) = refs[:-3], refs[-3:]
    block = pl.program_id(0)
    aux_width, size_block = tile_refs[0].shape[2:4]
    vectors = basis_ref.shape[0] // 2
    side = basis_ref.shape[1] // size_block
    pairs = [(m, n) for m in range(side) for n in range(low_block, side)]
    for (m, n), tile_ref in zip(pairs, tile_refs):
        used = jnp.bool_(False)
        for slot in range(list_ref.shape[0]):
            hit = jnp.logical_and(list_ref[slot, block] == m * side + n, slot < count_ref[block])
            used = jnp.logical_or(used, hit)
        tile = tile_ref[0, 0]
        column = (n - low_block) * size_block
        window_ref[:, m * size_block : (m + 1) * size_block, column : column + size_block] = (
            jnp.where(used, tile, jnp.zeros_like(tile))
        )

    together = aux_width if vectors <= 64 else 4

    def some(group, carry):
        low = group * together
        window = window_ref[pl.ds(low, together)]
        product = lax.dot_general(
            basis_ref[:, low_block * size_block :],
            window.reshape(together * window.shape[1], window.shape[2]),
            (((1,), (1,)), ((), ())),
            preferred_element_type=jnp.float32,
        )
        product = product[:vectors] + product[vectors:]
        for p in range(together):
            for m in range(side):
                column = (p * side + m) * size_block
                rows_ref[m, pl.ds(low + p, vectors, stride=aux_width), :] = product[
                    :, column : column + size_block
                ]
        return carry

    lax.fori_loop(0, aux_width // together, some, 0)
    for m in range(side):
        out_ref[..., m * size_block : (m + 1) * size_block] = (
            rows_ref[m].astype(jnp.bfloat16).reshape(out_ref.shape[:-1] + (size_block,))
        )


def half_transform(integrals, pair_list, pair_count, basis_rows, start, devices):
    blocks, slots, aux_width, size_block, _ = integrals.shape
    vectors, basis_total = basis_rows.shape[0] // 2, basis_rows.shape[1]
    own = vectors // devices
    side = basis_total // size_block
    low_block = start // size_block

    def tile_spec(pair):
        def place(b, list_ref, count_ref):
            slot_of = jnp.int32(0)
            for slot in range(1, slots):
                slot_of = jnp.where(list_ref[slot, b] == pair, slot, slot_of)
            return b, slot_of, 0, 0, 0

        return pl.BlockSpec((1, 1, aux_width, size_block, size_block), place)

    tiles = [tile_spec(m * side + n) for m in range(side) for n in range(low_block, side)]
    return pl.pallas_call(
        functools.partial(half_kernel, low_block),
        out_shape=jax.ShapeDtypeStruct(
            (devices, own, blocks * aux_width, basis_total), jnp.bfloat16
        ),
        grid_spec=pltpu.PrefetchScalarGridSpec(
            num_scalar_prefetch=2,
            grid=(blocks,),
            in_specs=[pl.BlockSpec(basis_rows.shape, lambda b, *_: (0, 0))] + tiles,
            out_specs=pl.BlockSpec(
                (devices, own, aux_width, basis_total), lambda b, *_: (0, 0, b, 0)
            ),
            scratch_shapes=[
                pltpu.VMEM(
                    (basis_total // size_block, vectors * aux_width, size_block), jnp.float32
                ),
                pltpu.VMEM(
                    (aux_width, basis_total, basis_total - low_block * size_block),
                    jnp.bfloat16,
                ),
            ],
        ),
        compiler_params=pltpu.CompilerParams(vmem_limit_bytes=VMEM_BYTES),
        cost_estimate=pl.CostEstimate(
            flops=4 * blocks * aux_width * vectors * basis_total * basis_total,
            bytes_accessed=integrals.size * 2 + vectors * blocks * aux_width * basis_total * 2,
            transcendentals=0,
        ),
        name="half_transform",
    )(pair_list.T, pair_count, basis_rows, *[integrals] * len(tiles))


def fit_kernel(
    step_rows,
    before_ref,
    factor_ref,
    half_ref,
    out_ref,
    sum_ref,
    lower_ref,
    columns_ref,
    sum_sem,
    factor_sems,
    half_sems,
):
    step = pl.program_id(0)
    aux_total = factor_ref.shape[0]
    basis_total = out_ref.shape[0]
    width = columns_ref.shape[-1] // basis_total
    blocks = aux_total // step_rows
    sources = half_ref.shape[0] // blocks
    sum_copy = pltpu.make_async_copy(before_ref, sum_ref, sum_sem)

    def factor_copy(number):
        low, high = number * step_rows, (number + 1) * step_rows
        part = (slice(low, high), slice(0, high))
        return pltpu.make_async_copy(
            factor_ref.at[part], lower_ref.at[part], factor_sems.at[number]
        )

    def half_copy(index, number, k):
        slot = lax.rem(index, 2)
        part = slice(number * sources, (number + 1) * sources)
        return pltpu.make_async_copy(
            half_ref.at[part, index * width + k],
            columns_ref.at[slot, part, :, k * basis_total : (k + 1) * basis_total],
            half_sems.at[slot, number, k],
        )

    def start_half(index):
        for number in range(blocks):
            for k in range(width):
                half_copy(index, number, k).start()

    @pl.when(step == 0)
    def _():
        for number in range(blocks):
            for k in range(width):
                half_copy(step, number, k).start()
            factor_copy(number).start()
        sum_copy.start()

    pl.when(step + 1 < pl.num_programs(0))(lambda: start_half(step + 1))

    total = jnp.zeros(out_ref.shape, jnp.float32)
    for number in range(blocks):
        low, high = number * step_rows, (number + 1) * step_rows
        for k in range(width):
            half_copy(step, number, k).wait()
        pl.when(step == 0)(lambda number=number: factor_copy(number).wait())
        columns = columns_ref[lax.rem(step, 2), : (number + 1) * sources]
        fitted = jnp.dot(
            lower_ref[low:high, :high],
            columns.reshape(high, columns.shape[-1]),
            preferred_element_type=jnp.float32,
        ).astype(jnp.bfloat16)
        for k in range(width):
            one = fitted[:, k * basis_total : (k + 1) * basis_total]
            total = total + lax.dot_general(
                one, one, (((0,), (0,)), ((), ())), preferred_element_type=jnp.float32
            )

    @pl.when(step == 0)
    def _():
        sum_copy.wait()
        out_ref[...] = sum_ref[...] + total

    @pl.when(step > 0)
    def _():
        out_ref[...] += total


def fit_exchange(factor, arrived, before):
    devices, own, aux_local, basis_total = arrived.shape
    aux_total = factor.shape[0]
    width = 2 if own % 2 == 0 else 1
    return pl.pallas_call(
        functools.partial(fit_kernel, aux_total // 8),
        out_shape=jax.ShapeDtypeStruct((basis_total, basis_total), jnp.float32),
        grid=(own // width,),
        in_specs=[
            pl.BlockSpec(memory_space=pl.ANY),
            pl.BlockSpec(memory_space=pl.ANY),
            pl.BlockSpec(memory_space=pl.ANY),
        ],
        out_specs=pl.BlockSpec((basis_total, basis_total), lambda k: (0, 0)),
        scratch_shapes=[
            pltpu.VMEM((basis_total, basis_total), jnp.float32),
            pltpu.VMEM((aux_total, aux_total), jnp.bfloat16),
            pltpu.VMEM((2, devices, aux_local, width * basis_total), jnp.bfloat16),
            pltpu.SemaphoreType.DMA,
            pltpu.SemaphoreType.DMA((8,)),
            pltpu.SemaphoreType.DMA((2, 8, width)),
        ],
        compiler_params=pltpu.CompilerParams(vmem_limit_bytes=FIT_VMEM_BYTES),
        cost_estimate=pl.CostEstimate(
            flops=own * aux_total * basis_total * (aux_total * 9 // 8 + 2 * basis_total),
            bytes_accessed=(factor.size + arrived.size) * 2,
            transcendentals=0,
        ),
        name="fit_exchange",
    )(before, factor, arrived)


def line_near(block):
    up = lax.ppermute(block, "occ", [(0, 1), (1, 2), (2, 3)])
    down = lax.ppermute(block, "occ", [(3, 2), (2, 1), (1, 0)])
    far = lax.ppermute(block, "occ", [(0, 2), (3, 1)])
    return up, down, far


def line_ends(block, up, down, far):
    me = lax.axis_index("occ")
    left = me < 2
    later = lax.ppermute(
        jnp.stack([jnp.where(left, down, up), far]), "occ", [(1, 0), (2, 3)]
    )
    order = lax.switch(
        me,
        [
            lambda: (block, down, later[0], later[1]),
            lambda: (up, block, down, far),
            lambda: (far, up, block, down),
            lambda: (later[1], later[0], up, block),
        ],
    )
    return jnp.concatenate(order)


def chunk_sizes(own):
    if own % 8 == 0:
        return [own // 8, 3 * own // 4, own // 8]
    return [1] * own


def per_device(integrals, pair_list, pair_count, coefficients, metric):
    devices = lax.axis_size("aux") * lax.axis_size("occ")
    basis_total = coefficients.shape[0]
    in_line = lax.axis_size("occ") == 4
    near = line_near(metric) if in_line else ()
    total = jnp.zeros((basis_total, basis_total), jnp.float32)
    state = (coefficients,)
    start = 0
    arrived = []
    factor = None
    for chunk, own in enumerate(chunk_sizes(basis_total // devices)):
        width = own * devices
        rows, state = factor_rows(start, width, basis_total, state)
        half = half_transform(integrals, pair_list, pair_count, rows, start, devices)
        if chunk == 0:
            half, state, near = lax.optimization_barrier((half, state, near))
            line = line_ends(metric, *near) if in_line else metric
        elif chunk == 1:
            half, state, line = lax.optimization_barrier((half, state, line))
            factor = lax.all_gather(line, "aux" if in_line else BOTH, axis=0, tiled=True)
        else:
            total = fit_exchange(factor, arrived[chunk - 2], total)
            half, state, arrived[chunk - 1], total = lax.optimization_barrier(
                (half, state, arrived[chunk - 1], total)
            )
        arrived.append(lax.all_to_all(half, BOTH, split_axis=0, concat_axis=0, tiled=True))
        start += width
    for piece in arrived[-2:]:
        total = fit_exchange(factor, piece, total)
    shares = total.reshape(devices, basis_total // devices, basis_total)
    return jnp.sum(lax.all_to_all(shares, BOTH, split_axis=0, concat_axis=0, tiled=True), axis=0)


def solution(mesh):
    in_specs = (
        P(("grp", "aux", "occ"), None, None, None, None),
        P(("grp", "aux", "occ"), None),
        P(("grp", "aux", "occ")),
        P("grp", None),
        P(("grp", "aux", "occ"), None),
    )
    out_specs = P(("grp", "aux", "occ"), None)
    return jax.shard_map(
        per_device, mesh=mesh, in_specs=in_specs, out_specs=out_specs, check_vma=False
    )
```

```python
import functools

import jax
import jax.numpy as jnp
from jax import lax
from jax.experimental import pallas as pl
from jax.experimental.pallas import tpu as pltpu
from jax.sharding import PartitionSpec as P

BOTH = ("aux", "occ")
VMEM_BYTES = 58 * 2**20
FIT_VMEM_BYTES = 63 * 2**20
PANEL = 16
SCALE = 2.0**40
PIVOT_FLOOR = 1e-6


def root(value):
    return value * lax.rsqrt(jnp.maximum(value, 1e-37))


def factor_kernel(start, *refs):
    if start == 0:
        coef_ref, rows_ref, rest_ref, diag_ref = refs
        scaled = (coef_ref[...].astype(jnp.float32) * SCALE).astype(jnp.bfloat16)
        gram = lax.dot_general(
            scaled, scaled, (((1,), (1,)), ((), ())), preferred_element_type=jnp.float32
        )
        total = gram.shape[0]
        on_diagonal = lax.broadcasted_iota(jnp.int32, gram.shape, 0) == (
            lax.broadcasted_iota(jnp.int32, gram.shape, 1)
        )
        diagonal = jnp.sum(jnp.where(on_diagonal, gram, 0.0), axis=0, keepdims=True)
        which = lax.broadcasted_iota(jnp.int32, diag_ref.shape, 0)
        diag_ref[...] = jnp.where(
            which == 0, diagonal, jnp.maximum(diagonal * PIVOT_FLOOR, 1e-37)
        )
        rest_ref[...] = gram
    else:
        rest_in_ref, diag_in_ref, rows_ref, rest_ref, diag_ref = refs
        rest_ref[...] = rest_in_ref[...]
        diag_ref[...] = diag_in_ref[...]
        total = rest_ref.shape[1]
    own = rows_ref.shape[0] // 2
    lanes = min(total, 128)
    parts = [slice(part * lanes, (part + 1) * lanes) for part in range(total // lanes)]
    row = lax.broadcasted_iota(jnp.int32, (PANEL, lanes), 0)
    lane = lax.broadcasted_iota(jnp.int32, (PANEL, lanes), 1)

    def panel(number, carry):
        low = pl.multiple_of(start + number * PANEL, PANEL)
        rest = [rest_ref[pl.ds(low, PANEL), part] for part in parts]
        left = [diag_ref[0:1, part] for part in parts]
        floor = [diag_ref[1:2, part] for part in parts]

        def as_column(values):
            picked = jnp.zeros((PANEL, lanes), jnp.float32)
            for part, value in zip(parts, values):
                picked = picked + jnp.where(lane + part.start == low + row, value, 0.0)
            return jnp.broadcast_to(jnp.sum(picked, axis=1, keepdims=True), (PANEL, lanes))

        left_column, floor_column = as_column(left), as_column(floor)
        corner = rest[0]
        for part, value in zip(parts[1:], rest[1:]):
            corner = jnp.where(low >= part.start, value, corner)
        corner = pltpu.roll(corner, lax.rem(lanes - lax.rem(low, lanes), lanes), 1)
        columns = [
            jnp.broadcast_to(corner[:, t : t + 1], (PANEL, lanes)) for t in range(PANEL)
        ]
        done = [jnp.zeros((PANEL, lanes), jnp.float32) for part in parts]
        for t in range(PANEL):
            pivot = jnp.maximum(left_column[t : t + 1], floor_column[t : t + 1])
            inverse = lax.rsqrt(pivot)
            inverse = inverse * (1.5 - 0.5 * (pivot * inverse) * inverse)
            most = root(left_column)
            weight = jnp.clip(columns[t] * inverse, -most, most)
            weight = jnp.where(row > t, weight, 0.0)
            left_column = jnp.maximum(left_column - weight * weight, 0.0)
            for s in range(t + 1, PANEL):
                columns[s] = columns[s] - weight * weight[s : s + 1]
            for i, part in enumerate(parts):
                place = lane[:1] + part.start
                most = root(left[i])
                here = jnp.clip(rest[i][t : t + 1] * inverse, -most, most)
                here = jnp.where(place > low + t, here, 0.0)
                left[i] = jnp.maximum(left[i] - here * here, 0.0)
                here = jnp.where(place == low + t, pivot * inverse, here)
                done[i] = jnp.where(row == t, here, done[i])
                rest[i] = rest[i] - weight * here
        for part, value in zip(parts, left):
            diag_ref[0:1, part] = value
        done = jnp.concatenate(done, axis=1)
        rest_ref[...] -= lax.dot_general(
            done,
            done,
            (((0,), (0,)), ((), ())),
            precision=lax.Precision.HIGHEST,
            preferred_element_type=jnp.float32,
        )
        done = done * (1.0 / SCALE)
        high = done.astype(jnp.bfloat16)
        place = pl.multiple_of(number * PANEL, PANEL)
        rows_ref[pl.ds(place, PANEL), :] = high
        rows_ref[pl.ds(own + place, PANEL), :] = (done - high.astype(jnp.float32)).astype(
            jnp.bfloat16
        )
        return carry

    lax.fori_loop(0, own // PANEL, panel, 0)


def factor_rows(start, own, total, operands):
    rows, rest, diagonals = pl.pallas_call(
        functools.partial(factor_kernel, start),
        out_shape=(
            jax.ShapeDtypeStruct((2 * own, total), jnp.bfloat16),
            jax.ShapeDtypeStruct((total, total), jnp.float32),
            jax.ShapeDtypeStruct((8, total), jnp.float32),
        ),
        compiler_params=pltpu.CompilerParams(vmem_limit_bytes=VMEM_BYTES),
        name="factor_rows",
    )(*operands)
    return rows, (rest, diagonals)


def half_kernel(low_block, list_ref, count_ref, basis_ref, *refs):
    tile_refs, (out_ref, rows_ref, window_ref) = refs[:-3], refs[-3:]
    block = pl.program_id(0)
    aux_width, size_block = tile_refs[0].shape[2:4]
    vectors = basis_ref.shape[0] // 2
    side = basis_ref.shape[1] // size_block
    pairs = [(m, n) for m in range(side) for n in range(low_block, side)]
    for (m, n), tile_ref in zip(pairs, tile_refs):
        used = jnp.bool_(False)
        for slot in range(list_ref.shape[0]):
            hit = jnp.logical_and(list_ref[slot, block] == m * side + n, slot < count_ref[block])
            used = jnp.logical_or(used, hit)
        tile = tile_ref[0, 0]
        column = (n - low_block) * size_block
        window_ref[:, m * size_block : (m + 1) * size_block, column : column + size_block] = (
            jnp.where(used, tile, jnp.zeros_like(tile))
        )

    together = aux_width if vectors <= 64 else 4

    def some(group, carry):
        low = group * together
        window = window_ref[pl.ds(low, together)]
        product = lax.dot_general(
            basis_ref[:, low_block * size_block :],
            window.reshape(together * window.shape[1], window.shape[2]),
            (((1,), (1,)), ((), ())),
            preferred_element_type=jnp.float32,
        )
        product = product[:vectors] + product[vectors:]
        for p in range(together):
            for m in range(side):
                column = (p * side + m) * size_block
                rows_ref[m, pl.ds(low + p, vectors, stride=aux_width), :] = product[
                    :, column : column + size_block
                ]
        return carry

    lax.fori_loop(0, aux_width // together, some, 0)
    for m in range(side):
        out_ref[..., m * size_block : (m + 1) * size_block] = (
            rows_ref[m].astype(jnp.bfloat16).reshape(out_ref.shape[:-1] + (size_block,))
        )


def half_transform(integrals, pair_list, pair_count, basis_rows, start, devices):
    blocks, slots, aux_width, size_block, _ = integrals.shape
    vectors, basis_total = basis_rows.shape[0] // 2, basis_rows.shape[1]
    own = vectors // devices
    side = basis_total // size_block
    low_block = start // size_block

    def tile_spec(pair):
        def place(b, list_ref, count_ref):
            slot_of = jnp.int32(0)
            for slot in range(1, slots):
                slot_of = jnp.where(list_ref[slot, b] == pair, slot, slot_of)
            return b, slot_of, 0, 0, 0

        return pl.BlockSpec((1, 1, aux_width, size_block, size_block), place)

    tiles = [tile_spec(m * side + n) for m in range(side) for n in range(low_block, side)]
    return pl.pallas_call(
        functools.partial(half_kernel, low_block),
        out_shape=jax.ShapeDtypeStruct(
            (devices, own, blocks * aux_width, basis_total), jnp.bfloat16
        ),
        grid_spec=pltpu.PrefetchScalarGridSpec(
            num_scalar_prefetch=2,
            grid=(blocks,),
            in_specs=[pl.BlockSpec(basis_rows.shape, lambda b, *_: (0, 0))] + tiles,
            out_specs=pl.BlockSpec(
                (devices, own, aux_width, basis_total), lambda b, *_: (0, 0, b, 0)
            ),
            scratch_shapes=[
                pltpu.VMEM(
                    (basis_total // size_block, vectors * aux_width, size_block), jnp.float32
                ),
                pltpu.VMEM(
                    (aux_width, basis_total, basis_total - low_block * size_block),
                    jnp.bfloat16,
                ),
            ],
        ),
        compiler_params=pltpu.CompilerParams(vmem_limit_bytes=VMEM_BYTES),
        cost_estimate=pl.CostEstimate(
            flops=4 * blocks * aux_width * vectors * basis_total * basis_total,
            bytes_accessed=integrals.size * 2 + vectors * blocks * aux_width * basis_total * 2,
            transcendentals=0,
        ),
        name="half_transform",
    )(pair_list.T, pair_count, basis_rows, *[integrals] * len(tiles))


def fit_kernel(
    step_rows,
    before_ref,
    factor_ref,
    half_ref,
    out_ref,
    sum_ref,
    lower_ref,
    columns_ref,
    sum_sem,
    factor_sems,
    half_sems,
):
    step = pl.program_id(0)
    aux_total = factor_ref.shape[0]
    basis_total = out_ref.shape[0]
    width = columns_ref.shape[-1] // basis_total
    blocks = aux_total // step_rows
    sources = half_ref.shape[0] // blocks
    sum_copy = pltpu.make_async_copy(before_ref, sum_ref, sum_sem)

    def factor_copy(number):
        low, high = number * step_rows, (number + 1) * step_rows
        part = (slice(low, high), slice(0, high))
        return pltpu.make_async_copy(
            factor_ref.at[part], lower_ref.at[part], factor_sems.at[number]
        )

    def half_copy(index, number, k):
        slot = lax.rem(index, 2)
        part = slice(number * sources, (number + 1) * sources)
        return pltpu.make_async_copy(
            half_ref.at[part, index * width + k],
            columns_ref.at[slot, part, :, k * basis_total : (k + 1) * basis_total],
            half_sems.at[slot, number, k],
        )

    def start_half(index):
        for number in range(blocks):
            for k in range(width):
                half_copy(index, number, k).start()

    @pl.when(step == 0)
    def _():
        for number in range(blocks):
            for k in range(width):
                half_copy(step, number, k).start()
            factor_copy(number).start()
        sum_copy.start()

    pl.when(step + 1 < pl.num_programs(0))(lambda: start_half(step + 1))

    total = jnp.zeros(out_ref.shape, jnp.float32)
    for number in range(blocks):
        low, high = number * step_rows, (number + 1) * step_rows
        for k in range(width):
            half_copy(step, number, k).wait()
        pl.when(step == 0)(lambda number=number: factor_copy(number).wait())
        columns = columns_ref[lax.rem(step, 2), : (number + 1) * sources]
        fitted = jnp.dot(
            lower_ref[low:high, :high],
            columns.reshape(high, columns.shape[-1]),
            preferred_element_type=jnp.float32,
        ).astype(jnp.bfloat16)
        for k in range(width):
            one = fitted[:, k * basis_total : (k + 1) * basis_total]
            total = total + lax.dot_general(
                one, one, (((0,), (0,)), ((), ())), preferred_element_type=jnp.float32
            )

    @pl.when(step == 0)
    def _():
        sum_copy.wait()
        out_ref[...] = sum_ref[...] + total

    @pl.when(step > 0)
    def _():
        out_ref[...] += total


def fit_exchange(factor, arrived, before):
    devices, own, aux_local, basis_total = arrived.shape
    aux_total = factor.shape[0]
    width = 2 if own % 2 == 0 else 1
    return pl.pallas_call(
        functools.partial(fit_kernel, aux_total // 8),
        out_shape=jax.ShapeDtypeStruct((basis_total, basis_total), jnp.float32),
        grid=(own // width,),
        in_specs=[
            pl.BlockSpec(memory_space=pl.ANY),
            pl.BlockSpec(memory_space=pl.ANY),
            pl.BlockSpec(memory_space=pl.ANY),
        ],
        out_specs=pl.BlockSpec((basis_total, basis_total), lambda k: (0, 0)),
        scratch_shapes=[
            pltpu.VMEM((basis_total, basis_total), jnp.float32),
            pltpu.VMEM((aux_total, aux_total), jnp.bfloat16),
            pltpu.VMEM((2, devices, aux_local, width * basis_total), jnp.bfloat16),
            pltpu.SemaphoreType.DMA,
            pltpu.SemaphoreType.DMA((8,)),
            pltpu.SemaphoreType.DMA((2, 8, width)),
        ],
        compiler_params=pltpu.CompilerParams(vmem_limit_bytes=FIT_VMEM_BYTES),
        cost_estimate=pl.CostEstimate(
            flops=own * aux_total * basis_total * (aux_total * 9 // 8 + 2 * basis_total),
            bytes_accessed=(factor.size + arrived.size) * 2,
            transcendentals=0,
        ),
        name="fit_exchange",
    )(before, factor, arrived)


def line_near(block):
    up = lax.ppermute(block, "occ", [(0, 1), (1, 2), (2, 3)])
    down = lax.ppermute(block, "occ", [(3, 2), (2, 1), (1, 0)])
    far = lax.ppermute(block, "occ", [(0, 2), (3, 1)])
    return up, down, far


def line_ends(block, up, down, far):
    me = lax.axis_index("occ")
    left = me < 2
    later = lax.ppermute(
        jnp.stack([jnp.where(left, down, up), far]), "occ", [(1, 0), (2, 3)]
    )
    order = lax.switch(
        me,
        [
            lambda: (block, down, later[0], later[1]),
            lambda: (up, block, down, far),
            lambda: (far, up, block, down),
            lambda: (later[1], later[0], up, block),
        ],
    )
    return jnp.concatenate(order)


def chunk_sizes(own):
    if own % 8 == 0:
        return [own // 4, 5 * own // 8, own // 8]
    return [1] * own


def per_device(integrals, pair_list, pair_count, coefficients, metric):
    devices = lax.axis_size("aux") * lax.axis_size("occ")
    basis_total = coefficients.shape[0]
    in_line = lax.axis_size("occ") == 4
    near = line_near(metric) if in_line else ()
    total = jnp.zeros((basis_total, basis_total), jnp.float32)
    state = (coefficients,)
    start = 0
    arrived = []
    factor = None
    for chunk, own in enumerate(chunk_sizes(basis_total // devices)):
        width = own * devices
        rows, state = factor_rows(start, width, basis_total, state)
        half = half_transform(integrals, pair_list, pair_count, rows, start, devices)
        if chunk == 0:
            half, state, near = lax.optimization_barrier((half, state, near))
            line = line_ends(metric, *near) if in_line else metric
        elif chunk == 1:
            half, state, line = lax.optimization_barrier((half, state, line))
            factor = lax.all_gather(line, "aux" if in_line else BOTH, axis=0, tiled=True)
        else:
            total = fit_exchange(factor, arrived[chunk - 2], total)
            half, state, arrived[chunk - 1], total = lax.optimization_barrier(
                (half, state, arrived[chunk - 1], total)
            )
        arrived.append(lax.all_to_all(half, BOTH, split_axis=0, concat_axis=0, tiled=True))
        start += width
    for piece in arrived[-2:]:
        total = fit_exchange(factor, piece, total)
    shares = total.reshape(devices, basis_total // devices, basis_total)
    return jnp.sum(lax.all_to_all(shares, BOTH, split_axis=0, concat_axis=0, tiled=True), axis=0)


def solution(mesh):
    in_specs = (
        P(("grp", "aux", "occ"), None, None, None, None),
        P(("grp", "aux", "occ"), None),
        P(("grp", "aux", "occ")),
        P("grp", None),
        P(("grp", "aux", "occ"), None),
    )
    out_specs = P(("grp", "aux", "occ"), None)
    return jax.shard_map(
        per_device, mesh=mesh, in_specs=in_specs, out_specs=out_specs, check_vma=False
    )
```

```python
import functools

import jax
import jax.numpy as jnp
from jax import lax
from jax.experimental import pallas as pl
from jax.experimental.pallas import tpu as pltpu
from jax.sharding import PartitionSpec as P

BOTH = ("aux", "occ")
VMEM_BYTES = 58 * 2**20
FIT_VMEM_BYTES = 63 * 2**20
PANEL = 16
SCALE = 2.0**40
PIVOT_FLOOR = 1e-6


def root(value):
    return value * lax.rsqrt(jnp.maximum(value, 1e-37))


def factor_kernel(start, *refs):
    if start == 0:
        coef_ref, rows_ref, rest_ref, diag_ref = refs
        scaled = (coef_ref[...].astype(jnp.float32) * SCALE).astype(jnp.bfloat16)
        gram = lax.dot_general(
            scaled, scaled, (((1,), (1,)), ((), ())), preferred_element_type=jnp.float32
        )
        total = gram.shape[0]
        on_diagonal = lax.broadcasted_iota(jnp.int32, gram.shape, 0) == (
            lax.broadcasted_iota(jnp.int32, gram.shape, 1)
        )
        diagonal = jnp.sum(jnp.where(on_diagonal, gram, 0.0), axis=0, keepdims=True)
        which = lax.broadcasted_iota(jnp.int32, diag_ref.shape, 0)
        diag_ref[...] = jnp.where(
            which == 0, diagonal, jnp.maximum(diagonal * PIVOT_FLOOR, 1e-37)
        )
        rest_ref[...] = gram
    else:
        rest_in_ref, diag_in_ref, rows_ref, rest_ref, diag_ref = refs
        rest_ref[...] = rest_in_ref[...]
        diag_ref[...] = diag_in_ref[...]
        total = rest_ref.shape[1]
    own = rows_ref.shape[0] // 2
    lanes = min(total, 128)
    parts = [slice(part * lanes, (part + 1) * lanes) for part in range(total // lanes)]
    row = lax.broadcasted_iota(jnp.int32, (PANEL, lanes), 0)
    lane = lax.broadcasted_iota(jnp.int32, (PANEL, lanes), 1)

    def panel(number, carry):
        low = pl.multiple_of(start + number * PANEL, PANEL)
        rest = [rest_ref[pl.ds(low, PANEL), part] for part in parts]
        left = [diag_ref[0:1, part] for part in parts]
        floor = [diag_ref[1:2, part] for part in parts]

        def as_column(values):
            picked = jnp.zeros((PANEL, lanes), jnp.float32)
            for part, value in zip(parts, values):
                picked = picked + jnp.where(lane + part.start == low + row, value, 0.0)
            return jnp.broadcast_to(jnp.sum(picked, axis=1, keepdims=True), (PANEL, lanes))

        left_column, floor_column = as_column(left), as_column(floor)
        corner = rest[0]
        for part, value in zip(parts[1:], rest[1:]):
            corner = jnp.where(low >= part.start, value, corner)
        corner = pltpu.roll(corner, lax.rem(lanes - lax.rem(low, lanes), lanes), 1)
        columns = [
            jnp.broadcast_to(corner[:, t : t + 1], (PANEL, lanes)) for t in range(PANEL)
        ]
        done = [jnp.zeros((PANEL, lanes), jnp.float32) for part in parts]
        for t in range(PANEL):
            pivot = jnp.maximum(left_column[t : t + 1], floor_column[t : t + 1])
            inverse = lax.rsqrt(pivot)
            inverse = inverse * (1.5 - 0.5 * (pivot * inverse) * inverse)
            most = root(left_column)
            weight = jnp.clip(columns[t] * inverse, -most, most)
            weight = jnp.where(row > t, weight, 0.0)
            left_column = jnp.maximum(left_column - weight * weight, 0.0)
            for s in range(t + 1, PANEL):
                columns[s] = columns[s] - weight * weight[s : s + 1]
            for i, part in enumerate(parts):
                place = lane[:1] + part.start
                most = root(left[i])
                here = jnp.clip(rest[i][t : t + 1] * inverse, -most, most)
                here = jnp.where(place > low + t, here, 0.0)
                left[i] = jnp.maximum(left[i] - here * here, 0.0)
                here = jnp.where(place == low + t, pivot * inverse, here)
                done[i] = jnp.where(row == t, here, done[i])
                rest[i] = rest[i] - weight * here
        for part, value in zip(parts, left):
            diag_ref[0:1, part] = value
        done = jnp.concatenate(done, axis=1)
        rest_ref[...] -= lax.dot_general(
            done,
            done,
            (((0,), (0,)), ((), ())),
            precision=lax.Precision.HIGHEST,
            preferred_element_type=jnp.float32,
        )
        done = done * (1.0 / SCALE)
        high = done.astype(jnp.bfloat16)
        place = pl.multiple_of(number * PANEL, PANEL)
        rows_ref[pl.ds(place, PANEL), :] = high
        rows_ref[pl.ds(own + place, PANEL), :] = (done - high.astype(jnp.float32)).astype(
            jnp.bfloat16
        )
        return carry

    lax.fori_loop(0, own // PANEL, panel, 0)


def factor_rows(start, own, total, operands):
    rows, rest, diagonals = pl.pallas_call(
        functools.partial(factor_kernel, start),
        out_shape=(
            jax.ShapeDtypeStruct((2 * own, total), jnp.bfloat16),
            jax.ShapeDtypeStruct((total, total), jnp.float32),
            jax.ShapeDtypeStruct((8, total), jnp.float32),
        ),
        compiler_params=pltpu.CompilerParams(vmem_limit_bytes=VMEM_BYTES),
        name="factor_rows",
    )(*operands)
    return rows, (rest, diagonals)


def half_kernel(low_block, list_ref, count_ref, basis_ref, *refs):
    tile_refs, (out_ref, rows_ref) = refs[:-2], refs[-2:]
    block = pl.program_id(0)
    aux_width, size_block = tile_refs[0].shape[2:4]
    vectors = basis_ref.shape[0] // 2
    side = basis_ref.shape[1] // size_block
    columns = range(low_block, side)
    for m in range(side):
        basis = []
        for n in columns:
            used = jnp.bool_(False)
            for slot in range(list_ref.shape[0]):
                hit = jnp.logical_and(
                    list_ref[slot, block] == m * side + n, slot < count_ref[block]
                )
                used = jnp.logical_or(used, hit)
            part = basis_ref[:, n * size_block : (n + 1) * size_block]
            basis.append(jnp.where(used, part, jnp.zeros_like(part)))
        tiles = [
            tile_refs[m * len(columns) + i][0, 0].reshape(aux_width * size_block, size_block)
            for i in range(len(columns))
        ]
        product = lax.dot_general(
            jnp.concatenate(basis, axis=1),
            jnp.concatenate(tiles, axis=1),
            (((1,), (1,)), ((), ())),
            preferred_element_type=jnp.float32,
        )
        product = product[:vectors] + product[vectors:]
        for p in range(aux_width):
            rows_ref[m, pl.ds(p, vectors, stride=aux_width), :] = product[
                :, p * size_block : (p + 1) * size_block
            ]
    for m in range(side):
        out_ref[..., m * size_block : (m + 1) * size_block] = (
            rows_ref[m].astype(jnp.bfloat16).reshape(out_ref.shape[:-1] + (size_block,))
        )


def half_transform(integrals, pair_list, pair_count, basis_rows, start, devices):
    blocks, slots, aux_width, size_block, _ = integrals.shape
    vectors, basis_total = basis_rows.shape[0] // 2, basis_rows.shape[1]
    own = vectors // devices
    side = basis_total // size_block
    low_block = start // size_block

    def tile_spec(pair):
        def place(b, list_ref, count_ref):
            slot_of = jnp.int32(0)
            for slot in range(1, slots):
                slot_of = jnp.where(list_ref[slot, b] == pair, slot, slot_of)
            return b, slot_of, 0, 0, 0

        return pl.BlockSpec((1, 1, aux_width, size_block, size_block), place)

    tiles = [tile_spec(m * side + n) for m in range(side) for n in range(low_block, side)]
    return pl.pallas_call(
        functools.partial(half_kernel, low_block),
        out_shape=jax.ShapeDtypeStruct(
            (devices, own, blocks * aux_width, basis_total), jnp.bfloat16
        ),
        grid_spec=pltpu.PrefetchScalarGridSpec(
            num_scalar_prefetch=2,
            grid=(blocks,),
            in_specs=[pl.BlockSpec(basis_rows.shape, lambda b, *_: (0, 0))] + tiles,
            out_specs=pl.BlockSpec(
                (devices, own, aux_width, basis_total), lambda b, *_: (0, 0, b, 0)
            ),
            scratch_shapes=[
                pltpu.VMEM(
                    (basis_total // size_block, vectors * aux_width, size_block), jnp.float32
                ),
            ],
        ),
        compiler_params=pltpu.CompilerParams(vmem_limit_bytes=VMEM_BYTES),
        cost_estimate=pl.CostEstimate(
            flops=4 * blocks * aux_width * vectors * basis_total * basis_total,
            bytes_accessed=integrals.size * 2 + vectors * blocks * aux_width * basis_total * 2,
            transcendentals=0,
        ),
        name="half_transform",
    )(pair_list.T, pair_count, basis_rows, *[integrals] * len(tiles))


def fit_kernel(
    step_rows,
    before_ref,
    factor_ref,
    half_ref,
    out_ref,
    sum_ref,
    lower_ref,
    columns_ref,
    sum_sem,
    factor_sems,
    half_sems,
):
    step = pl.program_id(0)
    aux_total = factor_ref.shape[0]
    basis_total = out_ref.shape[0]
    width = columns_ref.shape[-1] // basis_total
    blocks = aux_total // step_rows
    sources = half_ref.shape[0] // blocks
    sum_copy = pltpu.make_async_copy(before_ref, sum_ref, sum_sem)

    def factor_copy(number):
        low, high = number * step_rows, (number + 1) * step_rows
        part = (slice(low, high), slice(0, high))
        return pltpu.make_async_copy(
            factor_ref.at[part], lower_ref.at[part], factor_sems.at[number]
        )

    def half_copy(index, number, k):
        slot = lax.rem(index, 2)
        part = slice(number * sources, (number + 1) * sources)
        return pltpu.make_async_copy(
            half_ref.at[part, index * width + k],
            columns_ref.at[slot, part, :, k * basis_total : (k + 1) * basis_total],
            half_sems.at[slot, number, k],
        )

    def start_half(index):
        for number in range(blocks):
            for k in range(width):
                half_copy(index, number, k).start()

    @pl.when(step == 0)
    def _():
        for number in range(blocks):
            for k in range(width):
                half_copy(step, number, k).start()
            factor_copy(number).start()
        sum_copy.start()

    pl.when(step + 1 < pl.num_programs(0))(lambda: start_half(step + 1))

    total = jnp.zeros(out_ref.shape, jnp.float32)
    for number in range(blocks):
        low, high = number * step_rows, (number + 1) * step_rows
        for k in range(width):
            half_copy(step, number, k).wait()
        pl.when(step == 0)(lambda number=number: factor_copy(number).wait())
        columns = columns_ref[lax.rem(step, 2), : (number + 1) * sources]
        fitted = jnp.dot(
            lower_ref[low:high, :high],
            columns.reshape(high, columns.shape[-1]),
            preferred_element_type=jnp.float32,
        ).astype(jnp.bfloat16)
        for k in range(width):
            one = fitted[:, k * basis_total : (k + 1) * basis_total]
            total = total + lax.dot_general(
                one, one, (((0,), (0,)), ((), ())), preferred_element_type=jnp.float32
            )

    @pl.when(step == 0)
    def _():
        sum_copy.wait()
        out_ref[...] = sum_ref[...] + total

    @pl.when(step > 0)
    def _():
        out_ref[...] += total


def fit_exchange(factor, arrived, before):
    devices, own, aux_local, basis_total = arrived.shape
    aux_total = factor.shape[0]
    width = 2 if own % 2 == 0 else 1
    return pl.pallas_call(
        functools.partial(fit_kernel, aux_total // 8),
        out_shape=jax.ShapeDtypeStruct((basis_total, basis_total), jnp.float32),
        grid=(own // width,),
        in_specs=[
            pl.BlockSpec(memory_space=pl.ANY),
            pl.BlockSpec(memory_space=pl.ANY),
            pl.BlockSpec(memory_space=pl.ANY),
        ],
        out_specs=pl.BlockSpec((basis_total, basis_total), lambda k: (0, 0)),
        scratch_shapes=[
            pltpu.VMEM((basis_total, basis_total), jnp.float32),
            pltpu.VMEM((aux_total, aux_total), jnp.bfloat16),
            pltpu.VMEM((2, devices, aux_local, width * basis_total), jnp.bfloat16),
            pltpu.SemaphoreType.DMA,
            pltpu.SemaphoreType.DMA((8,)),
            pltpu.SemaphoreType.DMA((2, 8, width)),
        ],
        compiler_params=pltpu.CompilerParams(vmem_limit_bytes=FIT_VMEM_BYTES),
        cost_estimate=pl.CostEstimate(
            flops=own * aux_total * basis_total * (aux_total * 9 // 8 + 2 * basis_total),
            bytes_accessed=(factor.size + arrived.size) * 2,
            transcendentals=0,
        ),
        name="fit_exchange",
    )(before, factor, arrived)


def line_near(block):
    far = lax.ppermute(block, "occ", [(0, 2), (3, 1)])
    up = lax.ppermute(block, "occ", [(0, 1), (1, 2), (2, 3)])
    down = lax.ppermute(block, "occ", [(3, 2), (2, 1), (1, 0)])
    return up, down, far


def line_forward(up, down, far):
    nearer = jnp.where(lax.axis_index("occ") < 2, down, up)
    return lax.ppermute(jnp.stack([nearer, far]), "occ", [(1, 0), (2, 3)])


def line_order(block, up, down, far, later):
    order = lax.switch(
        lax.axis_index("occ"),
        [
            lambda: (block, down, later[0], later[1]),
            lambda: (up, block, down, far),
            lambda: (far, up, block, down),
            lambda: (later[1], later[0], up, block),
        ],
    )
    return jnp.concatenate(order)


def chunk_sizes(own):
    if own % 8 == 0:
        return [own // 4, 5 * own // 8, own // 8]
    return [1] * own


def per_device(integrals, pair_list, pair_count, coefficients, metric):
    devices = lax.axis_size("aux") * lax.axis_size("occ")
    basis_total = coefficients.shape[0]
    in_line = lax.axis_size("occ") == 4
    near = line_near(metric) if in_line else ()
    total = jnp.zeros((basis_total, basis_total), jnp.float32)
    state = (coefficients,)
    start = 0
    arrived = []
    factor = None
    for chunk, own in enumerate(chunk_sizes(basis_total // devices)):
        width = own * devices
        rows, state = factor_rows(start, width, basis_total, state)
        half = half_transform(integrals, pair_list, pair_count, rows, start, devices)
        if chunk == 0:
            half, state, near = lax.optimization_barrier((half, state, near))
            later = line_forward(*near) if in_line else ()
        elif chunk == 1:
            half, state, later = lax.optimization_barrier((half, state, later))
            if in_line:
                line = line_order(metric, *near, later)
                factor = lax.all_gather(line, "aux", axis=0, tiled=True)
            else:
                factor = lax.all_gather(metric, BOTH, axis=0, tiled=True)
        else:
            total = fit_exchange(factor, arrived[chunk - 2], total)
            half, state, arrived[chunk - 1], total = lax.optimization_barrier(
                (half, state, arrived[chunk - 1], total)
            )
        arrived.append(lax.all_to_all(half, BOTH, split_axis=0, concat_axis=0, tiled=True))
        start += width
    for piece in arrived[-2:]:
        total = fit_exchange(factor, piece, total)
    shares = total.reshape(devices, basis_total // devices, basis_total)
    return jnp.sum(lax.all_to_all(shares, BOTH, split_axis=0, concat_axis=0, tiled=True), axis=0)


def solution(mesh):
    in_specs = (
        P(("grp", "aux", "occ"), None, None, None, None),
        P(("grp", "aux", "occ"), None),
        P(("grp", "aux", "occ")),
        P("grp", None),
        P(("grp", "aux", "occ"), None),
    )
    out_specs = P(("grp", "aux", "occ"), None)
    return jax.shard_map(
        per_device, mesh=mesh, in_specs=in_specs, out_specs=out_specs, check_vma=False
    )
```

```python
import functools

import jax
import jax.numpy as jnp
from jax import lax
from jax.experimental import pallas as pl
from jax.experimental.pallas import tpu as pltpu
from jax.sharding import PartitionSpec as P

BOTH = ("aux", "occ")
VMEM_BYTES = 58 * 2**20
FIT_VMEM_BYTES = 63 * 2**20
PANEL = 16
SCALE = 2.0**40
PIVOT_FLOOR = 1e-6


def root(value):
    return value * lax.rsqrt(jnp.maximum(value, 1e-37))


def factor_kernel(start, *refs):
    if start == 0:
        coef_ref, rows_ref, rest_ref, diag_ref = refs
        scaled = (coef_ref[...].astype(jnp.float32) * SCALE).astype(jnp.bfloat16)
        gram = lax.dot_general(
            scaled, scaled, (((1,), (1,)), ((), ())), preferred_element_type=jnp.float32
        )
        total = gram.shape[0]
        on_diagonal = lax.broadcasted_iota(jnp.int32, gram.shape, 0) == (
            lax.broadcasted_iota(jnp.int32, gram.shape, 1)
        )
        diagonal = jnp.sum(jnp.where(on_diagonal, gram, 0.0), axis=0, keepdims=True)
        which = lax.broadcasted_iota(jnp.int32, diag_ref.shape, 0)
        diag_ref[...] = jnp.where(
            which == 0, diagonal, jnp.maximum(diagonal * PIVOT_FLOOR, 1e-37)
        )
        rest_ref[...] = gram
    else:
        rest_in_ref, diag_in_ref, rows_ref, rest_ref, diag_ref = refs
        rest_ref[...] = rest_in_ref[...]
        diag_ref[...] = diag_in_ref[...]
        total = rest_ref.shape[1]
    own = rows_ref.shape[0] // 2
    lanes = min(total, 128)
    parts = [slice(part * lanes, (part + 1) * lanes) for part in range(total // lanes)]
    row = lax.broadcasted_iota(jnp.int32, (PANEL, lanes), 0)
    lane = lax.broadcasted_iota(jnp.int32, (PANEL, lanes), 1)

    def panel(number, carry):
        low = pl.multiple_of(start + number * PANEL, PANEL)
        rest = [rest_ref[pl.ds(low, PANEL), part] for part in parts]
        left = [diag_ref[0:1, part] for part in parts]
        floor = [diag_ref[1:2, part] for part in parts]

        def as_column(values):
            picked = jnp.zeros((PANEL, lanes), jnp.float32)
            for part, value in zip(parts, values):
                picked = picked + jnp.where(lane + part.start == low + row, value, 0.0)
            return jnp.broadcast_to(jnp.sum(picked, axis=1, keepdims=True), (PANEL, lanes))

        left_column, floor_column = as_column(left), as_column(floor)
        corner = rest[0]
        for part, value in zip(parts[1:], rest[1:]):
            corner = jnp.where(low >= part.start, value, corner)
        corner = pltpu.roll(corner, lax.rem(lanes - lax.rem(low, lanes), lanes), 1)
        columns = [
            jnp.broadcast_to(corner[:, t : t + 1], (PANEL, lanes)) for t in range(PANEL)
        ]
        done = [jnp.zeros((PANEL, lanes), jnp.float32) for part in parts]
        for t in range(PANEL):
            pivot = jnp.maximum(left_column[t : t + 1], floor_column[t : t + 1])
            inverse = lax.rsqrt(pivot)
            inverse = inverse * (1.5 - 0.5 * (pivot * inverse) * inverse)
            most = root(left_column)
            weight = jnp.clip(columns[t] * inverse, -most, most)
            weight = jnp.where(row > t, weight, 0.0)
            left_column = jnp.maximum(left_column - weight * weight, 0.0)
            for s in range(t + 1, PANEL):
                columns[s] = columns[s] - weight * weight[s : s + 1]
            for i, part in enumerate(parts):
                place = lane[:1] + part.start
                most = root(left[i])
                here = jnp.clip(rest[i][t : t + 1] * inverse, -most, most)
                here = jnp.where(place > low + t, here, 0.0)
                left[i] = jnp.maximum(left[i] - here * here, 0.0)
                here = jnp.where(place == low + t, pivot * inverse, here)
                done[i] = jnp.where(row == t, here, done[i])
                rest[i] = rest[i] - weight * here
        for part, value in zip(parts, left):
            diag_ref[0:1, part] = value
        done = jnp.concatenate(done, axis=1)
        rest_ref[...] -= lax.dot_general(
            done,
            done,
            (((0,), (0,)), ((), ())),
            precision=lax.Precision.HIGHEST,
            preferred_element_type=jnp.float32,
        )
        done = done * (1.0 / SCALE)
        high = done.astype(jnp.bfloat16)
        place = pl.multiple_of(number * PANEL, PANEL)
        rows_ref[pl.ds(place, PANEL), :] = high
        rows_ref[pl.ds(own + place, PANEL), :] = (done - high.astype(jnp.float32)).astype(
            jnp.bfloat16
        )
        return carry

    lax.fori_loop(0, own // PANEL, panel, 0)


def factor_rows(start, own, total, operands):
    rows, rest, diagonals = pl.pallas_call(
        functools.partial(factor_kernel, start),
        out_shape=(
            jax.ShapeDtypeStruct((2 * own, total), jnp.bfloat16),
            jax.ShapeDtypeStruct((total, total), jnp.float32),
            jax.ShapeDtypeStruct((8, total), jnp.float32),
        ),
        compiler_params=pltpu.CompilerParams(vmem_limit_bytes=VMEM_BYTES),
        name="factor_rows",
    )(*operands)
    return rows, (rest, diagonals)


def half_kernel(low_block, list_ref, count_ref, basis_ref, *refs):
    tile_refs, (out_ref, rows_ref) = refs[:-2], refs[-2:]
    block = pl.program_id(0)
    aux_width, size_block = tile_refs[0].shape[2:4]
    vectors = basis_ref.shape[0] // 2
    side = basis_ref.shape[1] // size_block
    columns = range(low_block, side)
    for m in range(side):
        basis = []
        for n in columns:
            used = jnp.bool_(False)
            for slot in range(list_ref.shape[0]):
                hit = jnp.logical_and(
                    list_ref[slot, block] == m * side + n, slot < count_ref[block]
                )
                used = jnp.logical_or(used, hit)
            part = basis_ref[:, n * size_block : (n + 1) * size_block]
            basis.append(jnp.where(used, part, jnp.zeros_like(part)))
        tiles = [
            tile_refs[m * len(columns) + i][0, 0].reshape(aux_width * size_block, size_block)
            for i in range(len(columns))
        ]
        product = lax.dot_general(
            jnp.concatenate(basis, axis=1),
            jnp.concatenate(tiles, axis=1),
            (((1,), (1,)), ((), ())),
            preferred_element_type=jnp.float32,
        )
        product = product[:vectors] + product[vectors:]
        for p in range(aux_width):
            rows_ref[m, pl.ds(p, vectors, stride=aux_width), :] = product[
                :, p * size_block : (p + 1) * size_block
            ]
    for m in range(side):
        out_ref[..., m * size_block : (m + 1) * size_block] = (
            rows_ref[m].astype(jnp.bfloat16).reshape(out_ref.shape[:-1] + (size_block,))
        )


def half_transform(integrals, pair_list, pair_count, basis_rows, start, devices):
    blocks, slots, aux_width, size_block, _ = integrals.shape
    vectors, basis_total = basis_rows.shape[0] // 2, basis_rows.shape[1]
    own = vectors // devices
    side = basis_total // size_block
    low_block = start // size_block

    def tile_spec(pair):
        def place(b, list_ref, count_ref):
            slot_of = jnp.int32(0)
            for slot in range(1, slots):
                slot_of = jnp.where(list_ref[slot, b] == pair, slot, slot_of)
            return b, slot_of, 0, 0, 0

        return pl.BlockSpec((1, 1, aux_width, size_block, size_block), place)

    tiles = [tile_spec(m * side + n) for m in range(side) for n in range(low_block, side)]
    return pl.pallas_call(
        functools.partial(half_kernel, low_block),
        out_shape=jax.ShapeDtypeStruct(
            (devices, own, blocks * aux_width, basis_total), jnp.bfloat16
        ),
        grid_spec=pltpu.PrefetchScalarGridSpec(
            num_scalar_prefetch=2,
            grid=(blocks,),
            in_specs=[pl.BlockSpec(basis_rows.shape, lambda b, *_: (0, 0))] + tiles,
            out_specs=pl.BlockSpec(
                (devices, own, aux_width, basis_total), lambda b, *_: (0, 0, b, 0)
            ),
            scratch_shapes=[
                pltpu.VMEM(
                    (basis_total // size_block, vectors * aux_width, size_block), jnp.float32
                ),
            ],
        ),
        compiler_params=pltpu.CompilerParams(vmem_limit_bytes=VMEM_BYTES),
        cost_estimate=pl.CostEstimate(
            flops=4 * blocks * aux_width * vectors * basis_total * basis_total,
            bytes_accessed=integrals.size * 2 + vectors * blocks * aux_width * basis_total * 2,
            transcendentals=0,
        ),
        name="half_transform",
    )(pair_list.T, pair_count, basis_rows, *[integrals] * len(tiles))


def fit_kernel(
    step_rows,
    before_ref,
    factor_ref,
    half_ref,
    out_ref,
    sum_ref,
    lower_ref,
    columns_ref,
    sum_sem,
    factor_sems,
    half_sems,
):
    step = pl.program_id(0)
    aux_total = factor_ref.shape[0]
    basis_total = out_ref.shape[0]
    width = columns_ref.shape[-1] // basis_total
    blocks = aux_total // step_rows
    sources = half_ref.shape[0] // blocks
    sum_copy = pltpu.make_async_copy(before_ref, sum_ref, sum_sem)

    def factor_copy(number):
        low, high = number * step_rows, (number + 1) * step_rows
        part = (slice(low, high), slice(0, high))
        return pltpu.make_async_copy(
            factor_ref.at[part], lower_ref.at[part], factor_sems.at[number]
        )

    def half_copy(index, number, k):
        slot = lax.rem(index, 2)
        part = slice(number * sources, (number + 1) * sources)
        return pltpu.make_async_copy(
            half_ref.at[part, index * width + k],
            columns_ref.at[slot, part, :, k * basis_total : (k + 1) * basis_total],
            half_sems.at[slot, number, k],
        )

    def start_half(index):
        for number in range(blocks):
            for k in range(width):
                half_copy(index, number, k).start()

    @pl.when(step == 0)
    def _():
        for number in range(blocks):
            for k in range(width):
                half_copy(step, number, k).start()
            factor_copy(number).start()
        sum_copy.start()

    pl.when(step + 1 < pl.num_programs(0))(lambda: start_half(step + 1))

    total = jnp.zeros(out_ref.shape, jnp.float32)
    for number in range(blocks):
        low, high = number * step_rows, (number + 1) * step_rows
        for k in range(width):
            half_copy(step, number, k).wait()
        pl.when(step == 0)(lambda number=number: factor_copy(number).wait())
        fitted = None
        middle = (number + 1) // 2
        for first, last in ((0, middle), (middle, number + 1)):
            if first == last:
                continue
            columns = columns_ref[lax.rem(step, 2), first * sources : last * sources]
            product = jnp.dot(
                lower_ref[low:high, first * step_rows : last * step_rows],
                columns.reshape((last - first) * step_rows, columns.shape[-1]),
                preferred_element_type=jnp.float32,
            )
            fitted = product if fitted is None else fitted + product
        fitted = fitted.astype(jnp.bfloat16)
        for k in range(width):
            one = fitted[:, k * basis_total : (k + 1) * basis_total]
            total = total + lax.dot_general(
                one, one, (((0,), (0,)), ((), ())), preferred_element_type=jnp.float32
            )

    @pl.when(step == 0)
    def _():
        sum_copy.wait()
        out_ref[...] = sum_ref[...] + total

    @pl.when(step > 0)
    def _():
        out_ref[...] += total


def fit_exchange(factor, arrived, before):
    devices, own, aux_local, basis_total = arrived.shape
    aux_total = factor.shape[0]
    width = 2 if own % 2 == 0 else 1
    return pl.pallas_call(
        functools.partial(fit_kernel, aux_total // 8),
        out_shape=jax.ShapeDtypeStruct((basis_total, basis_total), jnp.float32),
        grid=(own // width,),
        in_specs=[
            pl.BlockSpec(memory_space=pl.ANY),
            pl.BlockSpec(memory_space=pl.ANY),
            pl.BlockSpec(memory_space=pl.ANY),
        ],
        out_specs=pl.BlockSpec((basis_total, basis_total), lambda k: (0, 0)),
        scratch_shapes=[
            pltpu.VMEM((basis_total, basis_total), jnp.float32),
            pltpu.VMEM((aux_total, aux_total), jnp.bfloat16),
            pltpu.VMEM((2, devices, aux_local, width * basis_total), jnp.bfloat16),
            pltpu.SemaphoreType.DMA,
            pltpu.SemaphoreType.DMA((8,)),
            pltpu.SemaphoreType.DMA((2, 8, width)),
        ],
        compiler_params=pltpu.CompilerParams(vmem_limit_bytes=FIT_VMEM_BYTES),
        cost_estimate=pl.CostEstimate(
            flops=own * aux_total * basis_total * (aux_total * 9 // 8 + 2 * basis_total),
            bytes_accessed=(factor.size + arrived.size) * 2,
            transcendentals=0,
        ),
        name="fit_exchange",
    )(before, factor, arrived)


def line_near(block):
    up = lax.ppermute(block, "occ", [(0, 1), (1, 2), (2, 3)])
    down = lax.ppermute(block, "occ", [(3, 2), (2, 1), (1, 0)])
    return up, down


def line_far(block):
    return lax.ppermute(block, "occ", [(0, 2), (3, 1)])


def line_forward(up, down, far):
    nearer = jnp.where(lax.axis_index("occ") < 2, down, up)
    return lax.ppermute(jnp.stack([nearer, far]), "occ", [(1, 0), (2, 3)])


def line_order(block, up, down, far, later):
    order = lax.switch(
        lax.axis_index("occ"),
        [
            lambda: (block, down, later[0], later[1]),
            lambda: (up, block, down, far),
            lambda: (far, up, block, down),
            lambda: (later[1], later[0], up, block),
        ],
    )
    return jnp.concatenate(order)


def chunk_sizes(own):
    if own % 8 == 0:
        return [own // 4, 5 * own // 8, own // 8]
    return [1] * own


def per_device(integrals, pair_list, pair_count, coefficients, metric):
    devices = lax.axis_size("aux") * lax.axis_size("occ")
    basis_total = coefficients.shape[0]
    in_line = lax.axis_size("occ") == 4
    near = line_near(metric) if in_line else ()
    total = jnp.zeros((basis_total, basis_total), jnp.float32)
    state = (coefficients,)
    start = 0
    arrived = []
    factor = None
    for chunk, own in enumerate(chunk_sizes(basis_total // devices)):
        width = own * devices
        rows, state = factor_rows(start, width, basis_total, state)
        if chunk == 0 and in_line:
            rows, block = lax.optimization_barrier((rows, metric))
            near += (line_far(block),)
        half = half_transform(integrals, pair_list, pair_count, rows, start, devices)
        if chunk == 0:
            half, state, near = lax.optimization_barrier((half, state, near))
            later = line_forward(*near) if in_line else ()
        elif chunk == 1:
            half, state, later = lax.optimization_barrier((half, state, later))
            if in_line:
                line = line_order(metric, *near, later)
                factor = lax.all_gather(line, "aux", axis=0, tiled=True)
            else:
                factor = lax.all_gather(metric, BOTH, axis=0, tiled=True)
        else:
            total = fit_exchange(factor, arrived[chunk - 2], total)
            half, state, arrived[chunk - 1], total = lax.optimization_barrier(
                (half, state, arrived[chunk - 1], total)
            )
        arrived.append(lax.all_to_all(half, BOTH, split_axis=0, concat_axis=0, tiled=True))
        start += width
    for piece in arrived[-2:]:
        total = fit_exchange(factor, piece, total)
    shares = total.reshape(devices, basis_total // devices, basis_total)
    return jnp.sum(lax.all_to_all(shares, BOTH, split_axis=0, concat_axis=0, tiled=True), axis=0)


def solution(mesh):
    in_specs = (
        P(("grp", "aux", "occ"), None, None, None, None),
        P(("grp", "aux", "occ"), None),
        P(("grp", "aux", "occ")),
        P("grp", None),
        P(("grp", "aux", "occ"), None),
    )
    out_specs = P(("grp", "aux", "occ"), None)
    return jax.shard_map(
        per_device, mesh=mesh, in_specs=in_specs, out_specs=out_specs, check_vma=False
    )
```

```python
import functools

import jax
import jax.numpy as jnp
from jax import lax
from jax.experimental import pallas as pl
from jax.experimental.pallas import tpu as pltpu
from jax.sharding import PartitionSpec as P

BOTH = ("aux", "occ")
VMEM_BYTES = 58 * 2**20
FIT_VMEM_BYTES = 63 * 2**20
PANEL = 16
SCALE = 2.0**40
PIVOT_FLOOR = 1e-6


def root(value):
    return value * lax.rsqrt(jnp.maximum(value, 1e-37))


def factor_kernel(start, *refs):
    if start == 0:
        coef_ref, rows_ref, rest_ref, diag_ref = refs
        scaled = (coef_ref[...].astype(jnp.float32) * SCALE).astype(jnp.bfloat16)
        gram = lax.dot_general(
            scaled, scaled, (((1,), (1,)), ((), ())), preferred_element_type=jnp.float32
        )
        total = gram.shape[0]
        on_diagonal = lax.broadcasted_iota(jnp.int32, gram.shape, 0) == (
            lax.broadcasted_iota(jnp.int32, gram.shape, 1)
        )
        diagonal = jnp.sum(jnp.where(on_diagonal, gram, 0.0), axis=0, keepdims=True)
        which = lax.broadcasted_iota(jnp.int32, diag_ref.shape, 0)
        diag_ref[...] = jnp.where(
            which == 0, diagonal, jnp.maximum(diagonal * PIVOT_FLOOR, 1e-37)
        )
        rest_ref[...] = gram
    else:
        rest_in_ref, diag_in_ref, rows_ref, rest_ref, diag_ref = refs
        rest_ref[...] = rest_in_ref[...]
        diag_ref[...] = diag_in_ref[...]
        total = rest_ref.shape[1]
    own = rows_ref.shape[0] // 2
    lanes = min(total, 128)
    parts = [slice(part * lanes, (part + 1) * lanes) for part in range(total // lanes)]
    row = lax.broadcasted_iota(jnp.int32, (PANEL, lanes), 0)
    lane = lax.broadcasted_iota(jnp.int32, (PANEL, lanes), 1)

    def panel(number, carry):
        low = pl.multiple_of(start + number * PANEL, PANEL)
        rest = [rest_ref[pl.ds(low, PANEL), part] for part in parts]
        left = [diag_ref[0:1, part] for part in parts]
        floor = [diag_ref[1:2, part] for part in parts]

        def as_column(values):
            picked = jnp.zeros((PANEL, lanes), jnp.float32)
            for part, value in zip(parts, values):
                picked = picked + jnp.where(lane + part.start == low + row, value, 0.0)
            return jnp.broadcast_to(jnp.sum(picked, axis=1, keepdims=True), (PANEL, lanes))

        left_column, floor_column = as_column(left), as_column(floor)
        corner = rest[0]
        for part, value in zip(parts[1:], rest[1:]):
            corner = jnp.where(low >= part.start, value, corner)
        corner = pltpu.roll(corner, lax.rem(lanes - lax.rem(low, lanes), lanes), 1)
        columns = [
            jnp.broadcast_to(corner[:, t : t + 1], (PANEL, lanes)) for t in range(PANEL)
        ]
        done = [jnp.zeros((PANEL, lanes), jnp.float32) for part in parts]
        for t in range(PANEL):
            pivot = jnp.maximum(left_column[t : t + 1], floor_column[t : t + 1])
            inverse = lax.rsqrt(pivot)
            inverse = inverse * (1.5 - 0.5 * (pivot * inverse) * inverse)
            most = root(left_column)
            weight = jnp.clip(columns[t] * inverse, -most, most)
            weight = jnp.where(row > t, weight, 0.0)
            left_column = jnp.maximum(left_column - weight * weight, 0.0)
            for s in range(t + 1, PANEL):
                columns[s] = columns[s] - weight * weight[s : s + 1]
            for i, part in enumerate(parts):
                place = lane[:1] + part.start
                most = root(left[i])
                here = jnp.clip(rest[i][t : t + 1] * inverse, -most, most)
                here = jnp.where(place > low + t, here, 0.0)
                left[i] = jnp.maximum(left[i] - here * here, 0.0)
                here = jnp.where(place == low + t, pivot * inverse, here)
                done[i] = jnp.where(row == t, here, done[i])
                rest[i] = rest[i] - weight * here
        for part, value in zip(parts, left):
            diag_ref[0:1, part] = value
        done = jnp.concatenate(done, axis=1)
        rest_ref[...] -= lax.dot_general(
            done,
            done,
            (((0,), (0,)), ((), ())),
            precision=lax.Precision.HIGHEST,
            preferred_element_type=jnp.float32,
        )
        done = done * (1.0 / SCALE)
        high = done.astype(jnp.bfloat16)
        place = pl.multiple_of(number * PANEL, PANEL)
        rows_ref[pl.ds(place, PANEL), :] = high
        rows_ref[pl.ds(own + place, PANEL), :] = (done - high.astype(jnp.float32)).astype(
            jnp.bfloat16
        )
        return carry

    lax.fori_loop(0, own // PANEL, panel, 0)


def factor_rows(start, own, total, operands):
    rows, rest, diagonals = pl.pallas_call(
        functools.partial(factor_kernel, start),
        out_shape=(
            jax.ShapeDtypeStruct((2 * own, total), jnp.bfloat16),
            jax.ShapeDtypeStruct((total, total), jnp.float32),
            jax.ShapeDtypeStruct((8, total), jnp.float32),
        ),
        compiler_params=pltpu.CompilerParams(vmem_limit_bytes=VMEM_BYTES),
        name="factor_rows",
    )(*operands)
    return rows, (rest, diagonals)


def half_kernel(low_block, together, list_ref, count_ref, basis_ref, *refs):
    tile_refs, (out_ref, rows_ref) = refs[:-2], refs[-2:]
    aux_width, size_block = tile_refs[0].shape[2:4]
    vectors = basis_ref.shape[0] // 2
    side = basis_ref.shape[1] // size_block
    columns = range(low_block, side)
    for here in range(together):
        block = pl.program_id(0) * together + here
        for m in range(side):
            basis = []
            for n in columns:
                used = jnp.bool_(False)
                for slot in range(list_ref.shape[0]):
                    hit = jnp.logical_and(
                        list_ref[slot, block] == m * side + n, slot < count_ref[block]
                    )
                    used = jnp.logical_or(used, hit)
                part = basis_ref[:, n * size_block : (n + 1) * size_block]
                basis.append(jnp.where(used, part, jnp.zeros_like(part)))
            low = (here * side + m) * len(columns)
            tiles = [
                tile_ref[0, 0].reshape(aux_width * size_block, size_block)
                for tile_ref in tile_refs[low : low + len(columns)]
            ]
            product = lax.dot_general(
                jnp.concatenate(basis, axis=1),
                jnp.concatenate(tiles, axis=1),
                (((1,), (1,)), ((), ())),
                preferred_element_type=jnp.float32,
            )
            product = product[:vectors] + product[vectors:]
            for p in range(aux_width):
                rows_ref[
                    m, pl.ds(here * aux_width + p, vectors, stride=together * aux_width), :
                ] = product[:, p * size_block : (p + 1) * size_block]
    for m in range(side):
        out_ref[..., m * size_block : (m + 1) * size_block] = (
            rows_ref[m].astype(jnp.bfloat16).reshape(out_ref.shape[:-1] + (size_block,))
        )


def half_transform(integrals, pair_list, pair_count, basis_rows, start, devices):
    blocks, slots, aux_width, size_block, _ = integrals.shape
    vectors, basis_total = basis_rows.shape[0] // 2, basis_rows.shape[1]
    own = vectors // devices
    side = basis_total // size_block
    low_block = start // size_block

    together = 2 if blocks % 2 == 0 else 1

    def tile_spec(here, pair):
        def place(step, list_ref, count_ref):
            b = step * together + here
            slot_of = jnp.int32(0)
            for slot in range(1, slots):
                slot_of = jnp.where(list_ref[slot, b] == pair, slot, slot_of)
            return b, slot_of, 0, 0, 0

        return pl.BlockSpec((1, 1, aux_width, size_block, size_block), place)

    tiles = [
        tile_spec(here, m * side + n)
        for here in range(together)
        for m in range(side)
        for n in range(low_block, side)
    ]
    return pl.pallas_call(
        functools.partial(half_kernel, low_block, together),
        out_shape=jax.ShapeDtypeStruct(
            (devices, own, blocks * aux_width, basis_total), jnp.bfloat16
        ),
        grid_spec=pltpu.PrefetchScalarGridSpec(
            num_scalar_prefetch=2,
            grid=(blocks // together,),
            in_specs=[pl.BlockSpec(basis_rows.shape, lambda b, *_: (0, 0))] + tiles,
            out_specs=pl.BlockSpec(
                (devices, own, together * aux_width, basis_total), lambda b, *_: (0, 0, b, 0)
            ),
            scratch_shapes=[
                pltpu.VMEM(
                    (basis_total // size_block, vectors * together * aux_width, size_block),
                    jnp.float32,
                ),
            ],
        ),
        compiler_params=pltpu.CompilerParams(vmem_limit_bytes=VMEM_BYTES),
        cost_estimate=pl.CostEstimate(
            flops=4 * blocks * aux_width * vectors * basis_total * basis_total,
            bytes_accessed=integrals.size * 2 + vectors * blocks * aux_width * basis_total * 2,
            transcendentals=0,
        ),
        name="half_transform",
    )(pair_list.T, pair_count, basis_rows, *[integrals] * len(tiles))


def fit_kernel(
    step_rows,
    before_ref,
    factor_ref,
    half_ref,
    out_ref,
    sum_ref,
    lower_ref,
    columns_ref,
    sum_sem,
    factor_sems,
    half_sems,
):
    step = pl.program_id(0)
    aux_total = factor_ref.shape[0]
    basis_total = out_ref.shape[0]
    width = columns_ref.shape[-1] // basis_total
    blocks = aux_total // step_rows
    sources = half_ref.shape[0] // blocks
    sum_copy = pltpu.make_async_copy(before_ref, sum_ref, sum_sem)

    def factor_copy(number):
        low, high = number * step_rows, (number + 1) * step_rows
        part = (slice(low, high), slice(0, high))
        return pltpu.make_async_copy(
            factor_ref.at[part], lower_ref.at[part], factor_sems.at[number]
        )

    def half_copy(index, number, k):
        slot = lax.rem(index, 2)
        part = slice(number * sources, (number + 1) * sources)
        return pltpu.make_async_copy(
            half_ref.at[part, index * width + k],
            columns_ref.at[slot, part, :, k * basis_total : (k + 1) * basis_total],
            half_sems.at[slot, number, k],
        )

    def start_half(index):
        for number in range(blocks):
            for k in range(width):
                half_copy(index, number, k).start()

    @pl.when(step == 0)
    def _():
        for number in range(blocks):
            for k in range(width):
                half_copy(step, number, k).start()
            factor_copy(number).start()
        sum_copy.start()

    pl.when(step + 1 < pl.num_programs(0))(lambda: start_half(step + 1))

    total = jnp.zeros(out_ref.shape, jnp.float32)
    for number in range(blocks):
        low, high = number * step_rows, (number + 1) * step_rows
        for k in range(width):
            half_copy(step, number, k).wait()
        pl.when(step == 0)(lambda number=number: factor_copy(number).wait())
        columns = columns_ref[lax.rem(step, 2), : (number + 1) * sources]
        fitted = jnp.dot(
            lower_ref[low:high, :high],
            columns.reshape(high, columns.shape[-1]),
            preferred_element_type=jnp.float32,
        ).astype(jnp.bfloat16)
        for k in range(width):
            one = fitted[:, k * basis_total : (k + 1) * basis_total]
            total = total + lax.dot_general(
                one, one, (((0,), (0,)), ((), ())), preferred_element_type=jnp.float32
            )

    @pl.when(step == 0)
    def _():
        sum_copy.wait()
        out_ref[...] = sum_ref[...] + total

    @pl.when(step > 0)
    def _():
        out_ref[...] += total


def fit_exchange(factor, arrived, before):
    devices, own, aux_local, basis_total = arrived.shape
    aux_total = factor.shape[0]
    width = 2 if own % 2 == 0 else 1
    return pl.pallas_call(
        functools.partial(fit_kernel, aux_total // 8),
        out_shape=jax.ShapeDtypeStruct((basis_total, basis_total), jnp.float32),
        grid=(own // width,),
        in_specs=[
            pl.BlockSpec(memory_space=pl.ANY),
            pl.BlockSpec(memory_space=pl.ANY),
            pl.BlockSpec(memory_space=pl.ANY),
        ],
        out_specs=pl.BlockSpec((basis_total, basis_total), lambda k: (0, 0)),
        scratch_shapes=[
            pltpu.VMEM((basis_total, basis_total), jnp.float32),
            pltpu.VMEM((aux_total, aux_total), jnp.bfloat16),
            pltpu.VMEM((2, devices, aux_local, width * basis_total), jnp.bfloat16),
            pltpu.SemaphoreType.DMA,
            pltpu.SemaphoreType.DMA((8,)),
            pltpu.SemaphoreType.DMA((2, 8, width)),
        ],
        compiler_params=pltpu.CompilerParams(vmem_limit_bytes=FIT_VMEM_BYTES),
        cost_estimate=pl.CostEstimate(
            flops=own * aux_total * basis_total * (aux_total * 9 // 8 + 2 * basis_total),
            bytes_accessed=(factor.size + arrived.size) * 2,
            transcendentals=0,
        ),
        name="fit_exchange",
    )(before, factor, arrived)


def line_near(block):
    far = lax.ppermute(block, "occ", [(0, 2), (3, 1)])
    up = lax.ppermute(block, "occ", [(0, 1), (1, 2), (2, 3)])
    down = lax.ppermute(block, "occ", [(3, 2), (2, 1), (1, 0)])
    return up, down, far


def line_forward(up, down, far):
    nearer = jnp.where(lax.axis_index("occ") < 2, down, up)
    return lax.ppermute(jnp.stack([nearer, far]), "occ", [(1, 0), (2, 3)])


def line_order(block, up, down, far, later):
    order = lax.switch(
        lax.axis_index("occ"),
        [
            lambda: (block, down, later[0], later[1]),
            lambda: (up, block, down, far),
            lambda: (far, up, block, down),
            lambda: (later[1], later[0], up, block),
        ],
    )
    return jnp.concatenate(order)


def chunk_sizes(own):
    if own % 8 == 0:
        return [own // 4, 5 * own // 8, own // 8]
    return [1] * own


def per_device(integrals, pair_list, pair_count, coefficients, metric):
    devices = lax.axis_size("aux") * lax.axis_size("occ")
    basis_total = coefficients.shape[0]
    in_line = lax.axis_size("occ") == 4
    near = line_near(metric) if in_line else ()
    total = jnp.zeros((basis_total, basis_total), jnp.float32)
    state = (coefficients,)
    start = 0
    arrived = []
    factor = None
    for chunk, own in enumerate(chunk_sizes(basis_total // devices)):
        width = own * devices
        rows, state = factor_rows(start, width, basis_total, state)
        half = half_transform(integrals, pair_list, pair_count, rows, start, devices)
        if chunk == 0:
            half, state, near = lax.optimization_barrier((half, state, near))
            later = line_forward(*near) if in_line else ()
        elif chunk == 1:
            half, state, later = lax.optimization_barrier((half, state, later))
            if in_line:
                line = line_order(metric, *near, later)
                factor = lax.all_gather(line, "aux", axis=0, tiled=True)
            else:
                factor = lax.all_gather(metric, BOTH, axis=0, tiled=True)
        else:
            total = fit_exchange(factor, arrived[chunk - 2], total)
            half, state, arrived[chunk - 1], total = lax.optimization_barrier(
                (half, state, arrived[chunk - 1], total)
            )
        arrived.append(lax.all_to_all(half, BOTH, split_axis=0, concat_axis=0, tiled=True))
        start += width
    for piece in arrived[-2:]:
        total = fit_exchange(factor, piece, total)
    shares = total.reshape(devices, basis_total // devices, basis_total)
    return jnp.sum(lax.all_to_all(shares, BOTH, split_axis=0, concat_axis=0, tiled=True), axis=0)


def solution(mesh):
    in_specs = (
        P(("grp", "aux", "occ"), None, None, None, None),
        P(("grp", "aux", "occ"), None),
        P(("grp", "aux", "occ")),
        P("grp", None),
        P(("grp", "aux", "occ"), None),
    )
    out_specs = P(("grp", "aux", "occ"), None)
    return jax.shard_map(
        per_device, mesh=mesh, in_specs=in_specs, out_specs=out_specs, check_vma=False
    )
```

```python
import functools

import jax
import jax.numpy as jnp
from jax import lax
from jax.experimental import pallas as pl
from jax.experimental.pallas import tpu as pltpu
from jax.sharding import PartitionSpec as P

BOTH = ("aux", "occ")
VMEM_BYTES = 58 * 2**20
FIT_VMEM_BYTES = 63 * 2**20
PANEL = 16
SCALE = 2.0**40
PIVOT_FLOOR = 1e-6


def root(value):
    return value * lax.rsqrt(jnp.maximum(value, 1e-37))


def factor_kernel(start, *refs):
    if start == 0:
        coef_ref, rows_ref, rest_ref, diag_ref = refs
        scaled = (coef_ref[...].astype(jnp.float32) * SCALE).astype(jnp.bfloat16)
        gram = lax.dot_general(
            scaled, scaled, (((1,), (1,)), ((), ())), preferred_element_type=jnp.float32
        )
        total = gram.shape[0]
        on_diagonal = lax.broadcasted_iota(jnp.int32, gram.shape, 0) == (
            lax.broadcasted_iota(jnp.int32, gram.shape, 1)
        )
        diagonal = jnp.sum(jnp.where(on_diagonal, gram, 0.0), axis=0, keepdims=True)
        which = lax.broadcasted_iota(jnp.int32, diag_ref.shape, 0)
        diag_ref[...] = jnp.where(
            which == 0, diagonal, jnp.maximum(diagonal * PIVOT_FLOOR, 1e-37)
        )
        rest_ref[...] = gram
    else:
        rest_in_ref, diag_in_ref, rows_ref, rest_ref, diag_ref = refs
        rest_ref[...] = rest_in_ref[...]
        diag_ref[...] = diag_in_ref[...]
        total = rest_ref.shape[1]
    own = rows_ref.shape[0] // 2
    lanes = min(total, 128)
    parts = [slice(part * lanes, (part + 1) * lanes) for part in range(total // lanes)]
    row = lax.broadcasted_iota(jnp.int32, (PANEL, lanes), 0)
    lane = lax.broadcasted_iota(jnp.int32, (PANEL, lanes), 1)

    def panel(number, carry):
        low = pl.multiple_of(start + number * PANEL, PANEL)
        rest = [rest_ref[pl.ds(low, PANEL), part] for part in parts]
        left = [diag_ref[0:1, part] for part in parts]
        floor = [diag_ref[1:2, part] for part in parts]

        def as_column(values):
            picked = jnp.zeros((PANEL, lanes), jnp.float32)
            for part, value in zip(parts, values):
                picked = picked + jnp.where(lane + part.start == low + row, value, 0.0)
            return jnp.broadcast_to(jnp.sum(picked, axis=1, keepdims=True), (PANEL, lanes))

        left_column, floor_column = as_column(left), as_column(floor)
        corner = rest[0]
        for part, value in zip(parts[1:], rest[1:]):
            corner = jnp.where(low >= part.start, value, corner)
        corner = pltpu.roll(corner, lax.rem(lanes - lax.rem(low, lanes), lanes), 1)
        columns = [
            jnp.broadcast_to(corner[:, t : t + 1], (PANEL, lanes)) for t in range(PANEL)
        ]
        done = [jnp.zeros((PANEL, lanes), jnp.float32) for part in parts]
        for t in range(PANEL):
            pivot = jnp.maximum(left_column[t : t + 1], floor_column[t : t + 1])
            inverse = lax.rsqrt(pivot)
            inverse = inverse * (1.5 - 0.5 * (pivot * inverse) * inverse)
            most = root(left_column)
            weight = jnp.clip(columns[t] * inverse, -most, most)
            weight = jnp.where(row > t, weight, 0.0)
            left_column = jnp.maximum(left_column - weight * weight, 0.0)
            for s in range(t + 1, PANEL):
                columns[s] = columns[s] - weight * weight[s : s + 1]
            for i, part in enumerate(parts):
                place = lane[:1] + part.start
                most = root(left[i])
                here = jnp.clip(rest[i][t : t + 1] * inverse, -most, most)
                here = jnp.where(place > low + t, here, 0.0)
                left[i] = jnp.maximum(left[i] - here * here, 0.0)
                here = jnp.where(place == low + t, pivot * inverse, here)
                done[i] = jnp.where(row == t, here, done[i])
                rest[i] = rest[i] - weight * here
        for part, value in zip(parts, left):
            diag_ref[0:1, part] = value
        done = jnp.concatenate(done, axis=1)
        rest_ref[...] -= lax.dot_general(
            done,
            done,
            (((0,), (0,)), ((), ())),
            precision=lax.Precision.HIGHEST,
            preferred_element_type=jnp.float32,
        )
        done = done * (1.0 / SCALE)
        high = done.astype(jnp.bfloat16)
        place = pl.multiple_of(number * PANEL, PANEL)
        rows_ref[pl.ds(place, PANEL), :] = high
        rows_ref[pl.ds(own + place, PANEL), :] = (done - high.astype(jnp.float32)).astype(
            jnp.bfloat16
        )
        return carry

    lax.fori_loop(0, own // PANEL, panel, 0)


def factor_rows(start, own, total, operands):
    rows, rest, diagonals = pl.pallas_call(
        functools.partial(factor_kernel, start),
        out_shape=(
            jax.ShapeDtypeStruct((2 * own, total), jnp.bfloat16),
            jax.ShapeDtypeStruct((total, total), jnp.float32),
            jax.ShapeDtypeStruct((8, total), jnp.float32),
        ),
        compiler_params=pltpu.CompilerParams(vmem_limit_bytes=VMEM_BYTES),
        name="factor_rows",
    )(*operands)
    return rows, (rest, diagonals)


def half_kernel(low_block, list_ref, count_ref, basis_ref, *refs):
    tile_refs, (out_ref, rows_ref) = refs[:-2], refs[-2:]
    block = pl.program_id(0)
    aux_width, size_block = tile_refs[0].shape[2:4]
    vectors = basis_ref.shape[0] // 2
    side = basis_ref.shape[1] // size_block
    columns = range(low_block, side)
    for m in range(side):
        basis = []
        for n in columns:
            used = jnp.bool_(False)
            for slot in range(list_ref.shape[0]):
                hit = jnp.logical_and(
                    list_ref[slot, block] == m * side + n, slot < count_ref[block]
                )
                used = jnp.logical_or(used, hit)
            part = basis_ref[:, n * size_block : (n + 1) * size_block]
            basis.append(jnp.where(used, part, jnp.zeros_like(part)))
        tiles = [
            tile_refs[m * len(columns) + i][0, 0].reshape(aux_width * size_block, size_block)
            for i in range(len(columns))
        ]
        product = lax.dot_general(
            jnp.concatenate(basis, axis=1),
            jnp.concatenate(tiles, axis=1),
            (((1,), (1,)), ((), ())),
            preferred_element_type=jnp.float32,
        )
        product = product[:vectors] + product[vectors:]
        for p in range(aux_width):
            rows_ref[m, pl.ds(p, vectors, stride=aux_width), :] = product[
                :, p * size_block : (p + 1) * size_block
            ]
    for m in range(side):
        out_ref[..., m * size_block : (m + 1) * size_block] = (
            rows_ref[m].astype(jnp.bfloat16).reshape(out_ref.shape[:-1] + (size_block,))
        )


def half_transform(integrals, pair_list, pair_count, basis_rows, start, devices):
    blocks, slots, aux_width, size_block, _ = integrals.shape
    vectors, basis_total = basis_rows.shape[0] // 2, basis_rows.shape[1]
    own = vectors // devices
    side = basis_total // size_block
    low_block = start // size_block

    def tile_spec(pair):
        def place(b, list_ref, count_ref):
            slot_of = jnp.int32(0)
            for slot in range(1, slots):
                slot_of = jnp.where(list_ref[slot, b] == pair, slot, slot_of)
            return b, slot_of, 0, 0, 0

        return pl.BlockSpec((1, 1, aux_width, size_block, size_block), place)

    tiles = [tile_spec(m * side + n) for m in range(side) for n in range(low_block, side)]
    return pl.pallas_call(
        functools.partial(half_kernel, low_block),
        out_shape=jax.ShapeDtypeStruct(
            (devices, own, blocks * aux_width, basis_total), jnp.bfloat16
        ),
        grid_spec=pltpu.PrefetchScalarGridSpec(
            num_scalar_prefetch=2,
            grid=(blocks,),
            in_specs=[pl.BlockSpec(basis_rows.shape, lambda b, *_: (0, 0))] + tiles,
            out_specs=pl.BlockSpec(
                (devices, own, aux_width, basis_total), lambda b, *_: (0, 0, b, 0)
            ),
            scratch_shapes=[
                pltpu.VMEM(
                    (basis_total // size_block, vectors * aux_width, size_block), jnp.float32
                ),
            ],
        ),
        compiler_params=pltpu.CompilerParams(vmem_limit_bytes=VMEM_BYTES),
        cost_estimate=pl.CostEstimate(
            flops=4 * blocks * aux_width * vectors * basis_total * basis_total,
            bytes_accessed=integrals.size * 2 + vectors * blocks * aux_width * basis_total * 2,
            transcendentals=0,
        ),
        name="half_transform",
    )(pair_list.T, pair_count, basis_rows, *[integrals] * len(tiles))


def fit_kernel(
    step_rows,
    before_ref,
    factor_ref,
    half_ref,
    out_ref,
    sum_ref,
    lower_ref,
    columns_ref,
    sum_sem,
    factor_sems,
    half_sems,
):
    step = pl.program_id(0)
    aux_total = factor_ref.shape[0]
    basis_total = out_ref.shape[0]
    width = columns_ref.shape[-1] // basis_total
    blocks = aux_total // step_rows
    sources = half_ref.shape[0] // blocks
    sum_copy = pltpu.make_async_copy(before_ref, sum_ref, sum_sem)

    def factor_copy(number):
        low, high = number * step_rows, (number + 1) * step_rows
        part = (slice(low, high), slice(0, high))
        return pltpu.make_async_copy(
            factor_ref.at[part], lower_ref.at[part], factor_sems.at[number]
        )

    def half_copy(index, number, k):
        slot = lax.rem(index, 2)
        part = slice(number * sources, (number + 1) * sources)
        return pltpu.make_async_copy(
            half_ref.at[part, index * width + k],
            columns_ref.at[slot, part, :, k * basis_total : (k + 1) * basis_total],
            half_sems.at[slot, number, k],
        )

    def start_half(index):
        for number in range(blocks):
            for k in range(width):
                half_copy(index, number, k).start()

    @pl.when(step == 0)
    def _():
        for number in range(blocks):
            for k in range(width):
                half_copy(step, number, k).start()
            factor_copy(number).start()
        sum_copy.start()

    pl.when(step + 1 < pl.num_programs(0))(lambda: start_half(step + 1))

    total = jnp.zeros(out_ref.shape, jnp.float32)
    for number in range(blocks):
        low, high = number * step_rows, (number + 1) * step_rows
        for k in range(width):
            half_copy(step, number, k).wait()
        pl.when(step == 0)(lambda number=number: factor_copy(number).wait())
        columns = columns_ref[lax.rem(step, 2), : (number + 1) * sources]
        fitted = jnp.dot(
            lower_ref[low:high, :high],
            columns.reshape(high, columns.shape[-1]),
            preferred_element_type=jnp.float32,
        ).astype(jnp.bfloat16)
        for k in range(width):
            one = fitted[:, k * basis_total : (k + 1) * basis_total]
            total = total + lax.dot_general(
                one, one, (((0,), (0,)), ((), ())), preferred_element_type=jnp.float32
            )

    @pl.when(step == 0)
    def _():
        sum_copy.wait()
        out_ref[...] = sum_ref[...] + total

    @pl.when(step > 0)
    def _():
        out_ref[...] += total


def fit_exchange(factor, arrived, before):
    devices, own, aux_local, basis_total = arrived.shape
    aux_total = factor.shape[0]
    width = 2 if own % 2 == 0 else 1
    return pl.pallas_call(
        functools.partial(fit_kernel, aux_total // 8),
        out_shape=jax.ShapeDtypeStruct((basis_total, basis_total), jnp.float32),
        grid=(own // width,),
        in_specs=[
            pl.BlockSpec(memory_space=pl.ANY),
            pl.BlockSpec(memory_space=pl.ANY),
            pl.BlockSpec(memory_space=pl.ANY),
        ],
        out_specs=pl.BlockSpec((basis_total, basis_total), lambda k: (0, 0)),
        scratch_shapes=[
            pltpu.VMEM((basis_total, basis_total), jnp.float32),
            pltpu.VMEM((aux_total, aux_total), jnp.bfloat16),
            pltpu.VMEM((2, devices, aux_local, width * basis_total), jnp.bfloat16),
            pltpu.SemaphoreType.DMA,
            pltpu.SemaphoreType.DMA((8,)),
            pltpu.SemaphoreType.DMA((2, 8, width)),
        ],
        compiler_params=pltpu.CompilerParams(vmem_limit_bytes=FIT_VMEM_BYTES),
        cost_estimate=pl.CostEstimate(
            flops=own * aux_total * basis_total * (aux_total * 9 // 8 + 2 * basis_total),
            bytes_accessed=(factor.size + arrived.size) * 2,
            transcendentals=0,
        ),
        name="fit_exchange",
    )(before, factor, arrived)


def line_near(block):
    far = lax.ppermute(block, "occ", [(0, 2), (3, 1)])
    up = lax.ppermute(block, "occ", [(0, 1), (1, 2), (2, 3)])
    down = lax.ppermute(block, "occ", [(3, 2), (2, 1), (1, 0)])
    return up, down, far


def line_forward(up, down, far):
    nearer = jnp.where(lax.axis_index("occ") < 2, down, up)
    return lax.ppermute(jnp.stack([nearer, far]), "occ", [(1, 0), (2, 3)])


def line_order(block, up, down, far, later):
    order = lax.switch(
        lax.axis_index("occ"),
        [
            lambda: (block, down, later[0], later[1]),
            lambda: (up, block, down, far),
            lambda: (far, up, block, down),
            lambda: (later[1], later[0], up, block),
        ],
    )
    return jnp.concatenate(order)


def chunk_sizes(own):
    if own % 8 == 0:
        return [own // 4, 5 * own // 8, own // 8]
    return [1] * own


def per_device(integrals, pair_list, pair_count, coefficients, metric):
    devices = lax.axis_size("aux") * lax.axis_size("occ")
    basis_total = coefficients.shape[0]
    in_line = lax.axis_size("occ") == 4
    near = line_near(metric) if in_line else ()
    total = jnp.zeros((basis_total, basis_total), jnp.float32)
    state = (coefficients,)
    start = 0
    arrived = []
    factor = None
    for chunk, own in enumerate(chunk_sizes(basis_total // devices)):
        width = own * devices
        rows, state = factor_rows(start, width, basis_total, state)
        half = half_transform(integrals, pair_list, pair_count, rows, start, devices)
        if chunk == 0:
            half, state, near = lax.optimization_barrier((half, state, near))
            later = line_forward(*near) if in_line else ()
        elif chunk == 1:
            half, state, later = lax.optimization_barrier((half, state, later))
            if in_line:
                line = line_order(metric, *near, later)
                factor = lax.all_gather(line, "aux", axis=0, tiled=True)
            else:
                factor = lax.all_gather(metric, BOTH, axis=0, tiled=True)
        else:
            total = fit_exchange(factor, arrived[chunk - 2], total)
            half, state, arrived[chunk - 1], total = lax.optimization_barrier(
                (half, state, arrived[chunk - 1], total)
            )
        arrived.append(lax.all_to_all(half, BOTH, split_axis=0, concat_axis=0, tiled=True))
        start += width
    for piece in arrived[-2:]:
        total = fit_exchange(factor, piece, total)
    for axis in BOTH:
        count = lax.axis_size(axis)
        shares = total.reshape(count, total.shape[0] // count, basis_total)
        total = jnp.sum(lax.all_to_all(shares, axis, split_axis=0, concat_axis=0, tiled=True), axis=0)
    return total


def solution(mesh):
    in_specs = (
        P(("grp", "aux", "occ"), None, None, None, None),
        P(("grp", "aux", "occ"), None),
        P(("grp", "aux", "occ")),
        P("grp", None),
        P(("grp", "aux", "occ"), None),
    )
    out_specs = P(("grp", "aux", "occ"), None)
    return jax.shard_map(
        per_device, mesh=mesh, in_specs=in_specs, out_specs=out_specs, check_vma=False
    )
```

```python
import functools

import jax
import jax.numpy as jnp
from jax import lax
from jax.experimental import pallas as pl
from jax.experimental.pallas import tpu as pltpu
from jax.sharding import PartitionSpec as P

BOTH = ("aux", "occ")
VMEM_BYTES = 58 * 2**20
FIT_VMEM_BYTES = 63 * 2**20
PANEL = 16
SCALE = 2.0**40
PIVOT_FLOOR = 1e-6


def root(value):
    return value * lax.rsqrt(jnp.maximum(value, 1e-37))


def factor_kernel(start, *refs):
    if start == 0:
        coef_ref, rows_ref, rest_ref, diag_ref = refs
        scaled = (coef_ref[...].astype(jnp.float32) * SCALE).astype(jnp.bfloat16)
        gram = lax.dot_general(
            scaled, scaled, (((1,), (1,)), ((), ())), preferred_element_type=jnp.float32
        )
        total = gram.shape[0]
        on_diagonal = lax.broadcasted_iota(jnp.int32, gram.shape, 0) == (
            lax.broadcasted_iota(jnp.int32, gram.shape, 1)
        )
        diagonal = jnp.sum(jnp.where(on_diagonal, gram, 0.0), axis=0, keepdims=True)
        which = lax.broadcasted_iota(jnp.int32, diag_ref.shape, 0)
        diag_ref[...] = jnp.where(
            which == 0, diagonal, jnp.maximum(diagonal * PIVOT_FLOOR, 1e-37)
        )
        rest_ref[...] = gram
    else:
        rest_in_ref, diag_in_ref, rows_ref, rest_ref, diag_ref = refs
        rest_ref[...] = rest_in_ref[...]
        diag_ref[...] = diag_in_ref[...]
        total = rest_ref.shape[1]
    own = rows_ref.shape[0] // 2
    lanes = min(total, 128)
    parts = [slice(part * lanes, (part + 1) * lanes) for part in range(total // lanes)]
    row = lax.broadcasted_iota(jnp.int32, (PANEL, lanes), 0)
    lane = lax.broadcasted_iota(jnp.int32, (PANEL, lanes), 1)

    def panel(number, carry):
        low = pl.multiple_of(start + number * PANEL, PANEL)
        rest = [rest_ref[pl.ds(low, PANEL), part] for part in parts]
        left = [diag_ref[0:1, part] for part in parts]
        floor = [diag_ref[1:2, part] for part in parts]

        def as_column(values):
            picked = jnp.zeros((PANEL, lanes), jnp.float32)
            for part, value in zip(parts, values):
                picked = picked + jnp.where(lane + part.start == low + row, value, 0.0)
            return jnp.broadcast_to(jnp.sum(picked, axis=1, keepdims=True), (PANEL, lanes))

        left_column, floor_column = as_column(left), as_column(floor)
        corner = rest[0]
        for part, value in zip(parts[1:], rest[1:]):
            corner = jnp.where(low >= part.start, value, corner)
        corner = pltpu.roll(corner, lax.rem(lanes - lax.rem(low, lanes), lanes), 1)
        columns = [
            jnp.broadcast_to(corner[:, t : t + 1], (PANEL, lanes)) for t in range(PANEL)
        ]
        done = [jnp.zeros((PANEL, lanes), jnp.float32) for part in parts]
        for t in range(PANEL):
            pivot = jnp.maximum(left_column[t : t + 1], floor_column[t : t + 1])
            inverse = lax.rsqrt(pivot)
            inverse = inverse * (1.5 - 0.5 * (pivot * inverse) * inverse)
            most = root(left_column)
            weight = jnp.clip(columns[t] * inverse, -most, most)
            weight = jnp.where(row > t, weight, 0.0)
            left_column = jnp.maximum(left_column - weight * weight, 0.0)
            for s in range(t + 1, PANEL):
                columns[s] = columns[s] - weight * weight[s : s + 1]
            for i, part in enumerate(parts):
                place = lane[:1] + part.start
                most = root(left[i])
                here = jnp.clip(rest[i][t : t + 1] * inverse, -most, most)
                here = jnp.where(place > low + t, here, 0.0)
                left[i] = jnp.maximum(left[i] - here * here, 0.0)
                here = jnp.where(place == low + t, pivot * inverse, here)
                done[i] = jnp.where(row == t, here, done[i])
                rest[i] = rest[i] - weight * here
        for part, value in zip(parts, left):
            diag_ref[0:1, part] = value
        done = jnp.concatenate(done, axis=1)
        rest_ref[...] -= lax.dot_general(
            done,
            done,
            (((0,), (0,)), ((), ())),
            precision=lax.Precision.HIGHEST,
            preferred_element_type=jnp.float32,
        )
        done = done * (1.0 / SCALE)
        high = done.astype(jnp.bfloat16)
        place = pl.multiple_of(number * PANEL, PANEL)
        rows_ref[pl.ds(place, PANEL), :] = high
        rows_ref[pl.ds(own + place, PANEL), :] = (done - high.astype(jnp.float32)).astype(
            jnp.bfloat16
        )
        return carry

    lax.fori_loop(0, own // PANEL, panel, 0)


def factor_rows(start, own, total, operands):
    rows, rest, diagonals = pl.pallas_call(
        functools.partial(factor_kernel, start),
        out_shape=(
            jax.ShapeDtypeStruct((2 * own, total), jnp.bfloat16),
            jax.ShapeDtypeStruct((total, total), jnp.float32),
            jax.ShapeDtypeStruct((8, total), jnp.float32),
        ),
        compiler_params=pltpu.CompilerParams(vmem_limit_bytes=VMEM_BYTES),
        name="factor_rows",
    )(*operands)
    return rows, (rest, diagonals)


def half_kernel(low_block, list_ref, count_ref, basis_ref, *refs):
    tile_refs, (out_ref, rows_ref) = refs[:-2], refs[-2:]
    block = pl.program_id(0)
    aux_width, size_block = tile_refs[0].shape[2:4]
    vectors = basis_ref.shape[0] // 2
    side = basis_ref.shape[1] // size_block
    columns = range(low_block, side)
    for m in range(side):
        basis = []
        for n in columns:
            used = jnp.bool_(False)
            for slot in range(list_ref.shape[0]):
                hit = jnp.logical_and(
                    list_ref[slot, block] == m * side + n, slot < count_ref[block]
                )
                used = jnp.logical_or(used, hit)
            part = basis_ref[:, n * size_block : (n + 1) * size_block]
            basis.append(jnp.where(used, part, jnp.zeros_like(part)))
        tiles = [
            tile_refs[m * len(columns) + i][0, 0].reshape(aux_width * size_block, size_block)
            for i in range(len(columns))
        ]
        product = lax.dot_general(
            jnp.concatenate(basis, axis=1),
            jnp.concatenate(tiles, axis=1),
            (((1,), (1,)), ((), ())),
            preferred_element_type=jnp.float32,
        )
        product = product[:vectors] + product[vectors:]
        for p in range(aux_width):
            rows_ref[m, pl.ds(p, vectors, stride=aux_width), :] = product[
                :, p * size_block : (p + 1) * size_block
            ]
    for m in range(side):
        out_ref[..., m * size_block : (m + 1) * size_block] = (
            rows_ref[m].astype(jnp.bfloat16).reshape(out_ref.shape[:-1] + (size_block,))
        )


def half_transform(integrals, pair_list, pair_count, basis_rows, start, devices):
    blocks, slots, aux_width, size_block, _ = integrals.shape
    vectors, basis_total = basis_rows.shape[0] // 2, basis_rows.shape[1]
    own = vectors // devices
    side = basis_total // size_block
    low_block = start // size_block

    def tile_spec(pair):
        def place(b, list_ref, count_ref):
            slot_of = jnp.int32(0)
            for slot in range(1, slots):
                slot_of = jnp.where(list_ref[slot, b] == pair, slot, slot_of)
            return b, slot_of, 0, 0, 0

        return pl.BlockSpec((1, 1, aux_width, size_block, size_block), place)

    tiles = [tile_spec(m * side + n) for m in range(side) for n in range(low_block, side)]
    return pl.pallas_call(
        functools.partial(half_kernel, low_block),
        out_shape=jax.ShapeDtypeStruct(
            (devices, own, blocks * aux_width, basis_total), jnp.bfloat16
        ),
        grid_spec=pltpu.PrefetchScalarGridSpec(
            num_scalar_prefetch=2,
            grid=(blocks,),
            in_specs=[pl.BlockSpec(basis_rows.shape, lambda b, *_: (0, 0))] + tiles,
            out_specs=pl.BlockSpec(
                (devices, own, aux_width, basis_total), lambda b, *_: (0, 0, b, 0)
            ),
            scratch_shapes=[
                pltpu.VMEM(
                    (basis_total // size_block, vectors * aux_width, size_block), jnp.float32
                ),
            ],
        ),
        compiler_params=pltpu.CompilerParams(vmem_limit_bytes=VMEM_BYTES),
        cost_estimate=pl.CostEstimate(
            flops=4 * blocks * aux_width * vectors * basis_total * basis_total,
            bytes_accessed=integrals.size * 2 + vectors * blocks * aux_width * basis_total * 2,
            transcendentals=0,
        ),
        name="half_transform",
    )(pair_list.T, pair_count, basis_rows, *[integrals] * len(tiles))


def fit_kernel(
    step_rows,
    before_ref,
    factor_ref,
    half_ref,
    out_ref,
    sum_ref,
    lower_ref,
    columns_ref,
    sum_sem,
    factor_sems,
    half_sems,
):
    step = pl.program_id(0)
    aux_total = factor_ref.shape[0]
    basis_total = out_ref.shape[0]
    width = columns_ref.shape[-1] // basis_total
    blocks = aux_total // step_rows
    sources = half_ref.shape[0] // blocks
    sum_copy = pltpu.make_async_copy(before_ref, sum_ref, sum_sem)

    def factor_copy(number):
        low, high = number * step_rows, (number + 1) * step_rows
        part = (slice(low, high), slice(0, high))
        return pltpu.make_async_copy(
            factor_ref.at[part], lower_ref.at[part], factor_sems.at[number]
        )

    def half_copy(index, number, k):
        slot = lax.rem(index, 2)
        part = slice(number * sources, (number + 1) * sources)
        return pltpu.make_async_copy(
            half_ref.at[part, index * width + k],
            columns_ref.at[slot, part, :, k * basis_total : (k + 1) * basis_total],
            half_sems.at[slot, number, k],
        )

    def start_half(index):
        for number in range(blocks):
            for k in range(width):
                half_copy(index, number, k).start()

    @pl.when(step == 0)
    def _():
        for number in range(blocks):
            for k in range(width):
                half_copy(step, number, k).start()
            factor_copy(number).start()
        sum_copy.start()

    pl.when(step + 1 < pl.num_programs(0))(lambda: start_half(step + 1))

    total = jnp.zeros(out_ref.shape, jnp.float32)
    for number in range(blocks):
        low, high = number * step_rows, (number + 1) * step_rows
        for k in range(width):
            half_copy(step, number, k).wait()
        pl.when(step == 0)(lambda number=number: factor_copy(number).wait())
        columns = columns_ref[lax.rem(step, 2), : (number + 1) * sources]
        fitted = jnp.dot(
            lower_ref[low:high, :high],
            columns.reshape(high, columns.shape[-1]),
            preferred_element_type=jnp.float32,
        ).astype(jnp.bfloat16)
        for k in range(width):
            one = fitted[:, k * basis_total : (k + 1) * basis_total]
            total = total + lax.dot_general(
                one, one, (((0,), (0,)), ((), ())), preferred_element_type=jnp.float32
            )

    @pl.when(step == 0)
    def _():
        sum_copy.wait()
        out_ref[...] = sum_ref[...] + total

    @pl.when(step > 0)
    def _():
        out_ref[...] += total


def fit_exchange(factor, arrived, before):
    devices, own, aux_local, basis_total = arrived.shape
    aux_total = factor.shape[0]
    width = 2 if own % 2 == 0 else 1
    return pl.pallas_call(
        functools.partial(fit_kernel, aux_total // 8),
        out_shape=jax.ShapeDtypeStruct((basis_total, basis_total), jnp.float32),
        grid=(own // width,),
        in_specs=[
            pl.BlockSpec(memory_space=pl.ANY),
            pl.BlockSpec(memory_space=pl.ANY),
            pl.BlockSpec(memory_space=pl.ANY),
        ],
        out_specs=pl.BlockSpec((basis_total, basis_total), lambda k: (0, 0)),
        scratch_shapes=[
            pltpu.VMEM((basis_total, basis_total), jnp.float32),
            pltpu.VMEM((aux_total, aux_total), jnp.bfloat16),
            pltpu.VMEM((2, devices, aux_local, width * basis_total), jnp.bfloat16),
            pltpu.SemaphoreType.DMA,
            pltpu.SemaphoreType.DMA((8,)),
            pltpu.SemaphoreType.DMA((2, 8, width)),
        ],
        compiler_params=pltpu.CompilerParams(vmem_limit_bytes=FIT_VMEM_BYTES),
        cost_estimate=pl.CostEstimate(
            flops=own * aux_total * basis_total * (aux_total * 9 // 8 + 2 * basis_total),
            bytes_accessed=(factor.size + arrived.size) * 2,
            transcendentals=0,
        ),
        name="fit_exchange",
    )(before, factor, arrived)


def line_near(block):
    before = lax.ppermute(block, "occ", [(i, (i + 1) % 4) for i in range(4)])
    after = lax.ppermute(block, "occ", [(i, (i + 3) % 4) for i in range(4)])
    return before, after


def line_forward(before, after):
    even = lax.axis_index("occ") % 2 == 0
    return lax.ppermute(
        jnp.where(even, before, after), "occ", [(i, i ^ 1) for i in range(4)]
    )


def line_order(block, before, after, opposite):
    order = lax.switch(
        lax.axis_index("occ"),
        [
            lambda: (block, after, opposite, before),
            lambda: (before, block, after, opposite),
            lambda: (opposite, before, block, after),
            lambda: (after, opposite, before, block),
        ],
    )
    return jnp.concatenate(order)


def chunk_sizes(own):
    if own % 8 == 0:
        return [own // 4, 5 * own // 8, own // 8]
    return [1] * own


def per_device(integrals, pair_list, pair_count, coefficients, metric):
    devices = lax.axis_size("aux") * lax.axis_size("occ")
    basis_total = coefficients.shape[0]
    in_line = lax.axis_size("occ") == 4
    near = line_near(metric) if in_line else ()
    total = jnp.zeros((basis_total, basis_total), jnp.float32)
    state = (coefficients,)
    start = 0
    arrived = []
    factor = None
    for chunk, own in enumerate(chunk_sizes(basis_total // devices)):
        width = own * devices
        rows, state = factor_rows(start, width, basis_total, state)
        half = half_transform(integrals, pair_list, pair_count, rows, start, devices)
        if chunk == 0:
            half, state, near = lax.optimization_barrier((half, state, near))
            later = line_forward(*near) if in_line else ()
        elif chunk == 1:
            half, state, later = lax.optimization_barrier((half, state, later))
            if in_line:
                line = line_order(metric, *near, later)
                factor = lax.all_gather(line, "aux", axis=0, tiled=True)
            else:
                factor = lax.all_gather(metric, BOTH, axis=0, tiled=True)
        else:
            total = fit_exchange(factor, arrived[chunk - 2], total)
            half, state, arrived[chunk - 1], total = lax.optimization_barrier(
                (half, state, arrived[chunk - 1], total)
            )
        arrived.append(lax.all_to_all(half, BOTH, split_axis=0, concat_axis=0, tiled=True))
        start += width
    for piece in arrived[-2:]:
        total = fit_exchange(factor, piece, total)
    shares = total.reshape(devices, basis_total // devices, basis_total)
    return jnp.sum(lax.all_to_all(shares, BOTH, split_axis=0, concat_axis=0, tiled=True), axis=0)


def solution(mesh):
    in_specs = (
        P(("grp", "aux", "occ"), None, None, None, None),
        P(("grp", "aux", "occ"), None),
        P(("grp", "aux", "occ")),
        P("grp", None),
        P(("grp", "aux", "occ"), None),
    )
    out_specs = P(("grp", "aux", "occ"), None)
    return jax.shard_map(
        per_device, mesh=mesh, in_specs=in_specs, out_specs=out_specs, check_vma=False
    )
```
